512 devices in a mesh: row: 32 (over y_lo, z), col: 16 (over y_hi, x, core).
Axes of the slice: x: 4, y: 8 (y_hi: 2, y_lo: 4; y = y_hi * 4 + y_lo), z: 8, core: 2. Of those that a mesh axis runs over, the one named last changes fastest.
Arguments:
- green: bfloat16 [128, 128, 4096], P('row', 'col'), may hold values from -4 to 4
- coupling: float32 [64], replicated, may hold values from 0.3 to 1
Outputs:
- collision: bfloat16 [128, 128, 4096], P('row', 'col')
- new_row: bfloat16 [128, 4096], P('col', 'row')
The draws below stay inside these ranges and needn't reach their ends.
All inputs are finite; a program needn't handle non-finite values.
Results may differ from the reference program's by a relative error of at most 0.0046.
Values may be sent and summed in bfloat16 or wider, within the bound.
A program may use at most 64 MiB of HBM per device.

```python
import math
import jax
import jax.numpy as jnp
from jax import lax

N = 64
NN = 4096
NT = 128


def steps_of(own_key, dims, split, low, top_value):
    loudness, own = 1.0, jax.random.fold_in(own_key, 6)
    for axis_at, shards_of in split:
        heights = jnp.exp(jax.random.uniform(jax.random.fold_in(own, axis_at), (shards_of,), jnp.float32, low / len(split), top_value / len(split)))
        loudness = loudness * jnp.repeat(heights, dims[axis_at] // shards_of).reshape([-1 if axis == axis_at else 1 for axis in range(len(dims))])
    return loudness


def centred(rng, extent, scale, limit, pieces=(), kind=jnp.bfloat16):
    values = jax.random.normal(rng, extent, jnp.float32) * scale
    if len(pieces) > 0:
        values = steps_of(rng, extent, pieces, -0.22, 0.18) * values
    return jnp.clip(values, min=-limit, max=limit).astype(kind)


def setup_inputs(seed: int = 0) -> dict:
    key_list = jax.random.split(jax.random.key(seed), 3)
    return {
        "green": centred(key_list[0], (NT, NT, NN), 1.0, 4.0, ((0, 32), (1, 16))),
        "coupling": jnp.clip(jnp.exp(jax.random.uniform(key_list[1], (N,), jnp.float32, math.log(0.3), math.log(1.0))), 0.3, 1.0),
    }


step_size = 0.01


def reference(green, coupling):
    g = green.reshape(NT, NT, N, N)
    gf = g.astype(jnp.float32)
    gt = jnp.transpose(gf, (1, 0, 3, 2))
    pair = coupling[:, None] * coupling[None, :]
    sigma = (pair * (gf * gf) * gt).astype(jnp.bfloat16)
    times = jnp.arange(NT, dtype=jnp.int32)
    keep = times[None, :] <= times[:, None]
    sigma = jnp.where(keep[:, :, None, None], sigma, jnp.zeros((), jnp.bfloat16))

    def one_row(srow):
        return jnp.einsum('sik,sbkj->bij', srow.astype(jnp.float32), gf)

    history = lax.map(one_row, sigma)
    collision = (step_size * history).astype(jnp.bfloat16).reshape(NT, NT, N * N)
    new_row = (gf[NT - 1] + step_size * history[NT - 1]).astype(jnp.bfloat16).reshape(NT, N * N)
    return (collision, new_row)
```

```python
import jax
import jax.numpy as jnp
from jax import lax
from jax.experimental import pallas as pl
from jax.experimental.pallas import tpu as pltpu
from jax.sharding import PartitionSpec as P

step_size = 0.01
MESH = pl.DeviceIdType.MESH
BF = jnp.bfloat16
F32 = jnp.float32


def kernel(
    x_ref,
    pair_ref,
    out_ref,
    new_ref,
    gz,
    mir,
    own,
    sig,
    part,
    cin,
    acc,
    row_mid,
    row_src,
    row_in,
    g_send,
    g_recv,
    m_send,
    m_recv,
    s_send,
    s_recv,
    x_send,
    x_recv,
    k_send,
    k_recv,
    c_send,
    c_recv,
    n_send,
    n_recv,
):
    r = lax.axis_index("row")
    c = lax.axis_index("col")
    yl, z = r // 8, r % 8
    yh, x, k = c // 8, (c // 2) % 4, c % 2
    goal = c // 4
    half = (x // 2 + yl) % 2
    makes = yl >= goal

    def at(yl_, z_, yh_, x_, k_):
        return (yl_ * 8 + z_, yh_ * 8 + x_ * 2 + k_)

    def remote(src, dst, send, recv, device):
        return pltpu.make_async_remote_copy(
            src, dst, send, recv, device_id=device, device_id_type=MESH
        )

    up, down = at(yl, (z + 1) % 8, yh, x, k), at(yl, (z + 7) % 8, yh, x, k)
    other = at(yl, z, yh, x, 1 - k)

    def mirror_to(h):
        return (2 * c + h, r // 2)

    def mirror_from(b):
        return (2 * c + b, r // 2)

    itself = c == r // 2

    def stage_to(yh_, h):
        return at(goal, z, yh_, x if h == 0 else 3 - x, k)

    def stage_self(yh_, h):
        return (yl == goal) & (yh == yh_) if h == 0 else False

    def stage_from(y):
        return at(y, z, yl // 2, jnp.where(half == 0, x, 3 - x), k)

    def from_self(y):
        return (y == yl) & (yh == yl // 2) & (half == 0)

    barrier = pltpu.get_barrier_semaphore()

    def greet(device):
        pl.semaphore_signal(barrier, inc=1, device_id=device, device_id_type=MESH)

    greet(up)
    greet(down)
    greet(other)
    for d in (1, 2, 3):
        greet(at(yl, z, yh, (x + d) % 4, k))
    for b in range(2):

        @pl.when(makes & jnp.logical_not(itself & (z % 2 == b)))
        def _():
            greet(mirror_from(b))

    for y in range(4):

        @pl.when((y >= yl) & jnp.logical_not(from_self(y)))
        def _():
            greet(stage_from(y))

    for q in range(3):

        @pl.when(q < yl)
        def _():
            greet(at(q, z, yh, x, k))

    @pl.when(r != 31)
    def _():
        greet((31, c))

    peers = 9 - yl + jnp.where(r == 31, 31, 0)
    peers += jnp.where(goal >= yl, 2 - itself.astype(jnp.int32), 0)
    peers += jnp.where(makes, 4 - (yl == goal).astype(jnp.int32), 0)
    pl.semaphore_wait(barrier, peers)

    def mirror_copy(h):
        return remote(
            x_ref.at[:, pl.ds(h * 256, 256)],
            mir.at[z % 2],
            m_send.at[h],
            m_recv.at[z % 2],
            mirror_to(h),
        )

    def mirror_arrival(b):
        return remote(
            x_ref.at[:, pl.ds(0, 256)], mir.at[b], m_send.at[0], m_recv.at[b], up
        )

    for h in range(2):

        @pl.when((goal >= yl) & jnp.logical_not(itself & (z % 2 == h)))
        def _():
            mirror_copy(h).start()

        @pl.when(itself & (z % 2 == h))
        def _():
            mir[h] = x_ref[:, h * 256 : (h + 1) * 256]

    def g_copy(way, step):
        held = (z - step + 8) % 8 if way == 0 else (z + step) % 8
        rows = pl.ds(0, 256) if step < 3 else pl.ds(way * 128, 128)
        src = x_ref if step == 0 else gz.at[held]
        return remote(
            src.at[rows],
            gz.at[held, rows],
            g_send.at[way, step],
            g_recv.at[way, step],
            up if way == 0 else down,
        )

    def g_arrival(way, step):
        held = (z - step + 7) % 8 if way == 0 else (z + step + 1) % 8
        rows = pl.ds(0, 256) if step < 3 else pl.ds(way * 128, 128)
        return remote(
            x_ref.at[rows],
            gz.at[held, rows],
            g_send.at[way, step],
            g_recv.at[way, step],
            up,
        )

    def g_pass(step):
        for way in range(2):
            g_arrival(way, step - 1).wait_recv()
            g_copy(way, step).start()

    for way in range(2):
        g_copy(way, 0).start()
    gz[z] = x_ref[...]

    def stage_copy(yh_, h):
        return remote(
            own.at[pl.ds(h * 128, 128)],
            sig.at[yl, c % 4, pl.ds(h * 128, 128)],
            s_send.at[yh_ * 2 + h],
            s_recv.at[yl],
            stage_to(yh_, h),
        )

    def piece(x_, k_):
        h = (x_ // 2 + yl) % 2
        hi = (x_ + h) % 2
        return hi * 2 + k_, pl.ds(pl.multiple_of(h * 128, 128), 128)

    def stage_arrival(y):
        m, rows = piece(x, k)
        return remote(
            own.at[pl.ds(0, 128)], sig.at[y, m, rows], s_send.at[0], s_recv.at[y], up
        )

    @pl.when(makes)
    def _():
        for b in range(2):

            @pl.when(jnp.logical_not(itself & (z % 2 == b)))
            def _():
                mirror_arrival(b).wait_recv()

        for b in range(2):
            lanes = slice(b * 256, (b + 1) * 256)
            partner = mir[b].T
            later = lax.broadcasted_iota(jnp.int32, (64, 256), 1) // 64 + b * 4
            for i in range(4):
                rows = slice(i * 64, (i + 1) * 64)
                g = x_ref[rows, lanes].astype(F32)
                value = pair_ref[:, lanes] * (g * g) * partner[rows].astype(F32)
                keep = later <= 4 * r + i - 8 * c
                own[rows, lanes] = jnp.where(keep, value, 0.0).astype(BF)
        for yh_ in range(2):
            for h in range(2):
                if h == 1:
                    stage_copy(yh_, h).start()
                else:

                    @pl.when(jnp.logical_not(stage_self(yh_, h)))
                    def _():
                        stage_copy(yh_, h).start()

                    @pl.when(stage_self(yh_, h))
                    def _():
                        sig[yl, c % 4, 0:128] = own[0:128]

    def x_copy(y, d):
        m, rows = piece(x, k)
        return remote(
            sig.at[y, m, rows],
            sig.at[y, m, rows],
            x_send.at[y, d - 1],
            x_recv.at[y, d - 1],
            at(yl, z, yh, (x + d) % 4, k),
        )

    def x_arrival(y, d):
        m, rows = piece((x + 4 - d) % 4, k)
        return remote(
            own.at[pl.ds(0, 128)],
            sig.at[y, m, rows],
            x_send.at[y, d - 1],
            x_recv.at[y, d - 1],
            up,
        )

    def k_copy(y, d):
        m, rows = piece((x + 4 - d) % 4, k)
        return remote(
            sig.at[y, m, rows],
            sig.at[y, m, rows],
            k_send.at[y, d],
            k_recv.at[y, d],
            other,
        )

    def k_arrival(y, d):
        m, rows = piece((x + 4 - d) % 4, 1 - k)
        return remote(
            own.at[pl.ds(0, 128)],
            sig.at[y, m, rows],
            k_send.at[y, d],
            k_recv.at[y, d],
            other,
        )

    def spread(y):
        @pl.when(y >= yl)
        def _():
            @pl.when(jnp.logical_not(from_self(y)))
            def _():
                stage_arrival(y).wait_recv()

            for d in (2, 1, 3):
                x_copy(y, d).start()
            k_copy(y, 0).start()

    def swap(y):
        @pl.when(y >= yl)
        def _():
            for d in (1, 3, 2):
                x_arrival(y, d).wait_recv()
                k_copy(y, d).start()

    def c_copy(y):
        return remote(
            part.at[y - 1],
            cin.at[yl],
            c_send.at[y - 1],
            c_recv.at[yl],
            at(y, z, yh, x, k),
        )

    def c_arrival(q):
        return remote(part.at[0], cin.at[q], c_send.at[0], c_recv.at[q], up)

    def product(y):
        @pl.when(y >= yl)
        def _():
            for d in range(4):
                k_arrival(y, d).wait_recv()
            for m in range(4):
                term = jnp.dot(
                    sig[y, m],
                    gz[2 * m : 2 * m + 2].reshape(512, 512),
                    preferred_element_type=F32,
                )
                if m == 0:
                    acc[...] = term
                else:
                    acc[...] += term

        if y > 0:

            @pl.when(y > yl)
            def _():
                part[y - 1] = acc[...].astype(BF)
                c_copy(y).start()

    g_pass(1)
    spread(3)
    g_pass(2)
    spread(2)
    swap(3)
    g_pass(3)
    spread(1)
    swap(2)
    spread(0)
    for way in range(2):
        g_arrival(way, 3).wait_recv()
    product(3)
    swap(1)
    product(2)
    swap(0)
    product(1)
    product(0)

    for q in range(3):

        @pl.when(q < yl)
        def _():
            c_arrival(q).wait_recv()
            acc[...] += cin[q].astype(F32)

    out_ref[...] = (step_size * acc[...]).astype(BF)

    def n_copy(to):
        return remote(
            row_src.at[pl.ds(pl.multiple_of(to * 8, 8), 8)],
            row_in,
            n_send.at[to],
            n_recv,
            (to, c),
        )

    @pl.when(r == 31)
    def _():
        for q in range(4):
            lanes = slice(q * 128, (q + 1) * 128)
            row_mid[q * 64 : (q + 1) * 64, :] = (
                x_ref[192:256, lanes].astype(F32) + step_size * acc[192:256, lanes]
            )
            for i in range(2):
                row_src[pl.ds(i * 4 + q, 32, stride=8), :] = row_mid[
                    pl.ds(q * 64 + i, 32, stride=2), :
                ]

        @pl.loop(0, 31)
        def _(to):
            n_copy(to).start()

        row_in[...] = row_src[248:256, :]

        @pl.loop(0, 31)
        def _(to):
            n_copy(to).wait_send()

    @pl.when(r != 31)
    def _():
        n_copy(0).wait_recv()

    new_ref[...] = row_in[...]

    for h in range(2):

        @pl.when((goal >= yl) & jnp.logical_not(itself & (z % 2 == h)))
        def _():
            mirror_copy(h).wait_send()

    for step in range(4):
        for way in range(2):
            g_copy(way, step).wait_send()
    for yh_ in range(2):
        for h in range(2):

            @pl.when(makes & jnp.logical_not(stage_self(yh_, h)))
            def _():
                stage_copy(yh_, h).wait_send()

    for y in range(4):

        @pl.when(y >= yl)
        def _():
            for d in (1, 2, 3):
                x_copy(y, d).wait_send()
            for d in range(4):
                k_copy(y, d).wait_send()

        if y > 0:

            @pl.when(y > yl)
            def _():
                c_copy(y).wait_send()


def shards(green, coupling):
    rows, cols, width = green.shape
    orbit = coupling.shape[0]
    high, wide = rows * orbit, cols * orbit
    matrix = jnp.transpose(green.reshape(rows, cols, orbit, orbit), (0, 2, 1, 3))
    matrix = matrix.reshape(high, wide)
    pair = coupling[:, None] * jnp.tile(coupling, cols)[None, :]
    vmem = pl.BlockSpec(memory_space=pltpu.VMEM)
    dma = pltpu.SemaphoreType.DMA
    collision, fresh = pl.pallas_call(
        kernel,
        out_shape=(
            jax.ShapeDtypeStruct((high, wide), BF),
            jax.ShapeDtypeStruct((8, 128), F32),
        ),
        in_specs=[vmem, vmem],
        out_specs=(vmem, vmem),
        scratch_shapes=[
            pltpu.VMEM((8, high, wide), BF),
            pltpu.VMEM((2, high, high), BF),
            pltpu.VMEM((high, wide), BF),
            pltpu.VMEM((4, 4, high, wide), BF),
            pltpu.VMEM((3, high, wide), BF),
            pltpu.VMEM((3, high, wide), BF),
            pltpu.VMEM((high, wide), F32),
            pltpu.VMEM((256, 128), F32),
            pltpu.VMEM((256, 128), F32),
            pltpu.VMEM((8, 128), F32),
            dma((2, 4)),
            dma((2, 4)),
            dma((2,)),
            dma((2,)),
            dma((4,)),
            dma((4,)),
            dma((4, 3)),
            dma((4, 3)),
            dma((4, 4)),
            dma((4, 4)),
            dma((3,)),
            dma((3,)),
            dma((31,)),
            dma(()),
        ],
        compiler_params=pltpu.CompilerParams(
            collective_id=0, has_side_effects=True, vmem_limit_bytes=40 << 20
        ),
        cost_estimate=pl.CostEstimate(
            flops=2 * high * wide * 8192, bytes_accessed=4 * high * wide, transcendentals=0
        ),
        name="collide",
    )(matrix, pair)
    collision = collision.reshape(rows, orbit, cols, orbit).transpose(0, 2, 1, 3)
    collision = collision.reshape(rows, cols, width)
    fresh = fresh.reshape(2, 4, 2, orbit).transpose(1, 2, 0, 3).reshape(cols, 128)
    return (collision, fresh.astype(BF))


def solution(mesh):
    placed = (P("row", "col", None), P())
    return jax.shard_map(
        shards,
        mesh=mesh,
        in_specs=placed,
        out_specs=(P("row", "col", None), P("col", "row")),
        check_vma=False,
    )
```

```python
import jax
import jax.numpy as jnp
from jax import lax
from jax.experimental import pallas as pl
from jax.experimental.pallas import tpu as pltpu
from jax.sharding import PartitionSpec as P

step_size = 0.01
MESH = pl.DeviceIdType.MESH
BF = jnp.bfloat16
F32 = jnp.float32


def kernel(
    x_ref,
    pair_ref,
    out_ref,
    new_ref,
    gz,
    mir,
    own,
    sig,
    part,
    cin,
    acc,
    row_mid,
    row_src,
    row_in,
    g_send,
    g_recv,
    m_send,
    m_recv,
    s_send,
    s_recv,
    y_send,
    y_recv,
    x_send,
    x_recv,
    k_send,
    k_recv,
    c_send,
    c_recv,
    f_send,
    f_recv,
    n_send,
    n_recv,
):
    r = lax.axis_index("row")
    c = lax.axis_index("col")
    yl, z = r // 8, r % 8
    yh, x, k = c // 8, (c // 2) % 4, c % 2
    goal = c // 4
    part_at = 2 * x + k

    def at(yl_, z_, yh_, x_, k_):
        return (yl_ * 8 + z_, yh_ * 8 + x_ * 2 + k_)

    def remote(src, dst, send, recv, device):
        return pltpu.make_async_remote_copy(
            src, dst, send, recv, device_id=device, device_id_type=MESH
        )

    up, down = at(yl, (z + 1) % 8, yh, x, k), at(yl, (z + 7) % 8, yh, x, k)
    other = at(yl, z, yh, x, 1 - k)
    across = at(yl, z, 1 - yh, x, k)

    gives_mirror = goal >= yl

    def mirror_to(h):
        return at(yl, (x % 2) * 4 + k * 2 + h, yh, z // 2, z % 2)

    def mirror_self(h):
        return (z == part_at) & (z == (x % 2) * 4 + k * 2 + h)

    def mirror_from(s):
        return at(yl, part_at, yh, s * 2 + z // 4, (z // 2) % 2)

    def mirror_from_self(s):
        return (z == part_at) & (x == s * 2 + z // 4) & (k == (z // 2) % 2)

    gives_piece = yl >= goal

    def piece_to(h):
        return at(goal, z, yl // 2, (x % 2) * 2 + k, h)

    def piece_self(h):
        return (goal == yl) & (x == (x % 2) * 2 + k) & (k == h)

    def piece_from(s):
        return at(2 * yh + s, z, yl // 2, (yl % 2) * 2 + x // 2, x % 2)

    def piece_from_self(s):
        mine = (2 * yh + s == yl) & (x == (yl % 2) * 2 + x // 2) & (k == x % 2)
        return mine & (yl // 2 == yh)

    def one(flag):
        return jnp.where(flag, 1, 0)

    barrier = pltpu.get_barrier_semaphore()

    def greet(device):
        pl.semaphore_signal(barrier, inc=1, device_id=device, device_id_type=MESH)

    greet(up)
    greet(down)
    greet(other)
    for d in (1, 2, 3):
        greet(at(yl, z, yh, (x + d) % 4, k))
    for s in range(2):

        @pl.when((2 * yh + s >= yl) & jnp.logical_not(mirror_from_self(s)))
        def _():
            greet(mirror_from(s))

        @pl.when((2 * yh + s >= yl) & jnp.logical_not(piece_from_self(s)))
        def _():
            greet(piece_from(s))

    @pl.when(3 - 2 * yh >= yl)
    def _():
        greet(across)

    for q in range(3):

        @pl.when(q < yl)
        def _():
            greet(at(q, z, yh, x, k))

    @pl.when(z != 7)
    def _():
        greet(at(yl, 7, yh, x, k))

    @pl.when((z == 7) & (yl != 3))
    def _():
        greet((31, c))

    peers = 9 - yl + jnp.where(z == 7, 7, 0) + jnp.where(r == 31, 3, 0)
    peers += one(2 * yh + 1 >= yl)
    for h in range(2):
        peers += one(gives_mirror & jnp.logical_not(mirror_self(h)))
        peers += one(gives_piece & jnp.logical_not(piece_self(h)))
    pl.semaphore_wait(barrier, peers)

    def half_of(h):
        return x_ref.at[:, pl.ds(h * 256, 256)]

    def mirror_copy(h):
        return remote(
            half_of(h), mir.at[x // 2], m_send.at[h], m_recv.at[x // 2], mirror_to(h)
        )

    def mirror_arrival(s):
        return remote(half_of(0), mir.at[s], m_send.at[0], m_recv.at[s], up)

    def piece_copy(h):
        return remote(
            half_of(h), own.at[yl % 2], s_send.at[h], s_recv.at[yl % 2], piece_to(h)
        )

    def piece_arrival(s):
        return remote(half_of(0), own.at[s], s_send.at[0], s_recv.at[s], up)

    for h in range(2):

        @pl.when(gives_mirror & jnp.logical_not(mirror_self(h)))
        def _():
            mirror_copy(h).start()

        @pl.when(gives_piece & jnp.logical_not(piece_self(h)))
        def _():
            piece_copy(h).start()

        @pl.when(gives_mirror & mirror_self(h))
        def _():
            mir[x // 2] = x_ref[:, h * 256 : (h + 1) * 256]

        @pl.when(gives_piece & piece_self(h))
        def _():
            own[yl % 2] = x_ref[:, h * 256 : (h + 1) * 256]

    def g_copy(way, step):
        held = (z - step + 8) % 8 if way == 0 else (z + step) % 8
        rows = pl.ds(0, 256) if step < 3 else pl.ds(way * 128, 128)
        src = x_ref if step == 0 else gz.at[held]
        return remote(
            src.at[rows],
            gz.at[held, rows],
            g_send.at[way, step],
            g_recv.at[way, step],
            up if way == 0 else down,
        )

    def g_arrival(way, step):
        held = (z - step + 7) % 8 if way == 0 else (z + step + 1) % 8
        rows = pl.ds(0, 256) if step < 3 else pl.ds(way * 128, 128)
        return remote(
            x_ref.at[rows],
            gz.at[held, rows],
            g_send.at[way, step],
            g_recv.at[way, step],
            up,
        )

    def g_pass(step):
        for way in range(2):
            g_arrival(way, step - 1).wait_recv()
            g_copy(way, step).start()

    for way in range(2):
        g_copy(way, 0).start()
    gz[z] = x_ref[...]

    def y_copy(y):
        return remote(
            sig.at[y, part_at], sig.at[y, part_at], y_send.at[y], y_recv.at[y], across
        )

    def x_copy(y, d):
        return remote(
            sig.at[y, part_at],
            sig.at[y, part_at],
            x_send.at[y, d - 1],
            x_recv.at[y, d - 1],
            at(yl, z, yh, (x + d) % 4, k),
        )

    def x_arrival(y, d):
        j = 2 * ((x + 4 - d) % 4) + k
        return remote(
            sig.at[y, j], sig.at[y, j], x_send.at[y, d - 1], x_recv.at[y, d - 1], up
        )

    def k_copy(y, d):
        j = 2 * ((x + 4 - d) % 4) + k
        return remote(
            sig.at[y, j], sig.at[y, j], k_send.at[y, d], k_recv.at[y, d], other
        )

    def k_arrival(y, d):
        j = 2 * ((x + 4 - d) % 4) + 1 - k
        return remote(
            sig.at[y, j], sig.at[y, j], k_send.at[y, d], k_recv.at[y, d], other
        )

    def spread(y):
        for d in (1, 3, 2):
            x_copy(y, d).start()
        k_copy(y, 0).start()

    def near(i):
        return 2 * yh + 1 - i

    def far(i):
        return 3 - 2 * yh - i

    def make(i):
        s = 1 - i
        y = near(i)

        @pl.when(y >= yl)
        def _():
            @pl.when(jnp.logical_not(mirror_from_self(s)))
            def _():
                mirror_arrival(s).wait_recv()

            @pl.when(jnp.logical_not(piece_from_self(s)))
            def _():
                piece_arrival(s).wait_recv()

            partner = mir[s].T
            pair = pair_ref[:, 0:256]
            later = lax.broadcasted_iota(jnp.int32, (64, 256), 1) // 64
            first = 32 * (y - yl) + 4 * z - 4 * part_at
            for i in range(4):
                rows = slice(i * 64, (i + 1) * 64)
                g = own[s, rows, :].astype(F32)
                value = pair * (g * g) * partner[rows].astype(F32)
                keep = later <= first + i
                sig[y, part_at, rows, :] = jnp.where(keep, value, 0.0).astype(BF)
            y_copy(y).start()
            spread(y)

    def hand_on(i):
        y = far(i)

        @pl.when(y >= yl)
        def _():
            y_copy(y).wait_recv()
            spread(y)

    def swap(y):
        @pl.when(y >= yl)
        def _():
            for d in (1, 3, 2):
                x_arrival(y, d).wait_recv()
                k_copy(y, d).start()

    def c_copy(y):
        return remote(
            part.at[y - 1],
            cin.at[yl],
            c_send.at[y - 1],
            c_recv.at[yl],
            at(y, z, yh, x, k),
        )

    def c_arrival(q):
        return remote(part.at[0], cin.at[q], c_send.at[0], c_recv.at[q], up)

    def product(y):
        @pl.when(y >= yl)
        def _():
            for d in range(4):
                k_arrival(y, d).wait_recv()
            total = jnp.zeros((256, 512), F32)
            for j in range(8):
                total += jnp.dot(sig[y, j], gz[j], preferred_element_type=F32)

            @pl.when(y > yl)
            def _():
                part[y - 1] = total.astype(BF)
                c_copy(y).start()

            @pl.when(y == yl)
            def _():
                acc[...] = total

    g_pass(1)
    make(0)
    make(1)
    g_pass(2)
    swap(near(0))
    swap(near(1))
    hand_on(0)
    g_pass(3)
    hand_on(1)
    for way in range(2):
        g_arrival(way, 3).wait_recv()
    product(near(0))
    product(near(1))
    swap(far(0))
    product(far(0))
    swap(far(1))
    product(far(1))

    for q in range(3):

        @pl.when(q < yl)
        def _():
            c_arrival(q).wait_recv()
            acc[...] += cin[q].astype(F32)

    out_ref[...] = (step_size * acc[...]).astype(BF)

    def far_copy(y):
        return remote(
            row_src.at[pl.ds(y * 64, 64)],
            row_src.at[pl.ds(y * 64, 64)],
            f_send.at[y],
            f_recv,
            at(y, 7, yh, x, k),
        )

    def n_copy(to):
        return remote(
            row_src.at[pl.ds(pl.multiple_of(yl * 64 + to * 8, 8), 8)],
            row_in,
            n_send.at[to],
            n_recv,
            at(yl, to, yh, x, k),
        )

    @pl.when(r == 31)
    def _():
        for q in range(4):
            lanes = slice(q * 128, (q + 1) * 128)
            row_mid[q * 64 : (q + 1) * 64, :] = (
                x_ref[192:256, lanes].astype(F32) + step_size * acc[192:256, lanes]
            )
            for i in range(2):
                row_src[pl.ds(i * 4 + q, 32, stride=8), :] = row_mid[
                    pl.ds(q * 64 + i, 32, stride=2), :
                ]
        for y in range(3):
            far_copy(y).start()

    @pl.when(z == 7)
    def _():
        @pl.when(yl != 3)
        def _():
            remote(
                row_src.at[pl.ds(0, 64)],
                row_src.at[pl.ds(pl.multiple_of(yl * 64, 64), 64)],
                f_send.at[0],
                f_recv,
                other,
            ).wait_recv()

        for to in range(7):
            n_copy(to).start()
        row_in[...] = row_src[pl.ds(pl.multiple_of(yl * 64 + 56, 8), 8), :]
        for to in range(7):
            n_copy(to).wait_send()

    @pl.when(z != 7)
    def _():
        n_copy(0).wait_recv()

    @pl.when(r == 31)
    def _():
        for y in range(3):
            far_copy(y).wait_send()

    new_ref[...] = row_in[...]

    for h in range(2):

        @pl.when(gives_mirror & jnp.logical_not(mirror_self(h)))
        def _():
            mirror_copy(h).wait_send()

        @pl.when(gives_piece & jnp.logical_not(piece_self(h)))
        def _():
            piece_copy(h).wait_send()

    for step in range(4):
        for way in range(2):
            g_copy(way, step).wait_send()
    for i in range(2):

        @pl.when(near(i) >= yl)
        def _():
            y_copy(near(i)).wait_send()

    for y in range(4):

        @pl.when(y >= yl)
        def _():
            for d in (1, 2, 3):
                x_copy(y, d).wait_send()
            for d in range(4):
                k_copy(y, d).wait_send()

        if y > 0:

            @pl.when(y > yl)
            def _():
                c_copy(y).wait_send()


def shards(green, coupling):
    rows, cols, width = green.shape
    orbit = coupling.shape[0]
    high, wide = rows * orbit, cols * orbit
    matrix = jnp.transpose(green.reshape(rows, cols, orbit, orbit), (0, 2, 1, 3))
    matrix = matrix.reshape(high, wide)
    pair = coupling[:, None] * jnp.tile(coupling, cols)[None, :]
    vmem = pl.BlockSpec(memory_space=pltpu.VMEM)
    dma = pltpu.SemaphoreType.DMA
    collision, fresh = pl.pallas_call(
        kernel,
        out_shape=(
            jax.ShapeDtypeStruct((high, wide), BF),
            jax.ShapeDtypeStruct((8, 128), F32),
        ),
        in_specs=[vmem, vmem],
        out_specs=(vmem, vmem),
        scratch_shapes=[
            pltpu.VMEM((8, high, wide), BF),
            pltpu.VMEM((2, high, high), BF),
            pltpu.VMEM((2, high, high), BF),
            pltpu.VMEM((4, 8, high, high), BF),
            pltpu.VMEM((3, high, wide), BF),
            pltpu.VMEM((3, high, wide), BF),
            pltpu.VMEM((high, wide), F32),
            pltpu.VMEM((256, 128), F32),
            pltpu.VMEM((256, 128), F32),
            pltpu.VMEM((8, 128), F32),
            dma((2, 4)),
            dma((2, 4)),
            dma((2,)),
            dma((2,)),
            dma((2,)),
            dma((2,)),
            dma((4,)),
            dma((4,)),
            dma((4, 3)),
            dma((4, 3)),
            dma((4, 4)),
            dma((4, 4)),
            dma((3,)),
            dma((3,)),
            dma((3,)),
            dma(()),
            dma((7,)),
            dma(()),
        ],
        compiler_params=pltpu.CompilerParams(
            collective_id=0, has_side_effects=True, vmem_limit_bytes=40 << 20
        ),
        cost_estimate=pl.CostEstimate(
            flops=2 * high * wide * 8192, bytes_accessed=4 * high * wide, transcendentals=0
        ),
        name="collide",
    )(matrix, pair)
    collision = collision.reshape(rows, orbit, cols, orbit).transpose(0, 2, 1, 3)
    collision = collision.reshape(rows, cols, width)
    fresh = fresh.reshape(2, 4, 2, orbit).transpose(1, 2, 0, 3).reshape(cols, 128)
    return (collision, fresh.astype(BF))


def solution(mesh):
    placed = (P("row", "col", None), P())
    return jax.shard_map(
        shards,
        mesh=mesh,
        in_specs=placed,
        out_specs=(P("row", "col", None), P("col", "row")),
        check_vma=False,
    )
```

```python
import jax
import jax.numpy as jnp
from jax import lax
from jax.experimental import pallas as pl
from jax.experimental.pallas import tpu as pltpu
from jax.sharding import PartitionSpec as P

step_size = 0.01
MESH = pl.DeviceIdType.MESH
BF = jnp.bfloat16
F32 = jnp.float32


def kernel(
    x_ref,
    pair_ref,
    out_ref,
    new_ref,
    gz,
    mir,
    own,
    sig,
    part,
    cin,
    acc,
    row_mid,
    row_src,
    row_in,
    g_send,
    g_recv,
    m_send,
    m_recv,
    s_send,
    s_recv,
    y_send,
    y_recv,
    x_send,
    x_recv,
    k_send,
    k_recv,
    c_send,
    c_recv,
    f_send,
    f_recv,
    n_send,
    n_recv,
):
    r = lax.axis_index("row")
    c = lax.axis_index("col")
    yl, z = r // 8, r % 8
    yh, x, k = c // 8, (c // 2) % 4, c % 2
    goal = c // 4
    part_at = 2 * x + k

    def at(yl_, z_, yh_, x_, k_):
        return (yl_ * 8 + z_, yh_ * 8 + x_ * 2 + k_)

    def remote(src, dst, send, recv, device):
        return pltpu.make_async_remote_copy(
            src, dst, send, recv, device_id=device, device_id_type=MESH
        )

    up, down = at(yl, (z + 1) % 8, yh, x, k), at(yl, (z + 7) % 8, yh, x, k)
    other = at(yl, z, yh, x, 1 - k)
    across = at(yl, z, 1 - yh, x, k)

    lends = (z // 2 == (x % 2) * 2 + k) & (goal >= yl)

    def mirror_from(s):
        return at(yl, z, yh, s * 2 + z // 4, (z // 2) % 2)

    def mirror_from_self(s):
        return (x == s * 2 + z // 4) & (k == (z // 2) % 2)

    gives_piece = yl >= goal

    def piece_to(h):
        return at(goal, z, yl // 2, (x % 2) * 2 + k, h)

    def piece_self(h):
        return (goal == yl) & (x == (x % 2) * 2 + k) & (k == h)

    def piece_from(s):
        return at(2 * yh + s, z, yl // 2, (yl % 2) * 2 + x // 2, x % 2)

    def piece_from_self(s):
        mine = (2 * yh + s == yl) & (x == (yl % 2) * 2 + x // 2) & (k == x % 2)
        return mine & (yl // 2 == yh)

    def one(flag):
        return jnp.where(flag, 1, 0)

    barrier = pltpu.get_barrier_semaphore()

    def greet(device):
        pl.semaphore_signal(barrier, inc=1, device_id=device, device_id_type=MESH)

    greet(up)
    greet(down)
    greet(other)
    for d in (1, 2, 3):
        greet(at(yl, z, yh, (x + d) % 4, k))
    for s in range(2):

        @pl.when((2 * yh + s >= yl) & jnp.logical_not(mirror_from_self(s)))
        def _():
            greet(mirror_from(s))

        @pl.when((2 * yh + s >= yl) & jnp.logical_not(piece_from_self(s)))
        def _():
            greet(piece_from(s))

    @pl.when(3 - 2 * yh >= yl)
    def _():
        greet(across)

    for q in range(3):

        @pl.when(q < yl)
        def _():
            greet(at(q, z, yh, x, k))

    @pl.when(z != 7)
    def _():
        greet(at(yl, 7, yh, x, k))

    @pl.when((z == 7) & (yl != 3))
    def _():
        greet((31, c))

    peers = 9 - yl + jnp.where(z == 7, 7, 0) + jnp.where(r == 31, 3, 0)
    peers += one(2 * yh + 1 >= yl) + jnp.where(lends, 7, 0)
    for h in range(2):
        peers += one(gives_piece & jnp.logical_not(piece_self(h)))
    pl.semaphore_wait(barrier, peers)

    def half_of(h):
        return x_ref.at[:, pl.ds(h * 256, 256)]

    def piece_copy(h):
        return remote(
            half_of(h), own.at[yl % 2], s_send.at[h], s_recv.at[yl % 2], piece_to(h)
        )

    def piece_arrival(s):
        return remote(half_of(0), own.at[s], s_send.at[0], s_recv.at[s], up)

    def g_copy(way, step, rows):
        held = (z - step + 8) % 8 if way == 0 else (z + step) % 8
        src = x_ref if step == 0 else gz.at[held]
        return remote(
            src.at[pl.ds(rows * 128, 128)],
            gz.at[held, pl.ds(rows * 128, 128)],
            g_send.at[way, step, rows],
            g_recv.at[way, step, rows],
            up if way == 0 else down,
        )

    def g_arrival(way, step, rows):
        held = (z - step + 7) % 8 if way == 0 else (z + step + 1) % 8
        return remote(
            x_ref.at[pl.ds(0, 128)],
            gz.at[held, pl.ds(rows * 128, 128)],
            g_send.at[way, step, rows],
            g_recv.at[way, step, rows],
            up,
        )

    def g_pass(step):
        for rows in range(2):
            for way in range(2):
                g_arrival(way, step - 1, rows).wait_recv()
                if step < 3 or rows == way:
                    g_copy(way, step, rows).start()

    def mirror_copy(b):
        lanes = pl.ds(pl.multiple_of((z % 2) * 256, 256), 256)
        return remote(
            gz.at[b, :, lanes],
            mir.at[x // 2],
            m_send.at[b],
            m_recv.at[x // 2],
            at(yl, z, yh, b // 2, b % 2),
        )

    def mirror_arrival(s):
        return remote(half_of(0), mir.at[s], m_send.at[0], m_recv.at[s], up)

    def lend(b):
        @pl.when(lends & (b != part_at))
        def _():
            mirror_copy(b).start()

        for h in range(2):

            @pl.when(lends & (b == part_at) & (z % 2 == h))
            def _():
                mir[x // 2] = gz[b, :, h * 256 : (h + 1) * 256]

    for rows in range(2):
        for way in range(2):
            g_copy(way, 0, rows).start()
    for h in range(2):

        @pl.when(gives_piece & jnp.logical_not(piece_self(h)))
        def _():
            piece_copy(h).start()

        @pl.when(gives_piece & piece_self(h))
        def _():
            own[yl % 2] = x_ref[:, h * 256 : (h + 1) * 256]

    gz[z] = x_ref[...]
    lend(z)

    def y_copy(y):
        return remote(
            sig.at[y, part_at], sig.at[y, part_at], y_send.at[y], y_recv.at[y], across
        )

    def x_copy(y, d):
        return remote(
            sig.at[y, part_at],
            sig.at[y, part_at],
            x_send.at[y, d - 1],
            x_recv.at[y, d - 1],
            at(yl, z, yh, (x + d) % 4, k),
        )

    def x_arrival(y, d):
        j = 2 * ((x + 4 - d) % 4) + k
        return remote(
            sig.at[y, j], sig.at[y, j], x_send.at[y, d - 1], x_recv.at[y, d - 1], up
        )

    def k_copy(y, d):
        j = 2 * ((x + 4 - d) % 4) + k
        return remote(
            sig.at[y, j], sig.at[y, j], k_send.at[y, d], k_recv.at[y, d], other
        )

    def k_arrival(y, d):
        j = 2 * ((x + 4 - d) % 4) + 1 - k
        return remote(
            sig.at[y, j], sig.at[y, j], k_send.at[y, d], k_recv.at[y, d], other
        )

    def spread(y):
        for d in (1, 3, 2):
            x_copy(y, d).start()
        k_copy(y, 0).start()

    def near(i):
        return 2 * yh + 1 - i

    def far(i):
        return 3 - 2 * yh - i

    def make(i):
        s = 1 - i
        y = near(i)

        @pl.when(y >= yl)
        def _():
            @pl.when(jnp.logical_not(mirror_from_self(s)))
            def _():
                mirror_arrival(s).wait_recv()

            @pl.when(jnp.logical_not(piece_from_self(s)))
            def _():
                piece_arrival(s).wait_recv()

            partner = mir[s].T
            pair = pair_ref[:, 0:256]
            later = lax.broadcasted_iota(jnp.int32, (64, 256), 1) // 64
            first = 32 * (y - yl) + 4 * z - 4 * part_at
            for i in range(4):
                rows = slice(i * 64, (i + 1) * 64)
                g = own[s, rows, :].astype(F32)
                value = pair * (g * g) * partner[rows].astype(F32)
                keep = later <= first + i
                sig[y, part_at, rows, :] = jnp.where(keep, value, 0.0).astype(BF)
            y_copy(y).start()
            spread(y)

    def hand_on(i):
        y = far(i)

        @pl.when(y >= yl)
        def _():
            y_copy(y).wait_recv()
            spread(y)

    def swap(y):
        @pl.when(y >= yl)
        def _():
            for d in (1, 3, 2):
                x_arrival(y, d).wait_recv()
                k_copy(y, d).start()

    def c_copy(y):
        return remote(
            part.at[y - 1],
            cin.at[yl],
            c_send.at[y - 1],
            c_recv.at[yl],
            at(y, z, yh, x, k),
        )

    def c_arrival(q):
        return remote(part.at[0], cin.at[q], c_send.at[0], c_recv.at[q], up)

    def product(y):
        @pl.when(y >= yl)
        def _():
            for d in range(4):
                k_arrival(y, d).wait_recv()
            total = jnp.zeros((256, 512), F32)
            for j in range(8):
                total += jnp.dot(sig[y, j], gz[j], preferred_element_type=F32)

            @pl.when(y > yl)
            def _():
                part[y - 1] = total.astype(BF)
                c_copy(y).start()

            @pl.when(y == yl)
            def _():
                acc[...] = total

    gap = (part_at - z + 8) % 8
    gap = jnp.minimum(gap, 8 - gap)

    for step in range(1, 5):
        if step < 4:
            g_pass(step)
            lend((z - step + 8) % 8)
            lend((z + step) % 8)
        else:
            for way in range(2):
                g_arrival(way, 3, way).wait_recv()
            lend((z + 4) % 8)
        if step > 1:

            @pl.when(jnp.maximum(gap, 1) == step - 1)
            def _():
                hand_on(0)
                hand_on(1)

        @pl.when(jnp.maximum(gap, 1) == step)
        def _():
            make(0)
            make(1)

    swap(near(0))
    swap(near(1))

    @pl.when(gap == 4)
    def _():
        hand_on(0)
        hand_on(1)

    product(near(0))
    product(near(1))
    swap(far(0))
    product(far(0))
    swap(far(1))
    product(far(1))

    for q in range(3):

        @pl.when(q < yl)
        def _():
            c_arrival(q).wait_recv()
            acc[...] += cin[q].astype(F32)

    out_ref[...] = (step_size * acc[...]).astype(BF)

    def far_copy(y):
        return remote(
            row_src.at[pl.ds(y * 64, 64)],
            row_src.at[pl.ds(y * 64, 64)],
            f_send.at[y],
            f_recv,
            at(y, 7, yh, x, k),
        )

    def n_copy(to):
        return remote(
            row_src.at[pl.ds(pl.multiple_of(yl * 64 + to * 8, 8), 8)],
            row_in,
            n_send.at[to],
            n_recv,
            at(yl, to, yh, x, k),
        )

    @pl.when(r == 31)
    def _():
        for q in range(4):
            lanes = slice(q * 128, (q + 1) * 128)
            row_mid[q * 64 : (q + 1) * 64, :] = (
                x_ref[192:256, lanes].astype(F32) + step_size * acc[192:256, lanes]
            )
            for i in range(2):
                row_src[pl.ds(i * 4 + q, 32, stride=8), :] = row_mid[
                    pl.ds(q * 64 + i, 32, stride=2), :
                ]
        for y in range(3):
            far_copy(y).start()

    @pl.when(z == 7)
    def _():
        @pl.when(yl != 3)
        def _():
            remote(
                row_src.at[pl.ds(0, 64)],
                row_src.at[pl.ds(pl.multiple_of(yl * 64, 64), 64)],
                f_send.at[0],
                f_recv,
                other,
            ).wait_recv()

        for to in range(7):
            n_copy(to).start()
        row_in[...] = row_src[pl.ds(pl.multiple_of(yl * 64 + 56, 8), 8), :]
        for to in range(7):
            n_copy(to).wait_send()

    @pl.when(z != 7)
    def _():
        n_copy(0).wait_recv()

    @pl.when(r == 31)
    def _():
        for y in range(3):
            far_copy(y).wait_send()

    new_ref[...] = row_in[...]

    for h in range(2):

        @pl.when(gives_piece & jnp.logical_not(piece_self(h)))
        def _():
            piece_copy(h).wait_send()

    for b in range(8):

        @pl.when(lends & (b != part_at))
        def _():
            mirror_copy(b).wait_send()

    for step in range(4):
        for way in range(2):
            for rows in range(2):
                if step < 3 or rows == way:
                    g_copy(way, step, rows).wait_send()
    for i in range(2):

        @pl.when(near(i) >= yl)
        def _():
            y_copy(near(i)).wait_send()

    for y in range(4):

        @pl.when(y >= yl)
        def _():
            for d in (1, 2, 3):
                x_copy(y, d).wait_send()
            for d in range(4):
                k_copy(y, d).wait_send()

        if y > 0:

            @pl.when(y > yl)
            def _():
                c_copy(y).wait_send()


def shards(green, coupling):
    rows, cols, width = green.shape
    orbit = coupling.shape[0]
    high, wide = rows * orbit, cols * orbit
    matrix = jnp.transpose(green.reshape(rows, cols, orbit, orbit), (0, 2, 1, 3))
    matrix = matrix.reshape(high, wide)
    pair = coupling[:, None] * jnp.tile(coupling, cols)[None, :]
    vmem = pl.BlockSpec(memory_space=pltpu.VMEM)
    dma = pltpu.SemaphoreType.DMA
    collision, fresh = pl.pallas_call(
        kernel,
        out_shape=(
            jax.ShapeDtypeStruct((high, wide), BF),
            jax.ShapeDtypeStruct((8, 128), F32),
        ),
        in_specs=[vmem, vmem],
        out_specs=(vmem, vmem),
        scratch_shapes=[
            pltpu.VMEM((8, high, wide), BF),
            pltpu.VMEM((2, high, high), BF),
            pltpu.VMEM((2, high, high), BF),
            pltpu.VMEM((4, 8, high, high), BF),
            pltpu.VMEM((3, high, wide), BF),
            pltpu.VMEM((3, high, wide), BF),
            pltpu.VMEM((high, wide), F32),
            pltpu.VMEM((256, 128), F32),
            pltpu.VMEM((256, 128), F32),
            pltpu.VMEM((8, 128), F32),
            dma((2, 4, 2)),
            dma((2, 4, 2)),
            dma((8,)),
            dma((2,)),
            dma((2,)),
            dma((2,)),
            dma((4,)),
            dma((4,)),
            dma((4, 3)),
            dma((4, 3)),
            dma((4, 4)),
            dma((4, 4)),
            dma((3,)),
            dma((3,)),
            dma((3,)),
            dma(()),
            dma((7,)),
            dma(()),
        ],
        compiler_params=pltpu.CompilerParams(
            collective_id=0, has_side_effects=True, vmem_limit_bytes=40 << 20
        ),
        cost_estimate=pl.CostEstimate(
            flops=2 * high * wide * 8192, bytes_accessed=4 * high * wide, transcendentals=0
        ),
        name="collide",
    )(matrix, pair)
    collision = collision.reshape(rows, orbit, cols, orbit).transpose(0, 2, 1, 3)
    collision = collision.reshape(rows, cols, width)
    fresh = fresh.reshape(2, 4, 2, orbit).transpose(1, 2, 0, 3).reshape(cols, 128)
    return (collision, fresh.astype(BF))


def solution(mesh):
    placed = (P("row", "col", None), P())
    return jax.shard_map(
        shards,
        mesh=mesh,
        in_specs=placed,
        out_specs=(P("row", "col", None), P("col", "row")),
        check_vma=False,
    )
```

```python
import jax
import jax.numpy as jnp
from jax import lax
from jax.experimental import pallas as pl
from jax.experimental.pallas import tpu as pltpu
from jax.sharding import PartitionSpec as P

step_size = 0.01
MESH = pl.DeviceIdType.MESH
BF = jnp.bfloat16
F32 = jnp.float32


def kernel(
    x_ref,
    pair_ref,
    out_ref,
    new_ref,
    gz,
    mir,
    own,
    sig,
    part,
    cin,
    acc,
    held,
    row_mid,
    row_src,
    row_in,
    g_send,
    g_recv,
    m_send,
    m_recv,
    s_send,
    s_recv,
    y_send,
    y_recv,
    x_send,
    x_recv,
    h_send,
    h_recv,
    k_send,
    k_recv,
    c_send,
    c_recv,
    f_send,
    f_recv,
    n_send,
    n_recv,
):
    r = lax.axis_index("row")
    c = lax.axis_index("col")
    yl, z = r // 8, r % 8
    yh, x, k = c // 8, (c // 2) % 4, c % 2
    goal = c // 4

    def part_of(x_):
        m = jnp.where((x_ == 1) | (x_ == 2), 2, 0) + x_ // 2
        return 2 * jnp.where(yl % 2 == 0, m, 3 - m) + k

    def place_of(j):
        m = jnp.where(yl % 2 == 0, j // 2, 3 - j // 2)
        return jnp.where(m == 1, 3, (m + 1) // 2)

    part_at = part_of(x)
    m_at = part_at // 2

    def at(yl_, z_, yh_, x_, k_):
        return (yl_ * 8 + z_, yh_ * 8 + x_ * 2 + k_)

    def remote(src, dst, send, recv, device):
        return pltpu.make_async_remote_copy(
            src, dst, send, recv, device_id=device, device_id_type=MESH
        )

    up, down = at(yl, (z + 1) % 8, yh, x, k), at(yl, (z + 7) % 8, yh, x, k)
    other = at(yl, z, yh, x, 1 - k)
    across = at(yl, z, 1 - yh, x, k)

    gives_mirror = goal >= yl

    def mirror_to(h):
        return at(yl, (x % 2) * 4 + k * 2 + h, yh, place_of(z), z % 2)

    def mirror_self(h):
        return (z == part_at) & (z == (x % 2) * 4 + k * 2 + h)

    def mirror_from(s):
        return at(yl, part_at, yh, s * 2 + z // 4, (z // 2) % 2)

    def mirror_from_self(s):
        return (z == part_at) & (x == s * 2 + z // 4) & (k == (z // 2) % 2)

    gives_piece = yl >= goal

    def piece_to(h):
        return at(goal, z, yl // 2, (x + 4 + k * (2 * (x % 2) - 1)) % 4, h)

    def piece_self(h):
        return (goal == yl) & (k == 0) if h == 0 else False

    def piece_from(s):
        return at(2 * yh + s, z, yl // 2, (yl % 2) * 2 + m_at // 2, m_at % 2)

    def piece_from_self(s):
        mine = (2 * yh + s == yl) & (x == (yl % 2) * 2 + m_at // 2) & (k == m_at % 2)
        return mine & (yl // 2 == yh)

    def adds(q):
        return (q < yl) & ((yl != 2) | (q == 1))

    def one(flag):
        return jnp.where(flag, 1, 0)

    barrier = pltpu.get_barrier_semaphore()

    def greet(device):
        pl.semaphore_signal(barrier, inc=1, device_id=device, device_id_type=MESH)

    greet(up)
    greet(down)
    greet(other)
    for d in (1, 3):
        greet(at(yl, z, yh, (x + d) % 4, k))
    for s in range(2):

        @pl.when((2 * yh + s >= yl) & jnp.logical_not(mirror_from_self(s)))
        def _():
            greet(mirror_from(s))

        @pl.when((2 * yh + s >= yl) & jnp.logical_not(piece_from_self(s)))
        def _():
            greet(piece_from(s))

    @pl.when(3 - 2 * yh >= yl)
    def _():
        greet(across)

    for q in range(3):

        @pl.when(adds(q))
        def _():
            greet(at(q, z, yh, x, k))

    @pl.when(z != 7)
    def _():
        greet(at(yl, 7, yh, x, k))

    @pl.when((z == 7) & (yl != 3))
    def _():
        greet((31, c))

    peers = 5 + jnp.minimum(3 - yl, 2) + jnp.where(z == 7, 7, 0) + jnp.where(r == 31, 3, 0)
    peers += one(2 * yh + 1 >= yl)
    for h in range(2):
        peers += one(gives_mirror & jnp.logical_not(mirror_self(h)))
        peers += one(gives_piece & jnp.logical_not(piece_self(h)))
    pl.semaphore_wait(barrier, peers)

    def half_of(h):
        return x_ref.at[:, pl.ds(h * 256, 256)]

    def piece_copy(h):
        return remote(
            half_of(h), own.at[yl % 2], s_send.at[h], s_recv.at[yl % 2], piece_to(h)
        )

    def piece_arrival(s):
        return remote(half_of(0), own.at[s], s_send.at[0], s_recv.at[s], up)

    def g_copy(way, step, rows):
        held = (z - step + 8) % 8 if way == 0 else (z + step) % 8
        src = x_ref if step == 0 else gz.at[held]
        return remote(
            src.at[pl.ds(rows * 128, 128)],
            gz.at[held, pl.ds(rows * 128, 128)],
            g_send.at[way, step, rows],
            g_recv.at[way, step, rows],
            up if way == 0 else down,
        )

    def g_arrival(way, step, rows):
        held = (z - step + 7) % 8 if way == 0 else (z + step + 1) % 8
        return remote(
            x_ref.at[pl.ds(0, 128)],
            gz.at[held, pl.ds(rows * 128, 128)],
            g_send.at[way, step, rows],
            g_recv.at[way, step, rows],
            up,
        )

    def g_pass(step):
        for rows in range(2):
            for way in range(2):
                g_arrival(way, step - 1, rows).wait_recv()
                if step < 3 or rows == way:
                    g_copy(way, step, rows).start()

    def mirror_copy(h):
        return remote(
            half_of(h), mir.at[x // 2], m_send.at[h], m_recv.at[x // 2], mirror_to(h)
        )

    def mirror_arrival(s):
        return remote(half_of(0), mir.at[s], m_send.at[0], m_recv.at[s], up)

    for h in range(2):

        @pl.when(gives_mirror & jnp.logical_not(mirror_self(h)))
        def _():
            mirror_copy(h).start()

        @pl.when(gives_mirror & mirror_self(h))
        def _():
            mir[x // 2] = x_ref[:, h * 256 : (h + 1) * 256]

    for rows in range(2):
        for way in range(2):
            g_copy(way, 0, rows).start()
    for h in range(2):

        @pl.when(gives_piece & jnp.logical_not(piece_self(h)))
        def _():
            piece_copy(h).start()

        @pl.when(gives_piece & piece_self(h))
        def _():
            own[yl % 2] = x_ref[:, h * 256 : (h + 1) * 256]

    gz[z] = x_ref[...]

    def y_copy(y):
        return remote(
            sig.at[y, part_at], sig.at[y, part_at], y_send.at[y], y_recv.at[y], across
        )

    def x_copy(y, d):
        return remote(
            sig.at[y, part_at],
            sig.at[y, part_at],
            x_send.at[y, d // 2],
            x_recv.at[y, d // 2],
            at(yl, z, yh, (x + d) % 4, k),
        )

    def behind(d):
        return part_of((x + 4 - d) % 4)

    def x_arrival(y, d):
        j = behind(d)
        return remote(
            sig.at[y, j], sig.at[y, j], x_send.at[y, 0], x_recv.at[y, d // 2], up
        )

    def h_copy(y, d):
        rows = pl.ds((d // 2) * 128, 128)
        block = sig.at[y, behind(d), rows]
        return remote(
            block,
            block,
            h_send.at[y, d // 2],
            h_recv.at[y, d // 2],
            at(yl, z, yh, (x + d) % 4, k),
        )

    def h_arrival(y, d):
        block = sig.at[y, behind(2), pl.ds((d // 2) * 128, 128)]
        return remote(block, block, h_send.at[y, 0], h_recv.at[y, d // 2], up)

    def k_copy(y, d):
        block = sig.at[y, behind(d)]
        return remote(block, block, k_send.at[y, d], k_recv.at[y, d], other)

    def k_arrival(y, d):
        block = sig.at[y, behind(d) + 1 - 2 * k]
        return remote(block, block, k_send.at[y, d], k_recv.at[y, d], other)

    def spread(y):
        for d in (1, 3):
            x_copy(y, d).start()
        k_copy(y, 0).start()

    def pass_on(y, d):
        @pl.when(y >= yl)
        def _():
            x_arrival(y, d).wait_recv()
            h_copy(y, d).start()
            k_copy(y, d).start()

    def near(i):
        return 2 * yh + 1 - i

    def far(i):
        return 3 - 2 * yh - i

    late = (yh == 0) & (yl < 2)

    def early(i):
        return jnp.logical_not(late & (near(i) == yl))

    def make(i):
        i_near = i
        s = 1 - i
        y = near(i)

        @pl.when(y >= yl)
        def _():
            @pl.when(jnp.logical_not(mirror_from_self(s)))
            def _():
                mirror_arrival(s).wait_recv()

            @pl.when(jnp.logical_not(piece_from_self(s)))
            def _():
                piece_arrival(s).wait_recv()

            partner = mir[s].T
            pair = pair_ref[:, 0:256]
            later = lax.broadcasted_iota(jnp.int32, (64, 256), 1) // 64
            first = 32 * (y - yl) + 4 * z - 4 * part_at
            for i in range(4):
                rows = slice(i * 64, (i + 1) * 64)
                g = own[s, rows, :].astype(F32)
                value = pair * (g * g) * partner[rows].astype(F32)
                keep = later <= first + i
                sig[y, part_at, rows, :] = jnp.where(keep, value, 0.0).astype(BF)
            y_copy(y).start()

            @pl.when(early(i_near))
            def _():
                spread(y)

    def hand_on(i):
        y = far(i)

        @pl.when(y >= yl)
        def _():
            y_copy(y).wait_recv()
            spread(y)

    def swap(y):
        @pl.when(y >= yl)
        def _():
            for d in (1, 3):
                h_arrival(y, d).wait_recv()
            k_copy(y, 2).start()

    def c_copy(y):
        to, slot = y, yl
        if y == 2:
            to, slot = jnp.where(yl == 0, 1, 2), 1
        return remote(
            part.at[y - 1],
            cin.at[slot],
            c_send.at[y - 1],
            c_recv.at[slot],
            at(to, z, yh, x, k),
        )

    def c_arrival(q):
        return remote(part.at[0], cin.at[q], c_send.at[0], c_recv.at[q], up)

    def product(y):
        @pl.when(y >= yl)
        def _():
            swap(y)
            for d in range(4):
                k_arrival(y, d).wait_recv()
            total = jnp.zeros((256, 512), F32)
            for j in range(8):
                total += jnp.dot(sig[y, j], gz[j], preferred_element_type=F32)

            @pl.when((y > yl) & ((y != 2) | (yl != 1)))
            def _():
                part[y - 1] = total.astype(BF)
                c_copy(y).start()

            @pl.when((y == 2) & (yl == 1))
            def _():
                held[...] = total

            @pl.when(y == yl)
            def _():
                acc[...] = total

    def pass_both(y, flag):
        @pl.when(flag)
        def _():
            pass_on(y, 1)
            pass_on(y, 3)

    make(0)
    make(1)
    g_pass(1)
    pass_both(near(0), early(0))
    hand_on(0)
    g_pass(2)
    pass_both(near(1), early(1))
    hand_on(1)

    @pl.when(late)
    def _():
        spread(yl)

    pass_both(far(0), True)
    g_pass(3)
    pass_both(far(1), True)
    pass_both(yl, late)
    for way in range(2):
        g_arrival(way, 3, way).wait_recv()
    for y in (3, 2, 1, 0):
        product(y)

    @pl.when(yl == 1)
    def _():
        c_arrival(1).wait_recv()
        part[1] = (held[...] + cin[1].astype(F32)).astype(BF)
        c_copy(2).start()

    for q in range(3):

        @pl.when(adds(q))
        def _():
            c_arrival(q).wait_recv()
            acc[...] += cin[q].astype(F32)

    out_ref[...] = (step_size * acc[...]).astype(BF)

    def far_copy(y):
        return remote(
            row_src.at[pl.ds(y * 64, 64)],
            row_src.at[pl.ds(y * 64, 64)],
            f_send.at[y],
            f_recv,
            at(y, 7, yh, x, k),
        )

    def n_copy(to):
        return remote(
            row_src.at[pl.ds(pl.multiple_of(yl * 64 + to * 8, 8), 8)],
            row_in,
            n_send.at[to],
            n_recv,
            at(yl, to, yh, x, k),
        )

    @pl.when(r == 31)
    def _():
        for q in range(4):
            lanes = slice(q * 128, (q + 1) * 128)
            row_mid[q * 64 : (q + 1) * 64, :] = (
                x_ref[192:256, lanes].astype(F32) + step_size * acc[192:256, lanes]
            )
            for i in range(2):
                row_src[pl.ds(i * 4 + q, 32, stride=8), :] = row_mid[
                    pl.ds(q * 64 + i, 32, stride=2), :
                ]
        for y in range(3):
            far_copy(y).start()

    @pl.when(z == 7)
    def _():
        @pl.when(yl != 3)
        def _():
            remote(
                row_src.at[pl.ds(0, 64)],
                row_src.at[pl.ds(pl.multiple_of(yl * 64, 64), 64)],
                f_send.at[0],
                f_recv,
                other,
            ).wait_recv()

        for to in range(7):
            n_copy(to).start()
        row_in[...] = row_src[pl.ds(pl.multiple_of(yl * 64 + 56, 8), 8), :]
        for to in range(7):
            n_copy(to).wait_send()

    @pl.when(z != 7)
    def _():
        n_copy(0).wait_recv()

    @pl.when(r == 31)
    def _():
        for y in range(3):
            far_copy(y).wait_send()

    new_ref[...] = row_in[...]

    for h in range(2):

        @pl.when(gives_piece & jnp.logical_not(piece_self(h)))
        def _():
            piece_copy(h).wait_send()

    for h in range(2):

        @pl.when(gives_mirror & jnp.logical_not(mirror_self(h)))
        def _():
            mirror_copy(h).wait_send()

    for step in range(4):
        for way in range(2):
            for rows in range(2):
                if step < 3 or rows == way:
                    g_copy(way, step, rows).wait_send()
    for i in range(2):

        @pl.when(near(i) >= yl)
        def _():
            y_copy(near(i)).wait_send()

    for y in range(4):

        @pl.when(y >= yl)
        def _():
            for d in (1, 3):
                x_copy(y, d).wait_send()
                h_copy(y, d).wait_send()
            for d in range(4):
                k_copy(y, d).wait_send()

        if y > 0:

            @pl.when(y > yl)
            def _():
                c_copy(y).wait_send()


def shards(green, coupling):
    rows, cols, width = green.shape
    orbit = coupling.shape[0]
    high, wide = rows * orbit, cols * orbit
    matrix = jnp.transpose(green.reshape(rows, cols, orbit, orbit), (0, 2, 1, 3))
    matrix = matrix.reshape(high, wide)
    pair = coupling[:, None] * jnp.tile(coupling, cols)[None, :]
    vmem = pl.BlockSpec(memory_space=pltpu.VMEM)
    dma = pltpu.SemaphoreType.DMA
    collision, fresh = pl.pallas_call(
        kernel,
        out_shape=(
            jax.ShapeDtypeStruct((high, wide), BF),
            jax.ShapeDtypeStruct((8, 128), F32),
        ),
        in_specs=[vmem, vmem],
        out_specs=(vmem, vmem),
        scratch_shapes=[
            pltpu.VMEM((8, high, wide), BF),
            pltpu.VMEM((2, high, high), BF),
            pltpu.VMEM((2, high, high), BF),
            pltpu.VMEM((4, 8, high, high), BF),
            pltpu.VMEM((3, high, wide), BF),
            pltpu.VMEM((3, high, wide), BF),
            pltpu.VMEM((high, wide), F32),
            pltpu.VMEM((high, wide), F32),
            pltpu.VMEM((256, 128), F32),
            pltpu.VMEM((256, 128), F32),
            pltpu.VMEM((8, 128), F32),
            dma((2, 4, 2)),
            dma((2, 4, 2)),
            dma((2,)),
            dma((2,)),
            dma((2,)),
            dma((2,)),
            dma((4,)),
            dma((4,)),
            dma((4, 2)),
            dma((4, 2)),
            dma((4, 2)),
            dma((4, 2)),
            dma((4, 4)),
            dma((4, 4)),
            dma((3,)),
            dma((3,)),
            dma((3,)),
            dma(()),
            dma((7,)),
            dma(()),
        ],
        compiler_params=pltpu.CompilerParams(
            collective_id=0, has_side_effects=True, vmem_limit_bytes=40 << 20
        ),
        cost_estimate=pl.CostEstimate(
            flops=2 * high * wide * 8192, bytes_accessed=4 * high * wide, transcendentals=0
        ),
        name="collide",
    )(matrix, pair)
    collision = collision.reshape(rows, orbit, cols, orbit).transpose(0, 2, 1, 3)
    collision = collision.reshape(rows, cols, width)
    fresh = fresh.reshape(2, 4, 2, orbit).transpose(1, 2, 0, 3).reshape(cols, 128)
    return (collision, fresh.astype(BF))


def solution(mesh):
    placed = (P("row", "col", None), P())
    return jax.shard_map(
        shards,
        mesh=mesh,
        in_specs=placed,
        out_specs=(P("row", "col", None), P("col", "row")),
        check_vma=False,
    )
```

```python
import jax
import jax.numpy as jnp
from jax import lax
from jax.experimental import pallas as pl
from jax.experimental.pallas import tpu as pltpu
from jax.sharding import PartitionSpec as P

step_size = 0.01
MESH = pl.DeviceIdType.MESH
BF = jnp.bfloat16
F32 = jnp.float32


def kernel(
    x_ref,
    coupling_ref,
    out_ref,
    new_ref,
    gz,
    mir,
    own,
    sig,
    part,
    cin,
    relay,
    acc,
    held,
    row_mid,
    row_src,
    row_in,
    g_send,
    g_recv,
    m_send,
    m_recv,
    s_send,
    s_recv,
    y_send,
    y_recv,
    x_send,
    x_recv,
    h_send,
    h_recv,
    k_send,
    k_recv,
    c_send,
    c_recv,
    r_send,
    r_recv,
    q_send,
    q_recv,
    f_send,
    f_recv,
    n_send,
    n_recv,
):
    r = lax.axis_index("row")
    c = lax.axis_index("col")
    yl, z = r // 8, r % 8
    yh, x, k = c // 8, (c // 2) % 4, c % 2
    goal = c // 4

    def part_of(x_):
        m = jnp.where((x_ == 1) | (x_ == 2), 2, 0) + x_ // 2
        return 2 * jnp.where(yl % 2 == 0, m, 3 - m) + k

    def place_of(j):
        m = jnp.where(yl % 2 == 0, j // 2, 3 - j // 2)
        return jnp.where(m == 1, 3, (m + 1) // 2)

    part_at = part_of(x)
    m_at = part_at // 2

    def at(yl_, z_, yh_, x_, k_):
        return (yl_ * 8 + z_, yh_ * 8 + x_ * 2 + k_)

    def remote(src, dst, send, recv, device):
        return pltpu.make_async_remote_copy(
            src, dst, send, recv, device_id=device, device_id_type=MESH
        )

    up, down = at(yl, (z + 1) % 8, yh, x, k), at(yl, (z + 7) % 8, yh, x, k)
    other = at(yl, z, yh, x, 1 - k)
    across = at(yl, z, 1 - yh, x, k)

    gives_mirror = goal >= yl

    def mirror_to(h):
        return at(yl, (x % 2) * 4 + k * 2 + h, yh, place_of(z), z % 2)

    def mirror_self(h):
        return (z == part_at) & (z == (x % 2) * 4 + k * 2 + h)

    def mirror_from(s):
        return at(yl, part_at, yh, s * 2 + z // 4, (z // 2) % 2)

    def mirror_from_self(s):
        return (z == part_at) & (x == s * 2 + z // 4) & (k == (z // 2) % 2)

    gives_piece = yl >= goal

    def piece_to(h):
        return at(goal, z, yl // 2, (x + 4 + k * (2 * (x % 2) - 1)) % 4, h)

    def piece_self(h):
        return (goal == yl) & (k == 0) if h == 0 else False

    def piece_from(s):
        return at(2 * yh + s, z, yl // 2, (yl % 2) * 2 + m_at // 2, m_at % 2)

    def piece_from_self(s):
        mine = (2 * yh + s == yl) & (x == (yl % 2) * 2 + m_at // 2) & (k == m_at % 2)
        return mine & (yl // 2 == yh)

    def adds(q):
        return (q < yl) & ((yl == 1) | (q != 0))

    def one(flag):
        return jnp.where(flag, 1, 0)

    barrier = pltpu.get_barrier_semaphore()

    def greet(device):
        pl.semaphore_signal(barrier, inc=1, device_id=device, device_id_type=MESH)

    greet(up)
    greet(down)
    greet(other)
    for d in (1, 2, 3):
        greet(at(yl, z, yh, (x + d) % 4, k))
    for s in range(2):

        @pl.when((2 * yh + s >= yl) & jnp.logical_not(mirror_from_self(s)))
        def _():
            greet(mirror_from(s))

        @pl.when((2 * yh + s >= yl) & jnp.logical_not(piece_from_self(s)))
        def _():
            greet(piece_from(s))

    @pl.when(3 - 2 * yh >= yl)
    def _():
        greet(across)

    for q in range(3):

        @pl.when(adds(q))
        def _():
            greet(at(q, z, yh, x, k))

    @pl.when(yl == 1)
    def _():
        greet(at(0, z, 1 - yh, x, k))

    @pl.when(yl == 3)
    def _():
        greet(at(1, z, 1 - yh, x, k))

    @pl.when(z != 7)
    def _():
        greet(at(yl, 7, yh, x, k))

    @pl.when((z == 7) & (yl != 3))
    def _():
        greet((31, c))

    peers = 6 + jnp.minimum(3 - yl, 2) + one(yl == 1) + jnp.where(z == 7, 7, 0) + jnp.where(r == 31, 3, 0)
    peers += one(2 * yh + 1 >= yl)
    for h in range(2):
        peers += one(gives_mirror & jnp.logical_not(mirror_self(h)))
        peers += one(gives_piece & jnp.logical_not(piece_self(h)))
    pl.semaphore_wait(barrier, peers)

    def half_of(h):
        return x_ref.at[:, pl.ds(h * 256, 256)]

    def piece_copy(h):
        return remote(
            half_of(h), own.at[yl % 2], s_send.at[h], s_recv.at[yl % 2], piece_to(h)
        )

    def piece_arrival(s):
        return remote(half_of(0), own.at[s], s_send.at[0], s_recv.at[s], up)

    def g_copy(way, step, rows):
        held = (z - step + 8) % 8 if way == 0 else (z + step) % 8
        src = x_ref if step == 0 else gz.at[held]
        return remote(
            src.at[pl.ds(rows * 128, 128)],
            gz.at[held, pl.ds(rows * 128, 128)],
            g_send.at[way, step, rows],
            g_recv.at[way, step, rows],
            up if way == 0 else down,
        )

    def g_arrival(way, step, rows):
        held = (z - step + 7) % 8 if way == 0 else (z + step + 1) % 8
        return remote(
            x_ref.at[pl.ds(0, 128)],
            gz.at[held, pl.ds(rows * 128, 128)],
            g_send.at[way, step, rows],
            g_recv.at[way, step, rows],
            up,
        )

    def g_pass(step):
        for rows in range(2):
            for way in range(2):
                g_arrival(way, step - 1, rows).wait_recv()
                if step < 3 or rows == way:
                    g_copy(way, step, rows).start()

    def mirror_copy(h):
        return remote(
            half_of(h), mir.at[x // 2], m_send.at[h], m_recv.at[x // 2], mirror_to(h)
        )

    def mirror_arrival(s):
        return remote(half_of(0), mir.at[s], m_send.at[0], m_recv.at[s], up)

    for h in range(2):

        @pl.when(gives_mirror & jnp.logical_not(mirror_self(h)))
        def _():
            mirror_copy(h).start()

        @pl.when(gives_mirror & mirror_self(h))
        def _():
            mir[x // 2] = x_ref[:, h * 256 : (h + 1) * 256]

    for rows in range(2):
        for way in range(2):
            g_copy(way, 0, rows).start()
    for h in range(2):

        @pl.when(gives_piece & jnp.logical_not(piece_self(h)))
        def _():
            piece_copy(h).start()

        @pl.when(gives_piece & piece_self(h))
        def _():
            own[yl % 2] = x_ref[:, h * 256 : (h + 1) * 256]

    gz[z] = x_ref[...]

    def y_copy(y):
        return remote(
            sig.at[y, part_at], sig.at[y, part_at], y_send.at[y], y_recv.at[y], across
        )

    def x_copy(y, d):
        return remote(
            sig.at[y, part_at],
            sig.at[y, part_at],
            x_send.at[y, d // 2],
            x_recv.at[y, d // 2],
            at(yl, z, yh, (x + d) % 4, k),
        )

    def two_copy(y):
        return remote(
            sig.at[y, part_at],
            sig.at[y, part_at],
            h_send.at[y, 0],
            h_recv.at[y, 0],
            at(yl, z, yh, (x + 2) % 4, k),
        )

    def two_arrival(y):
        j = behind(2)
        return remote(
            sig.at[y, j], sig.at[y, j], h_send.at[y, 0], h_recv.at[y, 0], up
        )

    def behind(d):
        return part_of((x + 4 - d) % 4)

    def x_arrival(y, d):
        j = behind(d)
        return remote(
            sig.at[y, j], sig.at[y, j], x_send.at[y, 0], x_recv.at[y, d // 2], up
        )

    def h_copy(y, d):
        rows = pl.ds((d // 2) * 128, 128)
        block = sig.at[y, behind(d), rows]
        return remote(
            block,
            block,
            h_send.at[y, d // 2],
            h_recv.at[y, d // 2],
            at(yl, z, yh, (x + d) % 4, k),
        )

    def h_arrival(y, d):
        block = sig.at[y, behind(2), pl.ds((d // 2) * 128, 128)]
        return remote(block, block, h_send.at[y, 0], h_recv.at[y, d // 2], up)

    def k_copy(y, d):
        block = sig.at[y, behind(d)]
        return remote(block, block, k_send.at[y, d], k_recv.at[y, d], other)

    def k_arrival(y, d):
        block = sig.at[y, behind(d) + 1 - 2 * k]
        return remote(block, block, k_send.at[y, d], k_recv.at[y, d], other)

    def spread(y):
        for d in (1, 3):
            x_copy(y, d).start()
        k_copy(y, 0).start()

    def pass_on(y, d):
        @pl.when(y >= yl)
        def _():
            x_arrival(y, d).wait_recv()
            h_copy(y, d).start()
            k_copy(y, d).start()

    def near(i):
        return 2 * yh + 1 - i

    def far(i):
        return 3 - 2 * yh - i

    late = (yh == 0) & (yl < 2)

    def early(i):
        return jnp.logical_not(late & (near(i) == yl))

    strength = coupling_ref[...]
    square = jnp.broadcast_to(strength, (64, 64))
    diagonal = lax.broadcasted_iota(jnp.int32, (64, 64), 0) == lax.broadcasted_iota(
        jnp.int32, (64, 64), 1
    )
    column = jnp.sum(jnp.where(diagonal, square, 0.0), axis=1, keepdims=True)
    pair = column * jnp.concatenate([strength] * 4, axis=1)

    def make(i):
        i_near = i
        s = 1 - i
        y = near(i)

        @pl.when(y >= yl)
        def _():
            @pl.when(jnp.logical_not(mirror_from_self(s)))
            def _():
                mirror_arrival(s).wait_recv()

            @pl.when(jnp.logical_not(piece_from_self(s)))
            def _():
                piece_arrival(s).wait_recv()

            partner = mir[s].T
            later = lax.broadcasted_iota(jnp.int32, (64, 256), 1) // 64
            first = 32 * (y - yl) + 4 * z - 4 * part_at
            for i in range(4):
                rows = slice(i * 64, (i + 1) * 64)
                g = own[s, rows, :].astype(F32)
                value = pair * (g * g) * partner[rows].astype(F32)
                keep = later <= first + i
                sig[y, part_at, rows, :] = jnp.where(keep, value, 0.0).astype(BF)
            y_copy(y).start()

            @pl.when(early(i_near))
            def _():
                spread(y)

    def hand_on(i):
        y = far(i)

        @pl.when(y >= yl)
        def _():
            y_copy(y).wait_recv()
            spread(y)
            two_copy(y).start()

    def swap(y):
        @pl.when((y >= yl) & (y // 2 == yh))
        def _():
            for d in (1, 3):
                h_arrival(y, d).wait_recv()
            k_copy(y, 2).start()

    def collect(y):
        @pl.when(y >= yl)
        def _():
            for d in (1, 3):
                x_arrival(y, d).wait_recv()
                k_copy(y, d).start()
            two_arrival(y).wait_recv()
            k_copy(y, 2).start()

    def c_copy(y):
        to, slot = y, yl
        if y == 2:
            to, slot = jnp.where(yl == 0, 1, 2), 1
        return remote(
            part.at[y - 1],
            cin.at[slot],
            c_send.at[y - 1],
            c_recv.at[slot],
            at(to, z, yh, x, k),
        )

    def round_copy(i):
        rows = pl.ds(i * 128, 128)
        return remote(
            part.at[2, rows],
            relay.at[rows],
            r_send.at[i],
            r_recv.at[i],
            at(1, z, 1 - yh, x, k),
        )

    def round_pass(i):
        rows = pl.ds(i * 128, 128)
        return remote(
            relay.at[rows],
            cin.at[0, rows],
            q_send.at[i],
            q_recv.at[i],
            at(3, z, 1 - yh, x, k),
        )

    def c_arrival(q):
        return remote(part.at[0], cin.at[q], c_send.at[0], c_recv.at[q], up)

    def product(y):
        @pl.when(y >= yl)
        def _():
            swap(y)
            for d in range(4):
                k_arrival(y, d).wait_recv()
            total = jnp.zeros((256, 512), F32)
            for j in range(8):
                total += jnp.dot(sig[y, j], gz[j], preferred_element_type=F32)

            @pl.when((y > yl) & ((y != 2) | (yl != 1)))
            def _():
                part[y - 1] = total.astype(BF)
                if y < 3:
                    c_copy(y).start()
                else:

                    @pl.when(yl != 0)
                    def _():
                        c_copy(y).start()

                    @pl.when(yl == 0)
                    def _():
                        for i in range(2):
                            round_copy(i).start()

            @pl.when((y == 2) & (yl == 1))
            def _():
                held[...] = total

            @pl.when(y == yl)
            def _():
                acc[...] = total

    def pass_both(y, flag):
        @pl.when(flag)
        def _():
            pass_on(y, 1)
            pass_on(y, 3)

    make(0)
    make(1)
    g_pass(1)
    pass_both(near(0), early(0))
    hand_on(0)
    g_pass(2)
    pass_both(near(1), early(1))
    hand_on(1)

    @pl.when(late)
    def _():
        spread(yl)

    g_pass(3)
    for way in range(2):
        g_arrival(way, 3, way).wait_recv()
    for y in (3, 2, 1, 0):

        @pl.when(y // 2 != yh)
        def _():
            collect(y)

        if y == 1:
            pass_both(yl, late)
        product(y)

    @pl.when(yl == 1)
    def _():
        for i in range(2):
            round_copy(i).wait_recv()
            round_pass(i).start()
        c_arrival(1).wait_recv()
        part[1] = (held[...] + cin[1].astype(F32)).astype(BF)
        c_copy(2).start()

    for q in range(3):

        @pl.when(adds(q))
        def _():
            c_arrival(q).wait_recv()
            acc[...] += cin[q].astype(F32)

    @pl.when(yl == 3)
    def _():
        for i in range(2):
            rows = slice(i * 128, (i + 1) * 128)
            round_pass(i).wait_recv()
            acc[rows, :] += cin[0, rows, :].astype(F32)

    out_ref[...] = (step_size * acc[...]).astype(BF)

    def far_copy(y):
        return remote(
            row_src.at[pl.ds(y * 64, 64)],
            row_src.at[pl.ds(y * 64, 64)],
            f_send.at[y],
            f_recv,
            at(y, 7, yh, x, k),
        )

    def n_copy(to):
        return remote(
            row_src.at[pl.ds(pl.multiple_of(yl * 64 + to * 8, 8), 8)],
            row_in,
            n_send.at[to],
            n_recv,
            at(yl, to, yh, x, k),
        )

    @pl.when(r == 31)
    def _():
        for q in range(4):
            lanes = slice(q * 128, (q + 1) * 128)
            row_mid[q * 64 : (q + 1) * 64, :] = (
                x_ref[192:256, lanes].astype(F32) + step_size * acc[192:256, lanes]
            )
            for i in range(2):
                row_src[pl.ds(i * 4 + q, 32, stride=8), :] = row_mid[
                    pl.ds(q * 64 + i, 32, stride=2), :
                ]
        for y in range(3):
            far_copy(y).start()

    @pl.when(z == 7)
    def _():
        @pl.when(yl != 3)
        def _():
            remote(
                row_src.at[pl.ds(0, 64)],
                row_src.at[pl.ds(pl.multiple_of(yl * 64, 64), 64)],
                f_send.at[0],
                f_recv,
                other,
            ).wait_recv()

        for to in (3, 2, 4, 1, 5, 0, 6):
            n_copy(to).start()
        row_in[...] = row_src[pl.ds(pl.multiple_of(yl * 64 + 56, 8), 8), :]
        for to in range(7):
            n_copy(to).wait_send()

    @pl.when(z != 7)
    def _():
        n_copy(0).wait_recv()

    @pl.when(r == 31)
    def _():
        for y in range(3):
            far_copy(y).wait_send()

    new_ref[...] = row_in[...]

    for h in range(2):

        @pl.when(gives_piece & jnp.logical_not(piece_self(h)))
        def _():
            piece_copy(h).wait_send()

    for h in range(2):

        @pl.when(gives_mirror & jnp.logical_not(mirror_self(h)))
        def _():
            mirror_copy(h).wait_send()

    for step in range(4):
        for way in range(2):
            for rows in range(2):
                if step < 3 or rows == way:
                    g_copy(way, step, rows).wait_send()
    for i in range(2):

        @pl.when(near(i) >= yl)
        def _():
            y_copy(near(i)).wait_send()

    for y in range(4):

        @pl.when(y >= yl)
        def _():
            for d in (1, 3):
                x_copy(y, d).wait_send()

                @pl.when(y // 2 == yh)
                def _():
                    h_copy(y, d).wait_send()

            @pl.when(y // 2 != yh)
            def _():
                two_copy(y).wait_send()

            for d in range(4):
                k_copy(y, d).wait_send()

        if y > 0:

            @pl.when((y > yl) & ((y != 3) | (yl != 0)))
            def _():
                c_copy(y).wait_send()

    for i in range(2):

        @pl.when(yl == 0)
        def _():
            round_copy(i).wait_send()

        @pl.when(yl == 1)
        def _():
            round_pass(i).wait_send()


def shards(green, coupling):
    rows, cols, width = green.shape
    orbit = coupling.shape[0]
    high, wide = rows * orbit, cols * orbit
    matrix = jnp.transpose(green.reshape(rows, cols, orbit, orbit), (0, 2, 1, 3))
    matrix = matrix.reshape(high, wide)
    vmem = pl.BlockSpec(memory_space=pltpu.VMEM)
    dma = pltpu.SemaphoreType.DMA
    collision, fresh = pl.pallas_call(
        kernel,
        out_shape=(
            jax.ShapeDtypeStruct((high, wide), BF),
            jax.ShapeDtypeStruct((8, 128), F32),
        ),
        in_specs=[vmem, vmem],
        out_specs=(vmem, vmem),
        scratch_shapes=[
            pltpu.VMEM((8, high, wide), BF),
            pltpu.VMEM((2, high, high), BF),
            pltpu.VMEM((2, high, high), BF),
            pltpu.VMEM((4, 8, high, high), BF),
            pltpu.VMEM((3, high, wide), BF),
            pltpu.VMEM((3, high, wide), BF),
            pltpu.VMEM((high, wide), BF),
            pltpu.VMEM((high, wide), F32),
            pltpu.VMEM((high, wide), F32),
            pltpu.VMEM((256, 128), F32),
            pltpu.VMEM((256, 128), F32),
            pltpu.VMEM((8, 128), F32),
            dma((2, 4, 2)),
            dma((2, 4, 2)),
            dma((2,)),
            dma((2,)),
            dma((2,)),
            dma((2,)),
            dma((4,)),
            dma((4,)),
            dma((4, 2)),
            dma((4, 2)),
            dma((4, 2)),
            dma((4, 2)),
            dma((4, 4)),
            dma((4, 4)),
            dma((3,)),
            dma((3,)),
            dma((2,)),
            dma((2,)),
            dma((2,)),
            dma((2,)),
            dma((3,)),
            dma(()),
            dma((7,)),
            dma(()),
        ],
        compiler_params=pltpu.CompilerParams(
            collective_id=0, has_side_effects=True, vmem_limit_bytes=40 << 20
        ),
        cost_estimate=pl.CostEstimate(
            flops=2 * high * wide * 8192, bytes_accessed=4 * high * wide, transcendentals=0
        ),
        name="collide",
    )(matrix, coupling.reshape(1, orbit))
    collision = collision.reshape(rows, orbit, cols, orbit).transpose(0, 2, 1, 3)
    collision = collision.reshape(rows, cols, width)
    fresh = fresh.reshape(2, 4, 2, orbit).transpose(1, 2, 0, 3).reshape(cols, 128)
    return (collision, fresh.astype(BF))


def solution(mesh):
    placed = (P("row", "col", None), P())
    return jax.shard_map(
        shards,
        mesh=mesh,
        in_specs=placed,
        out_specs=(P("row", "col", None), P("col", "row")),
        check_vma=False,
    )
```

```python
import jax
import jax.numpy as jnp
from jax import lax
from jax.experimental import pallas as pl
from jax.experimental.pallas import tpu as pltpu
from jax.sharding import PartitionSpec as P

step_size = 0.01
MESH = pl.DeviceIdType.MESH
BF = jnp.bfloat16
F32 = jnp.float32


def kernel(
    x_ref,
    coupling_ref,
    out_ref,
    new_ref,
    gz,
    mir,
    own,
    sig,
    part,
    cin,
    relay,
    acc,
    held,
    row_mid,
    row_src,
    row_in,
    g_send,
    g_recv,
    m_send,
    m_recv,
    s_send,
    s_recv,
    y_send,
    y_recv,
    x_send,
    x_recv,
    h_send,
    h_recv,
    k_send,
    k_recv,
    c_send,
    c_recv,
    r_send,
    r_recv,
    q_send,
    q_recv,
    n_send,
    n_recv,
):
    r = lax.axis_index("row")
    c = lax.axis_index("col")
    yl, z = r // 8, r % 8
    yh, x, k = c // 8, (c // 2) % 4, c % 2
    goal = c // 4

    def part_of(x_):
        m = jnp.where((x_ == 1) | (x_ == 2), 2, 0) + x_ // 2
        return 2 * jnp.where(yl % 2 == 0, m, 3 - m) + k

    def place_of(j):
        m = jnp.where(yl % 2 == 0, j // 2, 3 - j // 2)
        return jnp.where(m == 1, 3, (m + 1) // 2)

    part_at = part_of(x)
    m_at = part_at // 2

    def at(yl_, z_, yh_, x_, k_):
        return (yl_ * 8 + z_, yh_ * 8 + x_ * 2 + k_)

    def remote(src, dst, send, recv, device):
        return pltpu.make_async_remote_copy(
            src, dst, send, recv, device_id=device, device_id_type=MESH
        )

    up, down = at(yl, (z + 1) % 8, yh, x, k), at(yl, (z + 7) % 8, yh, x, k)
    other = at(yl, z, yh, x, 1 - k)
    across = at(yl, z, 1 - yh, x, k)

    gives_mirror = goal >= yl

    def mirror_to(h):
        return at(yl, (x % 2) * 4 + k * 2 + h, yh, place_of(z), z % 2)

    def mirror_self(h):
        return (z == part_at) & (z == (x % 2) * 4 + k * 2 + h)

    def mirror_from(s):
        return at(yl, part_at, yh, s * 2 + z // 4, (z // 2) % 2)

    def mirror_from_self(s):
        return (z == part_at) & (x == s * 2 + z // 4) & (k == (z // 2) % 2)

    gives_piece = yl >= goal

    def piece_to(h):
        return at(goal, z, yl // 2, (x + 4 + k * (2 * (x % 2) - 1)) % 4, h)

    def piece_self(h):
        return (goal == yl) & (k == 0) if h == 0 else False

    def piece_from(s):
        return at(2 * yh + s, z, yl // 2, (yl % 2) * 2 + m_at // 2, m_at % 2)

    def piece_from_self(s):
        mine = (2 * yh + s == yl) & (x == (yl % 2) * 2 + m_at // 2) & (k == m_at % 2)
        return mine & (yl // 2 == yh)

    def adds(q):
        return (q < yl) & ((yl == 1) | (q != 0))

    def one(flag):
        return jnp.where(flag, 1, 0)

    barrier = pltpu.get_barrier_semaphore()

    def greet(device):
        pl.semaphore_signal(barrier, inc=1, device_id=device, device_id_type=MESH)

    greet(up)
    greet(down)
    greet(other)
    for d in (1, 2, 3):
        greet(at(yl, z, yh, (x + d) % 4, k))
    for s in range(2):

        @pl.when((2 * yh + s >= yl) & jnp.logical_not(mirror_from_self(s)))
        def _():
            greet(mirror_from(s))

        @pl.when((2 * yh + s >= yl) & jnp.logical_not(piece_from_self(s)))
        def _():
            greet(piece_from(s))

    @pl.when(3 - 2 * yh >= yl)
    def _():
        greet(across)

    for q in range(3):

        @pl.when(adds(q))
        def _():
            greet(at(q, z, yh, x, k))

    @pl.when(yl == 1)
    def _():
        greet(at(0, z, 1 - yh, x, k))

    @pl.when(yl == 3)
    def _():
        greet(at(1, z, 1 - yh, x, k))

    for q in range(4):

        @pl.when((z != 7) | (yl != q))
        def _():
            greet(at(q, 7, yh, x, k))

    peers = 6 + jnp.minimum(3 - yl, 2) + one(yl == 1) + jnp.where(z == 7, 31, 0)
    peers += one(2 * yh + 1 >= yl)
    for h in range(2):
        peers += one(gives_mirror & jnp.logical_not(mirror_self(h)))
        peers += one(gives_piece & jnp.logical_not(piece_self(h)))
    pl.semaphore_wait(barrier, peers)

    def half_of(h):
        return x_ref.at[:, pl.ds(h * 256, 256)]

    def piece_copy(h):
        return remote(
            half_of(h), own.at[yl % 2], s_send.at[h], s_recv.at[yl % 2], piece_to(h)
        )

    def piece_arrival(s):
        return remote(half_of(0), own.at[s], s_send.at[0], s_recv.at[s], up)

    def g_copy(way, step, rows):
        held = (z - step + 8) % 8 if way == 0 else (z + step) % 8
        src = x_ref if step == 0 else gz.at[held]
        return remote(
            src.at[pl.ds(rows * 128, 128)],
            gz.at[held, pl.ds(rows * 128, 128)],
            g_send.at[way, step, rows],
            g_recv.at[way, step, rows],
            up if way == 0 else down,
        )

    def g_arrival(way, step, rows):
        held = (z - step + 7) % 8 if way == 0 else (z + step + 1) % 8
        return remote(
            x_ref.at[pl.ds(0, 128)],
            gz.at[held, pl.ds(rows * 128, 128)],
            g_send.at[way, step, rows],
            g_recv.at[way, step, rows],
            up,
        )

    def g_pass(step):
        for rows in range(2):
            for way in range(2):
                g_arrival(way, step - 1, rows).wait_recv()
                if step < 3 or rows == way:
                    g_copy(way, step, rows).start()

    def mirror_copy(h):
        return remote(
            half_of(h), mir.at[x // 2], m_send.at[h], m_recv.at[x // 2], mirror_to(h)
        )

    def mirror_arrival(s):
        return remote(half_of(0), mir.at[s], m_send.at[0], m_recv.at[s], up)

    for h in range(2):

        @pl.when(gives_mirror & jnp.logical_not(mirror_self(h)))
        def _():
            mirror_copy(h).start()

        @pl.when(gives_mirror & mirror_self(h))
        def _():
            mir[x // 2] = x_ref[:, h * 256 : (h + 1) * 256]

    for rows in range(2):
        for way in range(2):
            g_copy(way, 0, rows).start()
    for h in range(2):

        @pl.when(gives_piece & jnp.logical_not(piece_self(h)))
        def _():
            piece_copy(h).start()

        @pl.when(gives_piece & piece_self(h))
        def _():
            own[yl % 2] = x_ref[:, h * 256 : (h + 1) * 256]

    gz[z] = x_ref[...]

    def y_copy(y):
        return remote(
            sig.at[y, part_at], sig.at[y, part_at], y_send.at[y], y_recv.at[y], across
        )

    def x_copy(y, d):
        return remote(
            sig.at[y, part_at],
            sig.at[y, part_at],
            x_send.at[y, d // 2],
            x_recv.at[y, d // 2],
            at(yl, z, yh, (x + d) % 4, k),
        )

    def two_copy(y):
        return remote(
            sig.at[y, part_at],
            sig.at[y, part_at],
            h_send.at[y, 0],
            h_recv.at[y, 0],
            at(yl, z, yh, (x + 2) % 4, k),
        )

    def two_arrival(y):
        j = behind(2)
        return remote(
            sig.at[y, j], sig.at[y, j], h_send.at[y, 0], h_recv.at[y, 0], up
        )

    def behind(d):
        return part_of((x + 4 - d) % 4)

    def x_arrival(y, d):
        j = behind(d)
        return remote(
            sig.at[y, j], sig.at[y, j], x_send.at[y, 0], x_recv.at[y, d // 2], up
        )

    def h_copy(y, d):
        rows = pl.ds((d // 2) * 128, 128)
        block = sig.at[y, behind(d), rows]
        return remote(
            block,
            block,
            h_send.at[y, d // 2],
            h_recv.at[y, d // 2],
            at(yl, z, yh, (x + d) % 4, k),
        )

    def h_arrival(y, d):
        block = sig.at[y, behind(2), pl.ds((d // 2) * 128, 128)]
        return remote(block, block, h_send.at[y, 0], h_recv.at[y, d // 2], up)

    def k_copy(y, d):
        block = sig.at[y, behind(d)]
        return remote(block, block, k_send.at[y, d], k_recv.at[y, d], other)

    def k_arrival(y, d):
        block = sig.at[y, behind(d) + 1 - 2 * k]
        return remote(block, block, k_send.at[y, d], k_recv.at[y, d], other)

    def spread(y):
        for d in (1, 3):
            x_copy(y, d).start()
        k_copy(y, 0).start()

    def pass_on(y, d):
        @pl.when(y >= yl)
        def _():
            x_arrival(y, d).wait_recv()
            h_copy(y, d).start()
            k_copy(y, d).start()

    def near(i):
        return 2 * yh + 1 - i

    def far(i):
        return 3 - 2 * yh - i

    late = (yh == 0) & (yl < 2)

    def early(i):
        return jnp.logical_not(late & (near(i) == yl))

    strength = coupling_ref[...]
    square = jnp.broadcast_to(strength, (64, 64))
    diagonal = lax.broadcasted_iota(jnp.int32, (64, 64), 0) == lax.broadcasted_iota(
        jnp.int32, (64, 64), 1
    )
    column = jnp.sum(jnp.where(diagonal, square, 0.0), axis=1, keepdims=True)
    pair = column * jnp.concatenate([strength] * 4, axis=1)

    def make(i):
        i_near = i
        s = 1 - i
        y = near(i)

        @pl.when(y >= yl)
        def _():
            @pl.when(jnp.logical_not(mirror_from_self(s)))
            def _():
                mirror_arrival(s).wait_recv()

            @pl.when(jnp.logical_not(piece_from_self(s)))
            def _():
                piece_arrival(s).wait_recv()

            partner = mir[s].T
            later = lax.broadcasted_iota(jnp.int32, (64, 256), 1) // 64
            first = 32 * (y - yl) + 4 * z - 4 * part_at
            for i in range(4):
                rows = slice(i * 64, (i + 1) * 64)
                g = own[s, rows, :].astype(F32)
                value = pair * (g * g) * partner[rows].astype(F32)
                keep = later <= first + i
                sig[y, part_at, rows, :] = jnp.where(keep, value, 0.0).astype(BF)
            y_copy(y).start()

            @pl.when(early(i_near))
            def _():
                spread(y)

    def hand_on(i):
        y = far(i)

        @pl.when(y >= yl)
        def _():
            y_copy(y).wait_recv()
            spread(y)
            two_copy(y).start()

    def swap(y):
        @pl.when((y >= yl) & (y // 2 == yh))
        def _():
            for d in (1, 3):
                h_arrival(y, d).wait_recv()
            k_copy(y, 2).start()

    def collect(y):
        @pl.when(y >= yl)
        def _():
            for d in (1, 3):
                x_arrival(y, d).wait_recv()
                k_copy(y, d).start()
            two_arrival(y).wait_recv()
            k_copy(y, 2).start()

    def c_copy(y):
        to, slot = y, yl
        if y == 2:
            to, slot = jnp.where(yl == 0, 1, 2), 1
        return remote(
            part.at[y - 1],
            cin.at[slot],
            c_send.at[y - 1],
            c_recv.at[slot],
            at(to, z, yh, x, k),
        )

    def round_copy(i):
        rows = pl.ds(i * 128, 128)
        return remote(
            part.at[2, rows],
            relay.at[rows],
            r_send.at[i],
            r_recv.at[i],
            at(1, z, 1 - yh, x, k),
        )

    def round_pass(i):
        rows = pl.ds(i * 128, 128)
        return remote(
            relay.at[rows],
            cin.at[0, rows],
            q_send.at[i],
            q_recv.at[i],
            at(3, z, 1 - yh, x, k),
        )

    def c_arrival(q):
        return remote(part.at[0], cin.at[q], c_send.at[0], c_recv.at[q], up)

    def product(y):
        @pl.when(y >= yl)
        def _():
            swap(y)
            for d in range(4):
                k_arrival(y, d).wait_recv()
            total = jnp.zeros((256, 512), F32)
            for j in range(8):
                total += jnp.dot(sig[y, j], gz[j], preferred_element_type=F32)

            if y == 3:
                for q in range(4):
                    row_mid[q * 64 : (q + 1) * 64, :] = (
                        step_size * total[192:256, q * 128 : (q + 1) * 128]
                    )

            @pl.when((y > yl) & ((y != 2) | (yl != 1)))
            def _():
                part[y - 1] = total.astype(BF)
                if y < 3:
                    c_copy(y).start()
                else:

                    @pl.when(yl != 0)
                    def _():
                        c_copy(y).start()

                    @pl.when(yl == 0)
                    def _():
                        for i in range(2):
                            round_copy(i).start()

            @pl.when((y == 2) & (yl == 1))
            def _():
                held[...] = total

            @pl.when(y == yl)
            def _():
                acc[...] = total

    def pass_both(y, flag):
        @pl.when(flag)
        def _():
            pass_on(y, 1)
            pass_on(y, 3)

    make(0)
    make(1)
    g_pass(1)
    pass_both(near(0), early(0))
    hand_on(0)
    g_pass(2)
    pass_both(near(1), early(1))
    hand_on(1)

    @pl.when(late)
    def _():
        spread(yl)

    g_pass(3)
    for way in range(2):
        g_arrival(way, 3, way).wait_recv()
    for y in (3, 2, 1, 0):

        @pl.when(y // 2 != yh)
        def _():
            collect(y)

        if y == 1:
            pass_both(yl, late)
        product(y)

    def n_copy(to):
        return remote(
            row_src.at[pl.ds(pl.multiple_of(to * 8, 8), 8)],
            row_in.at[yl],
            n_send.at[to],
            n_recv.at[yl],
            (to, c),
        )

    @pl.when(z == 7)
    def _():
        @pl.when(yl == 3)
        def _():
            for q in range(4):
                row_mid[q * 64 : (q + 1) * 64, :] += x_ref[
                    192:256, q * 128 : (q + 1) * 128
                ].astype(F32)

        for q in range(4):
            for i in range(2):
                row_src[pl.ds(i * 4 + q, 32, stride=8), :] = row_mid[
                    pl.ds(q * 64 + i, 32, stride=2), :
                ]

        @pl.loop(0, 32)
        def _(to):
            @pl.when(to != r)
            def _():
                n_copy(to).start()

        row_in[yl] = row_src[pl.ds(pl.multiple_of(r * 8, 8), 8), :]

    @pl.when(yl == 1)
    def _():
        for i in range(2):
            round_copy(i).wait_recv()
            round_pass(i).start()
        c_arrival(1).wait_recv()
        part[1] = (held[...] + cin[1].astype(F32)).astype(BF)
        c_copy(2).start()

    for q in range(3):

        @pl.when(adds(q))
        def _():
            c_arrival(q).wait_recv()
            acc[...] += cin[q].astype(F32)

    @pl.when(yl == 3)
    def _():
        for i in range(2):
            rows = slice(i * 128, (i + 1) * 128)
            round_pass(i).wait_recv()
            acc[rows, :] += cin[0, rows, :].astype(F32)

    out_ref[...] = (step_size * acc[...]).astype(BF)

    for q in range(4):

        @pl.when((z != 7) | (yl != q))
        def _():
            remote(
                row_src.at[pl.ds(0, 8)], row_in.at[q], n_send.at[0], n_recv.at[q], up
            ).wait_recv()

    new_ref[...] = (row_in[0] + row_in[1]) + (row_in[2] + row_in[3])

    @pl.when(z == 7)
    def _():
        @pl.loop(0, 32)
        def _(to):
            @pl.when(to != r)
            def _():
                n_copy(to).wait_send()

    for h in range(2):

        @pl.when(gives_piece & jnp.logical_not(piece_self(h)))
        def _():
            piece_copy(h).wait_send()

    for h in range(2):

        @pl.when(gives_mirror & jnp.logical_not(mirror_self(h)))
        def _():
            mirror_copy(h).wait_send()

    for step in range(4):
        for way in range(2):
            for rows in range(2):
                if step < 3 or rows == way:
                    g_copy(way, step, rows).wait_send()
    for i in range(2):

        @pl.when(near(i) >= yl)
        def _():
            y_copy(near(i)).wait_send()

    for y in range(4):

        @pl.when(y >= yl)
        def _():
            for d in (1, 3):
                x_copy(y, d).wait_send()

                @pl.when(y // 2 == yh)
                def _():
                    h_copy(y, d).wait_send()

            @pl.when(y // 2 != yh)
            def _():
                two_copy(y).wait_send()

            for d in range(4):
                k_copy(y, d).wait_send()

        if y > 0:

            @pl.when((y > yl) & ((y != 3) | (yl != 0)))
            def _():
                c_copy(y).wait_send()

    for i in range(2):

        @pl.when(yl == 0)
        def _():
            round_copy(i).wait_send()

        @pl.when(yl == 1)
        def _():
            round_pass(i).wait_send()


def shards(green, coupling):
    rows, cols, width = green.shape
    orbit = coupling.shape[0]
    high, wide = rows * orbit, cols * orbit
    matrix = jnp.transpose(green.reshape(rows, cols, orbit, orbit), (0, 2, 1, 3))
    matrix = matrix.reshape(high, wide)
    vmem = pl.BlockSpec(memory_space=pltpu.VMEM)
    dma = pltpu.SemaphoreType.DMA
    collision, fresh = pl.pallas_call(
        kernel,
        out_shape=(
            jax.ShapeDtypeStruct((high, wide), BF),
            jax.ShapeDtypeStruct((8, 128), F32),
        ),
        in_specs=[vmem, vmem],
        out_specs=(vmem, vmem),
        scratch_shapes=[
            pltpu.VMEM((8, high, wide), BF),
            pltpu.VMEM((2, high, high), BF),
            pltpu.VMEM((2, high, high), BF),
            pltpu.VMEM((4, 8, high, high), BF),
            pltpu.VMEM((3, high, wide), BF),
            pltpu.VMEM((3, high, wide), BF),
            pltpu.VMEM((high, wide), BF),
            pltpu.VMEM((high, wide), F32),
            pltpu.VMEM((high, wide), F32),
            pltpu.VMEM((256, 128), F32),
            pltpu.VMEM((256, 128), F32),
            pltpu.VMEM((4, 8, 128), F32),
            dma((2, 4, 2)),
            dma((2, 4, 2)),
            dma((2,)),
            dma((2,)),
            dma((2,)),
            dma((2,)),
            dma((4,)),
            dma((4,)),
            dma((4, 2)),
            dma((4, 2)),
            dma((4, 2)),
            dma((4, 2)),
            dma((4, 4)),
            dma((4, 4)),
            dma((3,)),
            dma((3,)),
            dma((2,)),
            dma((2,)),
            dma((2,)),
            dma((2,)),
            dma((32,)),
            dma((4,)),
        ],
        compiler_params=pltpu.CompilerParams(
            collective_id=0, has_side_effects=True, vmem_limit_bytes=40 << 20
        ),
        cost_estimate=pl.CostEstimate(
            flops=2 * high * wide * 8192, bytes_accessed=4 * high * wide, transcendentals=0
        ),
        name="collide",
    )(matrix, coupling.reshape(1, orbit))
    collision = collision.reshape(rows, orbit, cols, orbit).transpose(0, 2, 1, 3)
    collision = collision.reshape(rows, cols, width)
    fresh = fresh.reshape(2, 4, 2, orbit).transpose(1, 2, 0, 3).reshape(cols, 128)
    return (collision, fresh.astype(BF))


def solution(mesh):
    placed = (P("row", "col", None), P())
    return jax.shard_map(
        shards,
        mesh=mesh,
        in_specs=placed,
        out_specs=(P("row", "col", None), P("col", "row")),
        check_vma=False,
    )
```

```python
import jax
import jax.numpy as jnp
from jax import lax
from jax.experimental import pallas as pl
from jax.experimental.pallas import tpu as pltpu
from jax.sharding import PartitionSpec as P

step_size = 0.01
MESH = pl.DeviceIdType.MESH
BF = jnp.bfloat16
F32 = jnp.float32


def kernel(
    green_ref,
    strength_ref,
    out_ref,
    new_ref,
    raw,
    coupling_ref,
    x_ref,
    in_sem,
    gz,
    mir,
    own,
    sig,
    part,
    cin,
    relay,
    acc,
    held,
    row_mid,
    row_src,
    row_in,
    g_send,
    g_recv,
    m_send,
    m_recv,
    s_send,
    s_recv,
    y_send,
    y_recv,
    x_send,
    x_recv,
    h_send,
    h_recv,
    k_send,
    k_recv,
    c_send,
    c_recv,
    r_send,
    r_recv,
    q_send,
    q_recv,
    n_send,
    n_recv,
):
    r = lax.axis_index("row")
    c = lax.axis_index("col")
    yl, z = r // 8, r % 8
    yh, x, k = c // 8, (c // 2) % 4, c % 2
    goal = c // 4

    def part_of(x_):
        m = jnp.where((x_ == 1) | (x_ == 2), 2, 0) + x_ // 2
        return 2 * jnp.where(yl % 2 == 0, m, 3 - m) + k

    def place_of(j):
        m = jnp.where(yl % 2 == 0, j // 2, 3 - j // 2)
        return jnp.where(m == 1, 3, (m + 1) // 2)

    part_at = part_of(x)
    m_at = part_at // 2

    def at(yl_, z_, yh_, x_, k_):
        return (yl_ * 8 + z_, yh_ * 8 + x_ * 2 + k_)

    def remote(src, dst, send, recv, device):
        return pltpu.make_async_remote_copy(
            src, dst, send, recv, device_id=device, device_id_type=MESH
        )

    up, down = at(yl, (z + 1) % 8, yh, x, k), at(yl, (z + 7) % 8, yh, x, k)
    other = at(yl, z, yh, x, 1 - k)
    across = at(yl, z, 1 - yh, x, k)

    gives_mirror = goal >= yl

    def mirror_to(h):
        return at(yl, (x % 2) * 4 + k * 2 + h, yh, place_of(z), z % 2)

    def mirror_self(h):
        return (z == part_at) & (z == (x % 2) * 4 + k * 2 + h)

    def mirror_from(s):
        return at(yl, part_at, yh, s * 2 + z // 4, (z // 2) % 2)

    def mirror_from_self(s):
        return (z == part_at) & (x == s * 2 + z // 4) & (k == (z // 2) % 2)

    gives_piece = yl >= goal

    def piece_to(h):
        return at(goal, z, yl // 2, (x + 4 + k * (2 * (x % 2) - 1)) % 4, h)

    def piece_self(h):
        return (goal == yl) & (k == 0) if h == 0 else False

    def piece_from(s):
        return at(2 * yh + s, z, yl // 2, (yl % 2) * 2 + m_at // 2, m_at % 2)

    def piece_from_self(s):
        mine = (2 * yh + s == yl) & (x == (yl % 2) * 2 + m_at // 2) & (k == m_at % 2)
        return mine & (yl // 2 == yh)

    def adds(q):
        return (q < yl) & ((yl == 1) | (q != 0))

    def one(flag):
        return jnp.where(flag, 1, 0)

    barrier = pltpu.get_barrier_semaphore()
    loads = [
        pltpu.make_async_copy(green_ref, raw, in_sem.at[0]),
        pltpu.make_async_copy(strength_ref, coupling_ref, in_sem.at[1]),
    ]
    for load in loads:
        load.start()

    def greet(device):
        pl.semaphore_signal(barrier, inc=1, device_id=device, device_id_type=MESH)

    greet(up)
    greet(down)
    greet(other)
    for d in (1, 2, 3):
        greet(at(yl, z, yh, (x + d) % 4, k))
    for s in range(2):

        @pl.when((2 * yh + s >= yl) & jnp.logical_not(mirror_from_self(s)))
        def _():
            greet(mirror_from(s))

        @pl.when((2 * yh + s >= yl) & jnp.logical_not(piece_from_self(s)))
        def _():
            greet(piece_from(s))

    @pl.when(3 - 2 * yh >= yl)
    def _():
        greet(across)

    for q in range(3):

        @pl.when(adds(q))
        def _():
            greet(at(q, z, yh, x, k))

    @pl.when(yl == 1)
    def _():
        greet(at(0, z, 1 - yh, x, k))

    @pl.when(yl == 3)
    def _():
        greet(at(1, z, 1 - yh, x, k))

    for q in range(4):

        @pl.when((z != 7) | (yl != q))
        def _():
            greet(at(q, 7, yh, x, k))

    for load in loads:
        load.wait()
    for t in range(4):
        block = raw[t].reshape(8, 64, 64).swapaxes(0, 1).reshape(64, 512)
        x_ref[t * 64 : (t + 1) * 64, :] = block

    peers = 6 + jnp.minimum(3 - yl, 2) + one(yl == 1) + jnp.where(z == 7, 31, 0)
    peers += one(2 * yh + 1 >= yl)
    for h in range(2):
        peers += one(gives_mirror & jnp.logical_not(mirror_self(h)))
        peers += one(gives_piece & jnp.logical_not(piece_self(h)))
    pl.semaphore_wait(barrier, peers)

    def half_of(h):
        return x_ref.at[:, pl.ds(h * 256, 256)]

    def piece_copy(h):
        return remote(
            half_of(h), own.at[yl % 2], s_send.at[h], s_recv.at[yl % 2], piece_to(h)
        )

    def piece_arrival(s):
        return remote(half_of(0), own.at[s], s_send.at[0], s_recv.at[s], up)

    def g_copy(way, step, rows):
        held = (z - step + 8) % 8 if way == 0 else (z + step) % 8
        src = x_ref if step == 0 else gz.at[held]
        return remote(
            src.at[pl.ds(rows * 128, 128)],
            gz.at[held, pl.ds(rows * 128, 128)],
            g_send.at[way, step, rows],
            g_recv.at[way, step, rows],
            up if way == 0 else down,
        )

    def g_arrival(way, step, rows):
        held = (z - step + 7) % 8 if way == 0 else (z + step + 1) % 8
        return remote(
            x_ref.at[pl.ds(0, 128)],
            gz.at[held, pl.ds(rows * 128, 128)],
            g_send.at[way, step, rows],
            g_recv.at[way, step, rows],
            up,
        )

    def g_pass(step):
        for rows in range(2):
            for way in range(2):
                g_arrival(way, step - 1, rows).wait_recv()
                if step < 3 or rows == way:
                    g_copy(way, step, rows).start()

    def mirror_copy(h):
        return remote(
            half_of(h), mir.at[x // 2], m_send.at[h], m_recv.at[x // 2], mirror_to(h)
        )

    def mirror_arrival(s):
        return remote(half_of(0), mir.at[s], m_send.at[0], m_recv.at[s], up)

    for h in range(2):

        @pl.when(gives_mirror & jnp.logical_not(mirror_self(h)))
        def _():
            mirror_copy(h).start()

        @pl.when(gives_mirror & mirror_self(h))
        def _():
            mir[x // 2] = x_ref[:, h * 256 : (h + 1) * 256]

    for rows in range(2):
        for way in range(2):
            g_copy(way, 0, rows).start()
    for h in range(2):

        @pl.when(gives_piece & jnp.logical_not(piece_self(h)))
        def _():
            piece_copy(h).start()

        @pl.when(gives_piece & piece_self(h))
        def _():
            own[yl % 2] = x_ref[:, h * 256 : (h + 1) * 256]

    gz[z] = x_ref[...]

    def y_copy(y):
        return remote(
            sig.at[y, part_at], sig.at[y, part_at], y_send.at[y], y_recv.at[y], across
        )

    def x_copy(y, d):
        return remote(
            sig.at[y, part_at],
            sig.at[y, part_at],
            x_send.at[y, d // 2],
            x_recv.at[y, d // 2],
            at(yl, z, yh, (x + d) % 4, k),
        )

    def two_copy(y):
        return remote(
            sig.at[y, part_at],
            sig.at[y, part_at],
            h_send.at[y, 0],
            h_recv.at[y, 0],
            at(yl, z, yh, (x + 2) % 4, k),
        )

    def two_arrival(y):
        j = behind(2)
        return remote(
            sig.at[y, j], sig.at[y, j], h_send.at[y, 0], h_recv.at[y, 0], up
        )

    def behind(d):
        return part_of((x + 4 - d) % 4)

    def x_arrival(y, d):
        j = behind(d)
        return remote(
            sig.at[y, j], sig.at[y, j], x_send.at[y, 0], x_recv.at[y, d // 2], up
        )

    def h_copy(y, d):
        rows = pl.ds((d // 2) * 128, 128)
        block = sig.at[y, behind(d), rows]
        return remote(
            block,
            block,
            h_send.at[y, d // 2],
            h_recv.at[y, d // 2],
            at(yl, z, yh, (x + d) % 4, k),
        )

    def h_arrival(y, d):
        block = sig.at[y, behind(2), pl.ds((d // 2) * 128, 128)]
        return remote(block, block, h_send.at[y, 0], h_recv.at[y, d // 2], up)

    def k_copy(y, d):
        block = sig.at[y, behind(d)]
        return remote(block, block, k_send.at[y, d], k_recv.at[y, d], other)

    def k_arrival(y, d):
        block = sig.at[y, behind(d) + 1 - 2 * k]
        return remote(block, block, k_send.at[y, d], k_recv.at[y, d], other)

    def spread(y):
        for d in (1, 3):
            x_copy(y, d).start()
        k_copy(y, 0).start()

    def pass_on(y, d):
        @pl.when(y >= yl)
        def _():
            x_arrival(y, d).wait_recv()
            h_copy(y, d).start()
            k_copy(y, d).start()

    def near(i):
        return 2 * yh + 1 - i

    def far(i):
        return 3 - 2 * yh - i

    late = (yh == 0) & (yl < 2)

    def early(i):
        return jnp.logical_not(late & (near(i) == yl))

    strength = coupling_ref[...]
    square = jnp.broadcast_to(strength, (64, 64))
    diagonal = lax.broadcasted_iota(jnp.int32, (64, 64), 0) == lax.broadcasted_iota(
        jnp.int32, (64, 64), 1
    )
    column = jnp.sum(jnp.where(diagonal, square, 0.0), axis=1, keepdims=True)
    pair = column * jnp.concatenate([strength] * 4, axis=1)

    def make(i):
        i_near = i
        s = 1 - i
        y = near(i)

        @pl.when(y >= yl)
        def _():
            @pl.when(jnp.logical_not(mirror_from_self(s)))
            def _():
                mirror_arrival(s).wait_recv()

            @pl.when(jnp.logical_not(piece_from_self(s)))
            def _():
                piece_arrival(s).wait_recv()

            partner = mir[s].T
            later = lax.broadcasted_iota(jnp.int32, (64, 256), 1) // 64
            first = 32 * (y - yl) + 4 * z - 4 * part_at
            for i in range(4):
                rows = slice(i * 64, (i + 1) * 64)
                g = own[s, rows, :].astype(F32)
                value = pair * (g * g) * partner[rows].astype(F32)
                keep = later <= first + i
                sig[y, part_at, rows, :] = jnp.where(keep, value, 0.0).astype(BF)
            y_copy(y).start()

            @pl.when(early(i_near))
            def _():
                spread(y)

    def hand_on(i):
        y = far(i)

        @pl.when(y >= yl)
        def _():
            y_copy(y).wait_recv()
            spread(y)
            two_copy(y).start()

    def swap(y):
        @pl.when((y >= yl) & (y // 2 == yh))
        def _():
            for d in (1, 3):
                h_arrival(y, d).wait_recv()
            k_copy(y, 2).start()

    def collect(y):
        @pl.when(y >= yl)
        def _():
            for d in (1, 3):
                x_arrival(y, d).wait_recv()
                k_copy(y, d).start()
            two_arrival(y).wait_recv()
            k_copy(y, 2).start()

    def c_copy(y):
        to, slot = y, yl
        if y == 2:
            to, slot = jnp.where(yl == 0, 1, 2), 1
        return remote(
            part.at[y - 1],
            cin.at[slot],
            c_send.at[y - 1],
            c_recv.at[slot],
            at(to, z, yh, x, k),
        )

    def round_copy(i):
        rows = pl.ds(i * 128, 128)
        return remote(
            part.at[2, rows],
            relay.at[rows],
            r_send.at[i],
            r_recv.at[i],
            at(1, z, 1 - yh, x, k),
        )

    def round_pass(i):
        rows = pl.ds(i * 128, 128)
        return remote(
            relay.at[rows],
            cin.at[0, rows],
            q_send.at[i],
            q_recv.at[i],
            at(3, z, 1 - yh, x, k),
        )

    def c_arrival(q):
        return remote(part.at[0], cin.at[q], c_send.at[0], c_recv.at[q], up)

    def product(y):
        @pl.when(y >= yl)
        def _():
            swap(y)
            for d in range(4):
                k_arrival(y, d).wait_recv()
            total = jnp.zeros((256, 512), F32)
            for j in range(8):
                total += jnp.dot(sig[y, j], gz[j], preferred_element_type=F32)

            if y == 3:
                for q in range(4):
                    row_mid[q * 64 : (q + 1) * 64, :] = (
                        step_size * total[192:256, q * 128 : (q + 1) * 128]
                    )

            @pl.when((y > yl) & ((y != 2) | (yl != 1)))
            def _():
                part[y - 1] = total.astype(BF)
                if y < 3:
                    c_copy(y).start()
                else:

                    @pl.when(yl != 0)
                    def _():
                        c_copy(y).start()

                    @pl.when(yl == 0)
                    def _():
                        for i in range(2):
                            round_copy(i).start()

            @pl.when((y == 2) & (yl == 1))
            def _():
                held[...] = total

            @pl.when(y == yl)
            def _():
                acc[...] = total

    def pass_both(y, flag):
        @pl.when(flag)
        def _():
            pass_on(y, 1)
            pass_on(y, 3)

    make(0)
    make(1)
    g_pass(1)
    pass_both(near(0), early(0))
    hand_on(0)
    g_pass(2)
    pass_both(near(1), early(1))
    hand_on(1)

    @pl.when(late)
    def _():
        spread(yl)

    g_pass(3)
    for way in range(2):
        g_arrival(way, 3, way).wait_recv()
    for y in (3, 2, 1, 0):

        @pl.when(y // 2 != yh)
        def _():
            collect(y)

        if y == 1:
            pass_both(yl, late)
        product(y)

    def n_copy(to):
        return remote(
            row_src.at[pl.ds(pl.multiple_of(to * 8, 8), 8)],
            row_in.at[yl],
            n_send.at[to],
            n_recv.at[yl],
            (to, c),
        )

    @pl.when(z == 7)
    def _():
        @pl.when(yl == 3)
        def _():
            for q in range(4):
                row_mid[q * 64 : (q + 1) * 64, :] += x_ref[
                    192:256, q * 128 : (q + 1) * 128
                ].astype(F32)

        for q in range(4):
            for i in range(2):
                row_src[pl.ds(i * 4 + q, 32, stride=8), :] = row_mid[
                    pl.ds(q * 64 + i, 32, stride=2), :
                ]

        @pl.loop(0, 32)
        def _(to):
            @pl.when(to != r)
            def _():
                n_copy(to).start()

        row_in[yl] = row_src[pl.ds(pl.multiple_of(r * 8, 8), 8), :]

    @pl.when(yl == 1)
    def _():
        for i in range(2):
            round_copy(i).wait_recv()
            round_pass(i).start()
        c_arrival(1).wait_recv()
        part[1] = (held[...] + cin[1].astype(F32)).astype(BF)
        c_copy(2).start()

    for q in range(3):

        @pl.when(adds(q))
        def _():
            c_arrival(q).wait_recv()
            acc[...] += cin[q].astype(F32)

    @pl.when(yl == 3)
    def _():
        for i in range(2):
            rows = slice(i * 128, (i + 1) * 128)
            round_pass(i).wait_recv()
            acc[rows, :] += cin[0, rows, :].astype(F32)

    out_ref[...] = (step_size * acc[...]).astype(BF)

    for q in range(4):

        @pl.when((z != 7) | (yl != q))
        def _():
            remote(
                row_src.at[pl.ds(0, 8)], row_in.at[q], n_send.at[0], n_recv.at[q], up
            ).wait_recv()

    new_ref[...] = (row_in[0] + row_in[1]) + (row_in[2] + row_in[3])

    @pl.when(z == 7)
    def _():
        @pl.loop(0, 32)
        def _(to):
            @pl.when(to != r)
            def _():
                n_copy(to).wait_send()

    for h in range(2):

        @pl.when(gives_piece & jnp.logical_not(piece_self(h)))
        def _():
            piece_copy(h).wait_send()

    for h in range(2):

        @pl.when(gives_mirror & jnp.logical_not(mirror_self(h)))
        def _():
            mirror_copy(h).wait_send()

    for step in range(4):
        for way in range(2):
            for rows in range(2):
                if step < 3 or rows == way:
                    g_copy(way, step, rows).wait_send()
    for i in range(2):

        @pl.when(near(i) >= yl)
        def _():
            y_copy(near(i)).wait_send()

    for y in range(4):

        @pl.when(y >= yl)
        def _():
            for d in (1, 3):
                x_copy(y, d).wait_send()

                @pl.when(y // 2 == yh)
                def _():
                    h_copy(y, d).wait_send()

            @pl.when(y // 2 != yh)
            def _():
                two_copy(y).wait_send()

            for d in range(4):
                k_copy(y, d).wait_send()

        if y > 0:

            @pl.when((y > yl) & ((y != 3) | (yl != 0)))
            def _():
                c_copy(y).wait_send()

    for i in range(2):

        @pl.when(yl == 0)
        def _():
            round_copy(i).wait_send()

        @pl.when(yl == 1)
        def _():
            round_pass(i).wait_send()


def shards(green, coupling):
    rows, cols, width = green.shape
    orbit = coupling.shape[0]
    high, wide = rows * orbit, cols * orbit
    vmem = pl.BlockSpec(memory_space=pltpu.VMEM)
    dma = pltpu.SemaphoreType.DMA
    collision, fresh = pl.pallas_call(
        kernel,
        out_shape=(
            jax.ShapeDtypeStruct((high, wide), BF),
            jax.ShapeDtypeStruct((8, 128), F32),
        ),
        in_specs=[pl.BlockSpec(memory_space=pl.ANY)] * 2,
        out_specs=(vmem, vmem),
        scratch_shapes=[
            pltpu.VMEM((rows, cols, width), BF),
            pltpu.VMEM((1, orbit), F32),
            pltpu.VMEM((high, wide), BF),
            dma((2,)),
            pltpu.VMEM((8, high, wide), BF),
            pltpu.VMEM((2, high, high), BF),
            pltpu.VMEM((2, high, high), BF),
            pltpu.VMEM((4, 8, high, high), BF),
            pltpu.VMEM((3, high, wide), BF),
            pltpu.VMEM((3, high, wide), BF),
            pltpu.VMEM((high, wide), BF),
            pltpu.VMEM((high, wide), F32),
            pltpu.VMEM((high, wide), F32),
            pltpu.VMEM((256, 128), F32),
            pltpu.VMEM((256, 128), F32),
            pltpu.VMEM((4, 8, 128), F32),
            dma((2, 4, 2)),
            dma((2, 4, 2)),
            dma((2,)),
            dma((2,)),
            dma((2,)),
            dma((2,)),
            dma((4,)),
            dma((4,)),
            dma((4, 2)),
            dma((4, 2)),
            dma((4, 2)),
            dma((4, 2)),
            dma((4, 4)),
            dma((4, 4)),
            dma((3,)),
            dma((3,)),
            dma((2,)),
            dma((2,)),
            dma((2,)),
            dma((2,)),
            dma((32,)),
            dma((4,)),
        ],
        compiler_params=pltpu.CompilerParams(
            collective_id=0, has_side_effects=True, vmem_limit_bytes=40 << 20
        ),
        cost_estimate=pl.CostEstimate(
            flops=2 * high * wide * 8192, bytes_accessed=4 * high * wide, transcendentals=0
        ),
        name="collide",
    )(green, coupling.reshape(1, orbit))
    collision = collision.reshape(rows, orbit, cols, orbit).transpose(0, 2, 1, 3)
    collision = collision.reshape(rows, cols, width)
    fresh = fresh.reshape(2, 4, 2, orbit).transpose(1, 2, 0, 3).reshape(cols, 128)
    return (collision, fresh.astype(BF))


def solution(mesh):
    placed = (P("row", "col", None), P())
    return jax.shard_map(
        shards,
        mesh=mesh,
        in_specs=placed,
        out_specs=(P("row", "col", None), P("col", "row")),
        check_vma=False,
    )
```

```python
import jax
import jax.numpy as jnp
from jax import lax
from jax.experimental import pallas as pl
from jax.experimental.pallas import tpu as pltpu
from jax.sharding import PartitionSpec as P

step_size = 0.01
MESH = pl.DeviceIdType.MESH
BF = jnp.bfloat16
F32 = jnp.float32


def kernel(
    green_ref,
    strength_ref,
    out_ref,
    new_ref,
    raw,
    coupling_ref,
    x_ref,
    in_sem,
    gz,
    mir,
    own,
    sig,
    part,
    cin,
    relay,
    acc,
    held,
    row_mid,
    row_src,
    row_in,
    g_send,
    g_recv,
    m_send,
    m_recv,
    s_send,
    s_recv,
    y_send,
    y_recv,
    x_send,
    x_recv,
    h_send,
    h_recv,
    k_send,
    k_recv,
    c_send,
    c_recv,
    r_send,
    r_recv,
    q_send,
    q_recv,
    n_send,
    n_recv,
):
    r = lax.axis_index("row")
    c = lax.axis_index("col")
    yl, z = r // 8, r % 8
    yh, x, k = c // 8, (c // 2) % 4, c % 2
    goal = c // 4

    def part_of(x_):
        m = jnp.where((x_ == 1) | (x_ == 2), 2, 0) + x_ // 2
        return 2 * jnp.where(yl % 2 == 0, m, 3 - m) + k

    def place_of(j):
        m = jnp.where(yl % 2 == 0, j // 2, 3 - j // 2)
        return jnp.where(m == 1, 3, (m + 1) // 2)

    part_at = part_of(x)
    m_at = part_at // 2

    def at(yl_, z_, yh_, x_, k_):
        return (yl_ * 8 + z_, yh_ * 8 + x_ * 2 + k_)

    def remote(src, dst, send, recv, device):
        return pltpu.make_async_remote_copy(
            src, dst, send, recv, device_id=device, device_id_type=MESH
        )

    up, down = at(yl, (z + 1) % 8, yh, x, k), at(yl, (z + 7) % 8, yh, x, k)
    other = at(yl, z, yh, x, 1 - k)
    across = at(yl, z, 1 - yh, x, k)

    gives_mirror = goal >= yl

    def mirror_to(h):
        return at(yl, (x % 2) * 4 + k * 2 + h, yh, place_of(z), z % 2)

    def mirror_self(h):
        return (z == part_at) & (z == (x % 2) * 4 + k * 2 + h)

    def mirror_from(s):
        return at(yl, part_at, yh, s * 2 + z // 4, (z // 2) % 2)

    def mirror_from_self(s):
        return (z == part_at) & (x == s * 2 + z // 4) & (k == (z // 2) % 2)

    gives_piece = yl >= goal

    def piece_to(h):
        return at(goal, z, yl // 2, (x + 4 + k * (2 * (x % 2) - 1)) % 4, h)

    def piece_self(h):
        return (goal == yl) & (k == 0) if h == 0 else False

    def piece_from(s):
        return at(2 * yh + s, z, yl // 2, (yl % 2) * 2 + m_at // 2, m_at % 2)

    def piece_from_self(s):
        mine = (2 * yh + s == yl) & (x == (yl % 2) * 2 + m_at // 2) & (k == m_at % 2)
        return mine & (yl // 2 == yh)

    def adds(q):
        return (q < yl) & ((yl == 1) | (q != 0))

    def one(flag):
        return jnp.where(flag, 1, 0)

    barrier = pltpu.get_barrier_semaphore()
    loads = [
        pltpu.make_async_copy(green_ref, raw, in_sem.at[0]),
        pltpu.make_async_copy(strength_ref, coupling_ref, in_sem.at[1]),
    ]
    for load in loads:
        load.start()

    def greet(device):
        pl.semaphore_signal(barrier, inc=1, device_id=device, device_id_type=MESH)

    greet(up)
    greet(down)
    greet(other)
    for d in (1, 2, 3):
        greet(at(yl, z, yh, (x + d) % 4, k))
    for s in range(2):

        @pl.when((2 * yh + s >= yl) & jnp.logical_not(mirror_from_self(s)))
        def _():
            greet(mirror_from(s))

        @pl.when((2 * yh + s >= yl) & jnp.logical_not(piece_from_self(s)))
        def _():
            greet(piece_from(s))

    @pl.when(3 - 2 * yh >= yl)
    def _():
        greet(across)

    for q in range(3):

        @pl.when(adds(q))
        def _():
            greet(at(q, z, yh, x, k))

    @pl.when(yl == 1)
    def _():
        greet(at(0, z, 1 - yh, x, k))

    @pl.when(yl == 3)
    def _():
        greet(at(1, z, 1 - yh, x, k))

    for q in range(4):

        @pl.when((z != 7) | (yl != q))
        def _():
            greet(at(q, 7, yh, x, k))

    for load in loads:
        load.wait()
    for t in range(4):
        block = raw[t].reshape(8, 64, 64).swapaxes(0, 1).reshape(64, 512)
        x_ref[t * 64 : (t + 1) * 64, :] = block

    peers = 6 + jnp.minimum(3 - yl, 2) + one(yl == 1) + jnp.where(z == 7, 31, 0)
    peers += one(2 * yh + 1 >= yl)
    for h in range(2):
        peers += one(gives_mirror & jnp.logical_not(mirror_self(h)))
        peers += one(gives_piece & jnp.logical_not(piece_self(h)))
    pl.semaphore_wait(barrier, peers)

    def half_of(h):
        return x_ref.at[:, pl.ds(h * 256, 256)]

    def piece_copy(h):
        return remote(
            half_of(h), own.at[yl % 2], s_send.at[h], s_recv.at[yl % 2], piece_to(h)
        )

    def piece_arrival(s):
        return remote(half_of(0), own.at[s], s_send.at[0], s_recv.at[s], up)

    def g_copy(way, step, rows):
        held = (z - step + 8) % 8 if way == 0 else (z + step) % 8
        src = x_ref if step == 0 else gz.at[held]
        return remote(
            src.at[pl.ds(rows * 128, 128)],
            gz.at[held, pl.ds(rows * 128, 128)],
            g_send.at[way, step, rows],
            g_recv.at[way, step, rows],
            up if way == 0 else down,
        )

    def g_arrival(way, step, rows):
        held = (z - step + 7) % 8 if way == 0 else (z + step + 1) % 8
        return remote(
            x_ref.at[pl.ds(0, 128)],
            gz.at[held, pl.ds(rows * 128, 128)],
            g_send.at[way, step, rows],
            g_recv.at[way, step, rows],
            up,
        )

    def g_pass(step):
        for rows in range(2):
            for way in range(2):
                g_arrival(way, step - 1, rows).wait_recv()
                if step < 3 or rows == way:
                    g_copy(way, step, rows).start()

    def mirror_copy(h):
        return remote(
            half_of(h), mir.at[x // 2], m_send.at[h], m_recv.at[x // 2], mirror_to(h)
        )

    def mirror_arrival(s):
        return remote(half_of(0), mir.at[s], m_send.at[0], m_recv.at[s], up)

    for h in range(2):

        @pl.when(gives_mirror & jnp.logical_not(mirror_self(h)))
        def _():
            mirror_copy(h).start()

        @pl.when(gives_mirror & mirror_self(h))
        def _():
            mir[x // 2] = x_ref[:, h * 256 : (h + 1) * 256]

    for rows in range(2):
        for way in range(2):
            g_copy(way, 0, rows).start()
    for h in range(2):

        @pl.when(gives_piece & jnp.logical_not(piece_self(h)))
        def _():
            piece_copy(h).start()

        @pl.when(gives_piece & piece_self(h))
        def _():
            own[yl % 2] = x_ref[:, h * 256 : (h + 1) * 256]

    gz[z] = x_ref[...]

    def y_copy(y):
        return remote(
            sig.at[y, part_at], sig.at[y, part_at], y_send.at[y], y_recv.at[y], across
        )

    def x_copy(y, d):
        return remote(
            sig.at[y, part_at],
            sig.at[y, part_at],
            x_send.at[y, d // 2],
            x_recv.at[y, d // 2],
            at(yl, z, yh, (x + d) % 4, k),
        )

    def two_copy(y):
        return remote(
            sig.at[y, part_at],
            sig.at[y, part_at],
            h_send.at[y, 0],
            h_recv.at[y, 0],
            at(yl, z, yh, (x + 2) % 4, k),
        )

    def two_arrival(y):
        j = behind(2)
        return remote(
            sig.at[y, j], sig.at[y, j], h_send.at[y, 0], h_recv.at[y, 0], up
        )

    def behind(d):
        return part_of((x + 4 - d) % 4)

    def x_arrival(y, d):
        j = behind(d)
        return remote(
            sig.at[y, j], sig.at[y, j], x_send.at[y, 0], x_recv.at[y, d // 2], up
        )

    def h_copy(y, d):
        rows = pl.ds((d // 2) * 128, 128)
        block = sig.at[y, behind(d), rows]
        return remote(
            block,
            block,
            h_send.at[y, d // 2],
            h_recv.at[y, d // 2],
            at(yl, z, yh, (x + d) % 4, k),
        )

    def h_arrival(y, d):
        block = sig.at[y, behind(2), pl.ds((d // 2) * 128, 128)]
        return remote(block, block, h_send.at[y, 0], h_recv.at[y, d // 2], up)

    def k_copy(y, d):
        block = sig.at[y, behind(d)]
        return remote(block, block, k_send.at[y, d], k_recv.at[y, d], other)

    def k_arrival(y, d):
        block = sig.at[y, behind(d) + 1 - 2 * k]
        return remote(block, block, k_send.at[y, d], k_recv.at[y, d], other)

    def spread(y):
        for d in (1, 3):
            x_copy(y, d).start()
        k_copy(y, 0).start()

    def pass_on(y, d):
        @pl.when(y >= yl)
        def _():
            x_arrival(y, d).wait_recv()
            h_copy(y, d).start()
            k_copy(y, d).start()

    def near(i):
        return 2 * yh + 1 - i

    def far(i):
        return 3 - 2 * yh - i

    late = (yh == 0) & (yl < 2)

    def early(i):
        return jnp.logical_not(late & (near(i) == yl))

    strength = coupling_ref[...]
    square = jnp.broadcast_to(strength, (64, 64))
    diagonal = lax.broadcasted_iota(jnp.int32, (64, 64), 0) == lax.broadcasted_iota(
        jnp.int32, (64, 64), 1
    )
    column = jnp.sum(jnp.where(diagonal, square, 0.0), axis=1, keepdims=True)
    pair = column * jnp.concatenate([strength] * 4, axis=1)

    def make(i):
        i_near = i
        s = 1 - i
        y = near(i)

        @pl.when(y >= yl)
        def _():
            @pl.when(jnp.logical_not(mirror_from_self(s)))
            def _():
                mirror_arrival(s).wait_recv()

            @pl.when(jnp.logical_not(piece_from_self(s)))
            def _():
                piece_arrival(s).wait_recv()

            partner = mir[s].T
            later = lax.broadcasted_iota(jnp.int32, (64, 256), 1) // 64
            first = 32 * (y - yl) + 4 * z - 4 * part_at
            for i in range(4):
                rows = slice(i * 64, (i + 1) * 64)
                g = own[s, rows, :].astype(F32)
                value = pair * (g * g) * partner[rows].astype(F32)
                keep = later <= first + i
                sig[y, part_at, rows, :] = jnp.where(keep, value, 0.0).astype(BF)
            y_copy(y).start()

            @pl.when(early(i_near))
            def _():
                spread(y)

    def hand_on(i):
        y = far(i)

        @pl.when(y >= yl)
        def _():
            y_copy(y).wait_recv()
            spread(y)
            two_copy(y).start()

    def swap(y):
        @pl.when((y >= yl) & (y // 2 == yh))
        def _():
            for d in (1, 3):
                h_arrival(y, d).wait_recv()
            k_copy(y, 2).start()

    def collect(y):
        @pl.when(y >= yl)
        def _():
            for d in (1, 3):
                x_arrival(y, d).wait_recv()
                k_copy(y, d).start()
            two_arrival(y).wait_recv()
            k_copy(y, 2).start()

    def c_copy(y):
        to, slot = y, yl
        if y == 2:
            to, slot = jnp.where(yl == 0, 1, 2), 1
        return remote(
            part.at[y - 1],
            cin.at[slot],
            c_send.at[y - 1],
            c_recv.at[slot],
            at(to, z, yh, x, k),
        )

    def round_copy(i):
        rows = pl.ds(i * 128, 128)
        return remote(
            part.at[2, rows],
            relay.at[rows],
            r_send.at[i],
            r_recv.at[i],
            at(1, z, 1 - yh, x, k),
        )

    def round_pass(i):
        rows = pl.ds(i * 128, 128)
        return remote(
            relay.at[rows],
            cin.at[0, rows],
            q_send.at[i],
            q_recv.at[i],
            at(3, z, 1 - yh, x, k),
        )

    def c_arrival(q):
        return remote(part.at[0], cin.at[q], c_send.at[0], c_recv.at[q], up)

    def product(y):
        @pl.when(y >= yl)
        def _():
            @pl.when(late & (y == yl))
            def _():
                swap(y)

            for d in range(4):
                k_arrival(y, d).wait_recv()
            total = jnp.zeros((256, 512), F32)
            for j in range(8):
                total += jnp.dot(sig[y, j], gz[j], preferred_element_type=F32)

            if y == 3:
                for q in range(4):
                    row_mid[q * 64 : (q + 1) * 64, :] = (
                        step_size * total[192:256, q * 128 : (q + 1) * 128]
                    )

            @pl.when((y > yl) & ((y != 2) | (yl != 1)))
            def _():
                part[y - 1] = total.astype(BF)
                if y < 3:
                    c_copy(y).start()
                else:

                    @pl.when(yl != 0)
                    def _():
                        c_copy(y).start()

                    @pl.when(yl == 0)
                    def _():
                        for i in range(2):
                            round_copy(i).start()

            @pl.when((y == 2) & (yl == 1))
            def _():
                held[...] = total

            @pl.when(y == yl)
            def _():
                acc[...] = total

    def pass_both(y, flag):
        @pl.when(flag)
        def _():
            pass_on(y, 1)
            pass_on(y, 3)

    make(0)
    make(1)
    g_pass(1)
    pass_both(near(0), early(0))
    hand_on(0)
    g_pass(2)
    pass_both(near(1), early(1))
    hand_on(1)

    @pl.when(late)
    def _():
        spread(yl)

    g_pass(3)
    for i in range(2):

        @pl.when(early(i))
        def _():
            swap(near(i))

    collect(far(0))
    for way in range(2):
        g_arrival(way, 3, way).wait_recv()
    for y in (3, 2, 1, 0):

        @pl.when(far(1) == y)
        def _():
            collect(y)

        if y == 1:
            pass_both(yl, late)
        product(y)

    def n_copy(to):
        return remote(
            row_src.at[pl.ds(pl.multiple_of(to * 8, 8), 8)],
            row_in.at[yl],
            n_send.at[to],
            n_recv.at[yl],
            (to, c),
        )

    @pl.when(z == 7)
    def _():
        @pl.when(yl == 3)
        def _():
            for q in range(4):
                row_mid[q * 64 : (q + 1) * 64, :] += x_ref[
                    192:256, q * 128 : (q + 1) * 128
                ].astype(F32)

        for q in range(4):
            for i in range(2):
                row_src[pl.ds(i * 4 + q, 32, stride=8), :] = row_mid[
                    pl.ds(q * 64 + i, 32, stride=2), :
                ]

        @pl.loop(0, 32)
        def _(to):
            @pl.when(to != r)
            def _():
                n_copy(to).start()

        row_in[yl] = row_src[pl.ds(pl.multiple_of(r * 8, 8), 8), :]

    @pl.when(yl == 1)
    def _():
        for i in range(2):
            round_copy(i).wait_recv()
            round_pass(i).start()
        c_arrival(1).wait_recv()
        part[1] = (held[...] + cin[1].astype(F32)).astype(BF)
        c_copy(2).start()

    for q in range(3):

        @pl.when(adds(q))
        def _():
            c_arrival(q).wait_recv()
            acc[...] += cin[q].astype(F32)

    @pl.when(yl == 3)
    def _():
        for i in range(2):
            rows = slice(i * 128, (i + 1) * 128)
            round_pass(i).wait_recv()
            acc[rows, :] += cin[0, rows, :].astype(F32)

    out_ref[...] = (step_size * acc[...]).astype(BF)

    for q in range(4):

        @pl.when((z != 7) | (yl != q))
        def _():
            remote(
                row_src.at[pl.ds(0, 8)], row_in.at[q], n_send.at[0], n_recv.at[q], up
            ).wait_recv()

    new_ref[...] = (row_in[0] + row_in[1]) + (row_in[2] + row_in[3])

    @pl.when(z == 7)
    def _():
        @pl.loop(0, 32)
        def _(to):
            @pl.when(to != r)
            def _():
                n_copy(to).wait_send()

    for h in range(2):

        @pl.when(gives_piece & jnp.logical_not(piece_self(h)))
        def _():
            piece_copy(h).wait_send()

    for h in range(2):

        @pl.when(gives_mirror & jnp.logical_not(mirror_self(h)))
        def _():
            mirror_copy(h).wait_send()

    for step in range(4):
        for way in range(2):
            for rows in range(2):
                if step < 3 or rows == way:
                    g_copy(way, step, rows).wait_send()
    for i in range(2):

        @pl.when(near(i) >= yl)
        def _():
            y_copy(near(i)).wait_send()

    for y in range(4):

        @pl.when(y >= yl)
        def _():
            for d in (1, 3):
                x_copy(y, d).wait_send()

                @pl.when(y // 2 == yh)
                def _():
                    h_copy(y, d).wait_send()

            @pl.when(y // 2 != yh)
            def _():
                two_copy(y).wait_send()

            for d in range(4):
                k_copy(y, d).wait_send()

        if y > 0:

            @pl.when((y > yl) & ((y != 3) | (yl != 0)))
            def _():
                c_copy(y).wait_send()

    for i in range(2):

        @pl.when(yl == 0)
        def _():
            round_copy(i).wait_send()

        @pl.when(yl == 1)
        def _():
            round_pass(i).wait_send()


def shards(green, coupling):
    rows, cols, width = green.shape
    orbit = coupling.shape[0]
    high, wide = rows * orbit, cols * orbit
    vmem = pl.BlockSpec(memory_space=pltpu.VMEM)
    dma = pltpu.SemaphoreType.DMA
    collision, fresh = pl.pallas_call(
        kernel,
        out_shape=(
            jax.ShapeDtypeStruct((high, wide), BF),
            jax.ShapeDtypeStruct((8, 128), F32),
        ),
        in_specs=[pl.BlockSpec(memory_space=pl.ANY)] * 2,
        out_specs=(vmem, vmem),
        scratch_shapes=[
            pltpu.VMEM((rows, cols, width), BF),
            pltpu.VMEM((1, orbit), F32),
            pltpu.VMEM((high, wide), BF),
            dma((2,)),
            pltpu.VMEM((8, high, wide), BF),
            pltpu.VMEM((2, high, high), BF),
            pltpu.VMEM((2, high, high), BF),
            pltpu.VMEM((4, 8, high, high), BF),
            pltpu.VMEM((3, high, wide), BF),
            pltpu.VMEM((3, high, wide), BF),
            pltpu.VMEM((high, wide), BF),
            pltpu.VMEM((high, wide), F32),
            pltpu.VMEM((high, wide), F32),
            pltpu.VMEM((256, 128), F32),
            pltpu.VMEM((256, 128), F32),
            pltpu.VMEM((4, 8, 128), F32),
            dma((2, 4, 2)),
            dma((2, 4, 2)),
            dma((2,)),
            dma((2,)),
            dma((2,)),
            dma((2,)),
            dma((4,)),
            dma((4,)),
            dma((4, 2)),
            dma((4, 2)),
            dma((4, 2)),
            dma((4, 2)),
            dma((4, 4)),
            dma((4, 4)),
            dma((3,)),
            dma((3,)),
            dma((2,)),
            dma((2,)),
            dma((2,)),
            dma((2,)),
            dma((32,)),
            dma((4,)),
        ],
        compiler_params=pltpu.CompilerParams(
            collective_id=0, has_side_effects=True, vmem_limit_bytes=56 << 20
        ),
        cost_estimate=pl.CostEstimate(
            flops=2 * high * wide * 8192, bytes_accessed=4 * high * wide, transcendentals=0
        ),
        name="collide",
    )(green, coupling.reshape(1, orbit))
    collision = collision.reshape(rows, orbit, cols, orbit).transpose(0, 2, 1, 3)
    collision = collision.reshape(rows, cols, width)
    fresh = fresh.reshape(2, 4, 2, orbit).transpose(1, 2, 0, 3).reshape(cols, 128)
    return (collision, fresh.astype(BF))


def solution(mesh):
    placed = (P("row", "col", None), P())
    return jax.shard_map(
        shards,
        mesh=mesh,
        in_specs=placed,
        out_specs=(P("row", "col", None), P("col", "row")),
        check_vma=False,
    )
```

```python
import jax
import jax.numpy as jnp
from jax import lax
from jax.experimental import pallas as pl
from jax.experimental.pallas import tpu as pltpu
from jax.sharding import PartitionSpec as P

step_size = 0.01
MESH = pl.DeviceIdType.MESH
BF = jnp.bfloat16
F32 = jnp.float32


def kernel(
    green_ref,
    strength_ref,
    out_ref,
    new_ref,
    raw,
    coupling_ref,
    x_ref,
    in_sem,
    gz,
    mir,
    own,
    sig,
    part,
    cin,
    relay,
    acc,
    held,
    row_mid,
    row_src,
    row_in,
    g_send,
    g_recv,
    m_send,
    m_recv,
    s_send,
    s_recv,
    y_send,
    y_recv,
    x_send,
    x_recv,
    h_send,
    h_recv,
    k_send,
    k_recv,
    c_send,
    c_recv,
    e_send,
    e_recv,
    r_send,
    r_recv,
    q_send,
    q_recv,
    n_send,
    n_recv,
):
    r = lax.axis_index("row")
    c = lax.axis_index("col")
    yl, z = r // 8, r % 8
    yh, x, k = c // 8, (c // 2) % 4, c % 2
    goal = c // 4

    def part_of(x_):
        m = jnp.where((x_ == 1) | (x_ == 2), 2, 0) + x_ // 2
        return 2 * jnp.where(yl % 2 == 0, m, 3 - m) + k

    def place_of(j):
        m = jnp.where(yl % 2 == 0, j // 2, 3 - j // 2)
        return jnp.where(m == 1, 3, (m + 1) // 2)

    part_at = part_of(x)
    m_at = part_at // 2

    def at(yl_, z_, yh_, x_, k_):
        return (yl_ * 8 + z_, yh_ * 8 + x_ * 2 + k_)

    def remote(src, dst, send, recv, device):
        return pltpu.make_async_remote_copy(
            src, dst, send, recv, device_id=device, device_id_type=MESH
        )

    up, down = at(yl, (z + 1) % 8, yh, x, k), at(yl, (z + 7) % 8, yh, x, k)
    other = at(yl, z, yh, x, 1 - k)
    across = at(yl, z, 1 - yh, x, k)

    gives_mirror = goal >= yl

    def mirror_to(h):
        return at(yl, (x % 2) * 4 + k * 2 + h, yh, place_of(z), z % 2)

    def mirror_self(h):
        return (z == part_at) & (z == (x % 2) * 4 + k * 2 + h)

    def mirror_from(s):
        return at(yl, part_at, yh, s * 2 + z // 4, (z // 2) % 2)

    def mirror_from_self(s):
        return (z == part_at) & (x == s * 2 + z // 4) & (k == (z // 2) % 2)

    gives_piece = yl >= goal

    def piece_to(h):
        return at(goal, z, yl // 2, (x + 4 + k * (2 * (x % 2) - 1)) % 4, h)

    def piece_self(h):
        return (goal == yl) & (k == 0) if h == 0 else False

    def piece_from(s):
        return at(2 * yh + s, z, yl // 2, (yl % 2) * 2 + m_at // 2, m_at % 2)

    def piece_from_self(s):
        mine = (2 * yh + s == yl) & (x == (yl % 2) * 2 + m_at // 2) & (k == m_at % 2)
        return mine & (yl // 2 == yh)

    def adds(q):
        return (q < yl) & ((yl == 1) | (q != 0))

    def one(flag):
        return jnp.where(flag, 1, 0)

    barrier = pltpu.get_barrier_semaphore()
    loads = [
        pltpu.make_async_copy(green_ref, raw, in_sem.at[0]),
        pltpu.make_async_copy(strength_ref, coupling_ref, in_sem.at[1]),
    ]
    for load in loads:
        load.start()

    def greet(device):
        pl.semaphore_signal(barrier, inc=1, device_id=device, device_id_type=MESH)

    greet(up)
    greet(down)
    greet(other)
    for d in (1, 2, 3):
        greet(at(yl, z, yh, (x + d) % 4, k))
    for s in range(2):

        @pl.when((2 * yh + s >= yl) & jnp.logical_not(mirror_from_self(s)))
        def _():
            greet(mirror_from(s))

        @pl.when((2 * yh + s >= yl) & jnp.logical_not(piece_from_self(s)))
        def _():
            greet(piece_from(s))

    @pl.when(3 - 2 * yh >= yl)
    def _():
        greet(across)

    for q in range(3):

        @pl.when(adds(q))
        def _():
            greet(at(q, z, yh, x, k))

    @pl.when(yl == 1)
    def _():
        greet(at(0, z, 1 - yh, x, k))

    @pl.when(yl == 3)
    def _():
        greet(at(1, z, 1 - yh, x, k))

    for q in range(4):

        @pl.when((z != 7) | (yl != q))
        def _():
            greet(at(q, 7, yh, x, k))

    for load in loads:
        load.wait()
    for t in range(4):
        block = raw[t].reshape(8, 64, 64).swapaxes(0, 1).reshape(64, 512)
        x_ref[t * 64 : (t + 1) * 64, :] = block

    peers = 6 + jnp.minimum(3 - yl, 2) + one(yl == 1) + jnp.where(z == 7, 31, 0)
    peers += one(2 * yh + 1 >= yl)
    for h in range(2):
        peers += one(gives_mirror & jnp.logical_not(mirror_self(h)))
        peers += one(gives_piece & jnp.logical_not(piece_self(h)))
    pl.semaphore_wait(barrier, peers)

    def half_of(h):
        return x_ref.at[:, pl.ds(h * 256, 256)]

    def piece_copy(h):
        return remote(
            half_of(h), own.at[yl % 2], s_send.at[h], s_recv.at[yl % 2], piece_to(h)
        )

    def piece_arrival(s):
        return remote(half_of(0), own.at[s], s_send.at[0], s_recv.at[s], up)

    def g_copy(way, step, rows):
        held = (z - step + 8) % 8 if way == 0 else (z + step) % 8
        src = x_ref if step == 0 else gz.at[held]
        return remote(
            src.at[pl.ds(rows * 128, 128)],
            gz.at[held, pl.ds(rows * 128, 128)],
            g_send.at[way, step, rows],
            g_recv.at[way, step, rows],
            up if way == 0 else down,
        )

    def g_arrival(way, step, rows):
        held = (z - step + 7) % 8 if way == 0 else (z + step + 1) % 8
        return remote(
            x_ref.at[pl.ds(0, 128)],
            gz.at[held, pl.ds(rows * 128, 128)],
            g_send.at[way, step, rows],
            g_recv.at[way, step, rows],
            up,
        )

    def g_pass(step):
        for rows in range(2):
            for way in range(2):
                g_arrival(way, step - 1, rows).wait_recv()
                if step < 3 or rows == way:
                    g_copy(way, step, rows).start()

    def mirror_copy(h):
        return remote(
            half_of(h), mir.at[x // 2], m_send.at[h], m_recv.at[x // 2], mirror_to(h)
        )

    def mirror_arrival(s):
        return remote(half_of(0), mir.at[s], m_send.at[0], m_recv.at[s], up)

    for h in range(2):

        @pl.when(gives_mirror & jnp.logical_not(mirror_self(h)))
        def _():
            mirror_copy(h).start()

        @pl.when(gives_mirror & mirror_self(h))
        def _():
            mir[x // 2] = x_ref[:, h * 256 : (h + 1) * 256]

    for rows in range(2):
        for way in range(2):
            g_copy(way, 0, rows).start()
    for h in range(2):

        @pl.when(gives_piece & jnp.logical_not(piece_self(h)))
        def _():
            piece_copy(h).start()

        @pl.when(gives_piece & piece_self(h))
        def _():
            own[yl % 2] = x_ref[:, h * 256 : (h + 1) * 256]

    gz[z] = x_ref[...]

    def y_copy(y):
        return remote(
            sig.at[y, part_at], sig.at[y, part_at], y_send.at[y], y_recv.at[y], across
        )

    def x_copy(y, d):
        return remote(
            sig.at[y, part_at],
            sig.at[y, part_at],
            x_send.at[y, d // 2],
            x_recv.at[y, d // 2],
            at(yl, z, yh, (x + d) % 4, k),
        )

    def two_copy(y):
        return remote(
            sig.at[y, part_at],
            sig.at[y, part_at],
            h_send.at[y, 0],
            h_recv.at[y, 0],
            at(yl, z, yh, (x + 2) % 4, k),
        )

    def two_arrival(y):
        j = behind(2)
        return remote(
            sig.at[y, j], sig.at[y, j], h_send.at[y, 0], h_recv.at[y, 0], up
        )

    def behind(d):
        return part_of((x + 4 - d) % 4)

    def x_arrival(y, d):
        j = behind(d)
        return remote(
            sig.at[y, j], sig.at[y, j], x_send.at[y, 0], x_recv.at[y, d // 2], up
        )

    def h_copy(y, d):
        rows = pl.ds((d // 2) * 128, 128)
        block = sig.at[y, behind(d), rows]
        return remote(
            block,
            block,
            h_send.at[y, d // 2],
            h_recv.at[y, d // 2],
            at(yl, z, yh, (x + d) % 4, k),
        )

    def h_arrival(y, d):
        block = sig.at[y, behind(2), pl.ds((d // 2) * 128, 128)]
        return remote(block, block, h_send.at[y, 0], h_recv.at[y, d // 2], up)

    def k_copy(y, d):
        block = sig.at[y, behind(d)]
        return remote(block, block, k_send.at[y, d], k_recv.at[y, d], other)

    def k_arrival(y, d):
        block = sig.at[y, behind(d) + 1 - 2 * k]
        return remote(block, block, k_send.at[y, d], k_recv.at[y, d], other)

    def spread(y):
        for d in (1, 3):
            x_copy(y, d).start()
        k_copy(y, 0).start()

    def pass_on(y, d):
        @pl.when(y >= yl)
        def _():
            x_arrival(y, d).wait_recv()
            h_copy(y, d).start()
            k_copy(y, d).start()

    def near(i):
        return 2 * yh + 1 - i

    def far(i):
        return 3 - 2 * yh - i

    late = (yh == 0) & (yl < 2)

    def early(i):
        return jnp.logical_not(late & (near(i) == yl))

    strength = coupling_ref[...]
    square = jnp.broadcast_to(strength, (64, 64))
    diagonal = lax.broadcasted_iota(jnp.int32, (64, 64), 0) == lax.broadcasted_iota(
        jnp.int32, (64, 64), 1
    )
    column = jnp.sum(jnp.where(diagonal, square, 0.0), axis=1, keepdims=True)
    pair = column * jnp.concatenate([strength] * 4, axis=1)

    def make(i):
        i_near = i
        s = 1 - i
        y = near(i)

        @pl.when(y >= yl)
        def _():
            @pl.when(jnp.logical_not(mirror_from_self(s)))
            def _():
                mirror_arrival(s).wait_recv()

            @pl.when(jnp.logical_not(piece_from_self(s)))
            def _():
                piece_arrival(s).wait_recv()

            partner = mir[s].T
            later = lax.broadcasted_iota(jnp.int32, (64, 256), 1) // 64
            first = 32 * (y - yl) + 4 * z - 4 * part_at
            for i in range(4):
                rows = slice(i * 64, (i + 1) * 64)
                g = own[s, rows, :].astype(F32)
                value = pair * (g * g) * partner[rows].astype(F32)
                keep = later <= first + i
                sig[y, part_at, rows, :] = jnp.where(keep, value, 0.0).astype(BF)
            y_copy(y).start()

            @pl.when(early(i_near))
            def _():
                spread(y)

    def hand_on(i):
        y = far(i)

        @pl.when(y >= yl)
        def _():
            y_copy(y).wait_recv()
            spread(y)
            two_copy(y).start()

    def swap(y):
        @pl.when((y >= yl) & (y // 2 == yh))
        def _():
            for d in (1, 3):
                h_arrival(y, d).wait_recv()
            k_copy(y, 2).start()

    def collect(y):
        @pl.when(y >= yl)
        def _():
            for d in (1, 3):
                x_arrival(y, d).wait_recv()
                k_copy(y, d).start()
            two_arrival(y).wait_recv()
            k_copy(y, 2).start()

    def c_copy(y):
        return remote(
            part.at[y - 1],
            cin.at[yl],
            c_send.at[y - 1],
            c_recv.at[yl],
            at(y, z, yh, x, k),
        )

    def half_copy(i):
        rows = pl.ds(i * 128, 128)
        return remote(
            part.at[1, rows],
            cin.at[1, rows],
            e_send.at[i],
            e_recv.at[i],
            at(jnp.minimum(yl + 1, 2), z, yh, x, k),
        )

    def round_copy(i):
        rows = pl.ds(i * 128, 128)
        return remote(
            part.at[2, rows],
            relay.at[rows],
            r_send.at[i],
            r_recv.at[i],
            at(1, z, 1 - yh, x, k),
        )

    def round_pass(i):
        rows = pl.ds(i * 128, 128)
        return remote(
            relay.at[rows],
            cin.at[0, rows],
            q_send.at[i],
            q_recv.at[i],
            at(3, z, 1 - yh, x, k),
        )

    def c_arrival(q):
        return remote(part.at[0], cin.at[q], c_send.at[0], c_recv.at[q], up)

    def product(y, flag=True):
        @pl.when((y >= yl) & flag)
        def _():
            @pl.when(late & (y == yl))
            def _():
                swap(y)

            for d in range(4):
                k_arrival(y, d).wait_recv()
            total = jnp.zeros((256, 512), F32)
            for j in range(8):
                total += jnp.dot(sig[y, j], gz[j], preferred_element_type=F32)

            if y == 3:
                for q in range(4):
                    row_mid[q * 64 : (q + 1) * 64, :] = (
                        step_size * total[192:256, q * 128 : (q + 1) * 128]
                    )

            @pl.when((y > yl) & ((y != 2) | (yl != 1)))
            def _():
                part[y - 1] = total.astype(BF)
                if y == 1:
                    c_copy(y).start()
                elif y == 2:
                    for i in range(2):
                        half_copy(i).start()
                else:

                    @pl.when(yl != 0)
                    def _():
                        c_copy(y).start()

                    @pl.when(yl == 0)
                    def _():
                        for i in range(2):
                            round_copy(i).start()

            @pl.when((y == 2) & (yl == 1))
            def _():
                held[...] = total

            @pl.when(y == yl)
            def _():
                acc[...] = total

    def pass_both(y, flag):
        @pl.when(flag)
        def _():
            pass_on(y, 1)
            pass_on(y, 3)

    make(0)
    make(1)
    g_pass(1)
    pass_both(near(0), early(0))
    hand_on(0)
    g_pass(2)
    pass_both(near(1), early(1))
    hand_on(1)

    @pl.when(late)
    def _():
        spread(yl)

    g_pass(3)
    for i in range(2):

        @pl.when(early(i))
        def _():
            swap(near(i))

    collect(far(0))
    for way in range(2):
        g_arrival(way, 3, way).wait_recv()
    first = (yh == 0) & (yl == 0)
    product(1, first)
    for y in (3, 2, 1, 0):

        @pl.when(far(1) == y)
        def _():
            collect(y)

        if y == 1:
            pass_both(yl, late)
        product(y, jnp.logical_not(first) if y == 1 else True)

    def n_copy(to):
        return remote(
            row_src.at[pl.ds(pl.multiple_of(to * 8, 8), 8)],
            row_in.at[yl],
            n_send.at[to],
            n_recv.at[yl],
            (to, c),
        )

    @pl.when(z == 7)
    def _():
        @pl.when(yl == 3)
        def _():
            for q in range(4):
                row_mid[q * 64 : (q + 1) * 64, :] += x_ref[
                    192:256, q * 128 : (q + 1) * 128
                ].astype(F32)

        for q in range(4):
            for i in range(2):
                row_src[pl.ds(i * 4 + q, 32, stride=8), :] = row_mid[
                    pl.ds(q * 64 + i, 32, stride=2), :
                ]

        @pl.loop(0, 32)
        def _(to):
            @pl.when(to != r)
            def _():
                n_copy(to).start()

        row_in[yl] = row_src[pl.ds(pl.multiple_of(r * 8, 8), 8), :]

    def finish(rows, *slots):
        total = acc[rows, :]
        for q in slots:
            total += cin[q, rows, :].astype(F32)
        out_ref[rows, :] = (step_size * total).astype(BF)

    halves = [slice(0, 128), slice(128, 256)]

    @pl.when(yl == 0)
    def _():
        for i in range(2):
            finish(halves[i])

    @pl.when(yl == 1)
    def _():
        for i in range(2):
            round_copy(i).wait_recv()
            round_pass(i).start()
        for i in range(2):
            rows = halves[i]
            half_copy(i).wait_recv()
            part[1, rows, :] = (held[rows, :] + cin[1, rows, :].astype(F32)).astype(BF)
            half_copy(i).start()
        c_arrival(0).wait_recv()
        for i in range(2):
            finish(halves[i], 0)

    @pl.when(yl == 2)
    def _():
        for i in range(2):
            half_copy(i).wait_recv()
            finish(halves[i], 1)

    @pl.when(yl == 3)
    def _():
        c_arrival(2).wait_recv()
        c_arrival(1).wait_recv()
        for i in range(2):
            round_pass(i).wait_recv()
            finish(halves[i], 1, 2, 0)

    for q in range(4):

        @pl.when((z != 7) | (yl != q))
        def _():
            remote(
                row_src.at[pl.ds(0, 8)], row_in.at[q], n_send.at[0], n_recv.at[q], up
            ).wait_recv()

    new_ref[...] = (row_in[0] + row_in[1]) + (row_in[2] + row_in[3])

    @pl.when(z == 7)
    def _():
        @pl.loop(0, 32)
        def _(to):
            @pl.when(to != r)
            def _():
                n_copy(to).wait_send()

    for h in range(2):

        @pl.when(gives_piece & jnp.logical_not(piece_self(h)))
        def _():
            piece_copy(h).wait_send()

    for h in range(2):

        @pl.when(gives_mirror & jnp.logical_not(mirror_self(h)))
        def _():
            mirror_copy(h).wait_send()

    for step in range(4):
        for way in range(2):
            for rows in range(2):
                if step < 3 or rows == way:
                    g_copy(way, step, rows).wait_send()
    for i in range(2):

        @pl.when(near(i) >= yl)
        def _():
            y_copy(near(i)).wait_send()

    for y in range(4):

        @pl.when(y >= yl)
        def _():
            for d in (1, 3):
                x_copy(y, d).wait_send()

                @pl.when(y // 2 == yh)
                def _():
                    h_copy(y, d).wait_send()

            @pl.when(y // 2 != yh)
            def _():
                two_copy(y).wait_send()

            for d in range(4):
                k_copy(y, d).wait_send()

        if y > 0:

            if y != 2:

                @pl.when((y > yl) & ((y != 3) | (yl != 0)))
                def _():
                    c_copy(y).wait_send()

    for i in range(2):

        @pl.when(yl == 0)
        def _():
            round_copy(i).wait_send()
            half_copy(i).wait_send()

        @pl.when(yl == 1)
        def _():
            round_pass(i).wait_send()
            half_copy(i).wait_send()


def shards(green, coupling):
    rows, cols, width = green.shape
    orbit = coupling.shape[0]
    high, wide = rows * orbit, cols * orbit
    vmem = pl.BlockSpec(memory_space=pltpu.VMEM)
    dma = pltpu.SemaphoreType.DMA
    collision, fresh = pl.pallas_call(
        kernel,
        out_shape=(
            jax.ShapeDtypeStruct((high, wide), BF),
            jax.ShapeDtypeStruct((8, 128), F32),
        ),
        in_specs=[pl.BlockSpec(memory_space=pl.ANY)] * 2,
        out_specs=(vmem, vmem),
        scratch_shapes=[
            pltpu.VMEM((rows, cols, width), BF),
            pltpu.VMEM((1, orbit), F32),
            pltpu.VMEM((high, wide), BF),
            dma((2,)),
            pltpu.VMEM((8, high, wide), BF),
            pltpu.VMEM((2, high, high), BF),
            pltpu.VMEM((2, high, high), BF),
            pltpu.VMEM((4, 8, high, high), BF),
            pltpu.VMEM((3, high, wide), BF),
            pltpu.VMEM((3, high, wide), BF),
            pltpu.VMEM((high, wide), BF),
            pltpu.VMEM((high, wide), F32),
            pltpu.VMEM((high, wide), F32),
            pltpu.VMEM((256, 128), F32),
            pltpu.VMEM((256, 128), F32),
            pltpu.VMEM((4, 8, 128), F32),
            dma((2, 4, 2)),
            dma((2, 4, 2)),
            dma((2,)),
            dma((2,)),
            dma((2,)),
            dma((2,)),
            dma((4,)),
            dma((4,)),
            dma((4, 2)),
            dma((4, 2)),
            dma((4, 2)),
            dma((4, 2)),
            dma((4, 4)),
            dma((4, 4)),
            dma((3,)),
            dma((3,)),
            dma((2,)),
            dma((2,)),
            dma((2,)),
            dma((2,)),
            dma((2,)),
            dma((2,)),
            dma((32,)),
            dma((4,)),
        ],
        compiler_params=pltpu.CompilerParams(
            collective_id=0, has_side_effects=True, vmem_limit_bytes=54848 << 10
        ),
        cost_estimate=pl.CostEstimate(
            flops=2 * high * wide * 8192, bytes_accessed=4 * high * wide, transcendentals=0
        ),
        name="collide",
    )(green, coupling.reshape(1, orbit))
    collision = collision.reshape(rows, orbit, cols, orbit).transpose(0, 2, 1, 3)
    collision = collision.reshape(rows, cols, width)
    fresh = fresh.reshape(2, 4, 2, orbit).transpose(1, 2, 0, 3).reshape(cols, 128)
    return (collision, fresh.astype(BF))


def solution(mesh):
    placed = (P("row", "col", None), P())
    return jax.shard_map(
        shards,
        mesh=mesh,
        in_specs=placed,
        out_specs=(P("row", "col", None), P("col", "row")),
        check_vma=False,
    )
```

```python
import jax
import jax.numpy as jnp
from jax import lax
from jax.experimental import pallas as pl
from jax.experimental.pallas import tpu as pltpu
from jax.sharding import PartitionSpec as P

step_size = 0.01
MESH = pl.DeviceIdType.MESH
BF = jnp.bfloat16
F32 = jnp.float32


def kernel(
    green_ref,
    strength_ref,
    out_ref,
    new_ref,
    raw,
    coupling_ref,
    x_ref,
    in_sem,
    gz,
    mir,
    own,
    sig,
    part,
    cin,
    relay,
    acc,
    held,
    row_mid,
    row_src,
    row_in,
    g_send,
    g_recv,
    m_send,
    m_recv,
    s_send,
    s_recv,
    y_send,
    y_recv,
    x_send,
    x_recv,
    h_send,
    h_recv,
    k_send,
    k_recv,
    c_send,
    c_recv,
    e_send,
    e_recv,
    r_send,
    r_recv,
    q_send,
    q_recv,
    n_send,
    n_recv,
):
    r = lax.axis_index("row")
    c = lax.axis_index("col")
    yl, z = r // 8, r % 8
    yh, x, k = c // 8, (c // 2) % 4, c % 2
    goal = c // 4

    def part_of(x_):
        m = jnp.where((x_ == 1) | (x_ == 2), 2, 0) + x_ // 2
        return 2 * jnp.where(yl % 2 == 0, m, 3 - m) + k

    def place_of(j):
        m = jnp.where(yl % 2 == 0, j // 2, 3 - j // 2)
        return jnp.where(m == 1, 3, (m + 1) // 2)

    part_at = part_of(x)
    m_at = part_at // 2

    def at(yl_, z_, yh_, x_, k_):
        return (yl_ * 8 + z_, yh_ * 8 + x_ * 2 + k_)

    def remote(src, dst, send, recv, device):
        return pltpu.make_async_remote_copy(
            src, dst, send, recv, device_id=device, device_id_type=MESH
        )

    up, down = at(yl, (z + 1) % 8, yh, x, k), at(yl, (z + 7) % 8, yh, x, k)
    other = at(yl, z, yh, x, 1 - k)
    across = at(yl, z, 1 - yh, x, k)

    gives_mirror = goal >= yl

    def mirror_to(h):
        return at(yl, (x % 2) * 4 + k * 2 + h, yh, place_of(z), z % 2)

    def mirror_self(h):
        return (z == part_at) & (z == (x % 2) * 4 + k * 2 + h)

    def mirror_from(s):
        return at(yl, part_at, yh, s * 2 + z // 4, (z // 2) % 2)

    def mirror_from_self(s):
        return (z == part_at) & (x == s * 2 + z // 4) & (k == (z // 2) % 2)

    gives_piece = yl >= goal

    def piece_to(h):
        return at(goal, z, yl // 2, (x + 4 + k * (2 * (x % 2) - 1)) % 4, h)

    def piece_self(h):
        return (goal == yl) & (k == 0) if h == 0 else False

    def piece_from(s):
        return at(2 * yh + s, z, yl // 2, (yl % 2) * 2 + m_at // 2, m_at % 2)

    def piece_from_self(s):
        mine = (2 * yh + s == yl) & (x == (yl % 2) * 2 + m_at // 2) & (k == m_at % 2)
        return mine & (yl // 2 == yh)

    def adds(q):
        return (q < yl) & ((yl == 1) | (q != 0))

    def one(flag):
        return jnp.where(flag, 1, 0)

    barrier = pltpu.get_barrier_semaphore()
    loads = [
        pltpu.make_async_copy(green_ref, raw, in_sem.at[0]),
        pltpu.make_async_copy(strength_ref, coupling_ref, in_sem.at[1]),
    ]
    for load in loads:
        load.start()

    def greet(device):
        pl.semaphore_signal(barrier, inc=1, device_id=device, device_id_type=MESH)

    greet(up)
    greet(down)
    greet(other)
    for d in (1, 2, 3):
        greet(at(yl, z, yh, (x + d) % 4, k))
    for s in range(2):

        @pl.when((2 * yh + s >= yl) & jnp.logical_not(mirror_from_self(s)))
        def _():
            greet(mirror_from(s))

        @pl.when((2 * yh + s >= yl) & jnp.logical_not(piece_from_self(s)))
        def _():
            greet(piece_from(s))

    @pl.when(3 - 2 * yh >= yl)
    def _():
        greet(across)

    for q in range(3):

        @pl.when(adds(q))
        def _():
            greet(at(q, z, yh, x, k))

    @pl.when(yl == 1)
    def _():
        greet(at(0, z, 1 - yh, x, k))

    @pl.when(yl == 3)
    def _():
        greet(at(1, z, 1 - yh, x, k))

    for q in range(4):

        @pl.when((z != 7) | (yl != q))
        def _():
            greet(at(q, 7, yh, x, k))

    for load in loads:
        load.wait()
    for t in range(0, 4, 2):
        pair_of_times = raw[t * 8 : t * 8 + 16, :]
        for i in range(2):
            block = pair_of_times[i * 8 : i * 8 + 8, :].reshape(8, 64, 64)
            first_row = (t + i) * 64
            x_ref[first_row : first_row + 64, :] = block.swapaxes(0, 1).reshape(64, 512)

    peers = 6 + jnp.minimum(3 - yl, 2) + one(yl == 1) + jnp.where(z == 7, 31, 0)
    peers += one(2 * yh + 1 >= yl)
    for h in range(2):
        peers += one(gives_mirror & jnp.logical_not(mirror_self(h)))
        peers += one(gives_piece & jnp.logical_not(piece_self(h)))
    pl.semaphore_wait(barrier, peers)

    def half_of(h):
        return x_ref.at[:, pl.ds(h * 256, 256)]

    def piece_copy(h):
        return remote(
            half_of(h), own.at[yl % 2], s_send.at[h], s_recv.at[yl % 2], piece_to(h)
        )

    def piece_arrival(s):
        return remote(half_of(0), own.at[s], s_send.at[0], s_recv.at[s], up)

    def g_copy(way, step, rows):
        held = (z - step + 8) % 8 if way == 0 else (z + step) % 8
        src = x_ref if step == 0 else gz.at[held]
        return remote(
            src.at[pl.ds(rows * 128, 128)],
            gz.at[held, pl.ds(rows * 128, 128)],
            g_send.at[way, step, rows],
            g_recv.at[way, step, rows],
            up if way == 0 else down,
        )

    def g_arrival(way, step, rows):
        held = (z - step + 7) % 8 if way == 0 else (z + step + 1) % 8
        return remote(
            x_ref.at[pl.ds(0, 128)],
            gz.at[held, pl.ds(rows * 128, 128)],
            g_send.at[way, step, rows],
            g_recv.at[way, step, rows],
            up,
        )

    def g_pass(step):
        for rows in range(2):
            for way in range(2):
                g_arrival(way, step - 1, rows).wait_recv()
                if step < 3 or rows == way:
                    g_copy(way, step, rows).start()

    def mirror_copy(h):
        return remote(
            half_of(h), mir.at[x // 2], m_send.at[h], m_recv.at[x // 2], mirror_to(h)
        )

    def mirror_arrival(s):
        return remote(half_of(0), mir.at[s], m_send.at[0], m_recv.at[s], up)

    for h in range(2):

        @pl.when(gives_mirror & jnp.logical_not(mirror_self(h)))
        def _():
            mirror_copy(h).start()

        @pl.when(gives_mirror & mirror_self(h))
        def _():
            mir[x // 2] = x_ref[:, h * 256 : (h + 1) * 256]

    for rows in range(2):
        for way in range(2):
            g_copy(way, 0, rows).start()
    for h in range(2):

        @pl.when(gives_piece & jnp.logical_not(piece_self(h)))
        def _():
            piece_copy(h).start()

        @pl.when(gives_piece & piece_self(h))
        def _():
            own[yl % 2] = x_ref[:, h * 256 : (h + 1) * 256]

    gz[z] = x_ref[...]

    def y_copy(y):
        return remote(
            sig.at[y, part_at], sig.at[y, part_at], y_send.at[y], y_recv.at[y], across
        )

    def x_copy(y, d):
        return remote(
            sig.at[y, part_at],
            sig.at[y, part_at],
            x_send.at[y, d // 2],
            x_recv.at[y, d // 2],
            at(yl, z, yh, (x + d) % 4, k),
        )

    def two_copy(y):
        return remote(
            sig.at[y, part_at],
            sig.at[y, part_at],
            h_send.at[y, 0],
            h_recv.at[y, 0],
            at(yl, z, yh, (x + 2) % 4, k),
        )

    def two_arrival(y):
        j = behind(2)
        return remote(
            sig.at[y, j], sig.at[y, j], h_send.at[y, 0], h_recv.at[y, 0], up
        )

    def behind(d):
        return part_of((x + 4 - d) % 4)

    def x_arrival(y, d):
        j = behind(d)
        return remote(
            sig.at[y, j], sig.at[y, j], x_send.at[y, 0], x_recv.at[y, d // 2], up
        )

    def h_copy(y, d):
        rows = pl.ds((d // 2) * 128, 128)
        block = sig.at[y, behind(d), rows]
        return remote(
            block,
            block,
            h_send.at[y, d // 2],
            h_recv.at[y, d // 2],
            at(yl, z, yh, (x + d) % 4, k),
        )

    def h_arrival(y, d):
        block = sig.at[y, behind(2), pl.ds((d // 2) * 128, 128)]
        return remote(block, block, h_send.at[y, 0], h_recv.at[y, d // 2], up)

    def k_copy(y, d):
        block = sig.at[y, behind(d)]
        return remote(block, block, k_send.at[y, d], k_recv.at[y, d], other)

    def k_arrival(y, d):
        block = sig.at[y, behind(d) + 1 - 2 * k]
        return remote(block, block, k_send.at[y, d], k_recv.at[y, d], other)

    def spread(y):
        for d in (1, 3):
            x_copy(y, d).start()
        k_copy(y, 0).start()

    def pass_on(y, d):
        @pl.when(y >= yl)
        def _():
            x_arrival(y, d).wait_recv()
            h_copy(y, d).start()
            k_copy(y, d).start()

    def near(i):
        return 2 * yh + 1 - i

    def far(i):
        return 3 - 2 * yh - i

    late = (yh == 0) & (yl < 2)

    def early(i):
        return jnp.logical_not(late & (near(i) == yl))

    strength = coupling_ref[...]
    square = jnp.broadcast_to(strength, (64, 64))
    diagonal = lax.broadcasted_iota(jnp.int32, (64, 64), 0) == lax.broadcasted_iota(
        jnp.int32, (64, 64), 1
    )
    column = jnp.sum(jnp.where(diagonal, square, 0.0), axis=1, keepdims=True)
    pair = column * jnp.concatenate([strength] * 4, axis=1)

    def make(i):
        i_near = i
        s = 1 - i
        y = near(i)

        @pl.when(y >= yl)
        def _():
            @pl.when(jnp.logical_not(mirror_from_self(s)))
            def _():
                mirror_arrival(s).wait_recv()

            @pl.when(jnp.logical_not(piece_from_self(s)))
            def _():
                piece_arrival(s).wait_recv()

            partner = mir[s].T
            later = lax.broadcasted_iota(jnp.int32, (64, 256), 1) // 64
            first = 32 * (y - yl) + 4 * z - 4 * part_at
            for i in range(4):
                rows = slice(i * 64, (i + 1) * 64)
                g = own[s, rows, :].astype(F32)
                value = pair * (g * g) * partner[rows].astype(F32)
                keep = later <= first + i
                sig[y, part_at, rows, :] = jnp.where(keep, value, 0.0).astype(BF)
            y_copy(y).start()

            @pl.when(early(i_near))
            def _():
                spread(y)

    def hand_on(i):
        y = far(i)

        @pl.when(y >= yl)
        def _():
            y_copy(y).wait_recv()
            spread(y)
            two_copy(y).start()

    def swap(y):
        @pl.when((y >= yl) & (y // 2 == yh))
        def _():
            for d in (1, 3):
                h_arrival(y, d).wait_recv()
            k_copy(y, 2).start()

    def collect(y):
        @pl.when(y >= yl)
        def _():
            for d in (1, 3):
                x_arrival(y, d).wait_recv()
                k_copy(y, d).start()
            two_arrival(y).wait_recv()
            k_copy(y, 2).start()

    def c_copy(y):
        return remote(
            part.at[y - 1],
            cin.at[yl],
            c_send.at[y - 1],
            c_recv.at[yl],
            at(y, z, yh, x, k),
        )

    def half_copy(i):
        rows = pl.ds(i * 128, 128)
        return remote(
            part.at[1, rows],
            cin.at[1, rows],
            e_send.at[i],
            e_recv.at[i],
            at(jnp.minimum(yl + 1, 2), z, yh, x, k),
        )

    def round_copy(i):
        rows = pl.ds(i * 128, 128)
        return remote(
            part.at[2, rows],
            relay.at[rows],
            r_send.at[i],
            r_recv.at[i],
            at(1, z, 1 - yh, x, k),
        )

    def round_pass(i):
        rows = pl.ds(i * 128, 128)
        return remote(
            relay.at[rows],
            cin.at[0, rows],
            q_send.at[i],
            q_recv.at[i],
            at(3, z, 1 - yh, x, k),
        )

    def c_arrival(q):
        return remote(part.at[0], cin.at[q], c_send.at[0], c_recv.at[q], up)

    def product(y, flag=True):
        @pl.when((y >= yl) & flag)
        def _():
            @pl.when(late & (y == yl))
            def _():
                swap(y)

            for d in range(4):
                k_arrival(y, d).wait_recv()
            total = jnp.zeros((256, 512), F32)
            for j in range(8):
                total += jnp.dot(sig[y, j], gz[j], preferred_element_type=F32)

            if y == 3:
                for q in range(4):
                    row_mid[q * 64 : (q + 1) * 64, :] = (
                        step_size * total[192:256, q * 128 : (q + 1) * 128]
                    )

            @pl.when((y > yl) & ((y != 2) | (yl != 1)))
            def _():
                part[y - 1] = total.astype(BF)
                if y == 1:
                    c_copy(y).start()
                elif y == 2:
                    for i in range(2):
                        half_copy(i).start()
                else:

                    @pl.when(yl != 0)
                    def _():
                        c_copy(y).start()

                    @pl.when(yl == 0)
                    def _():
                        for i in range(2):
                            round_copy(i).start()

            @pl.when((y == 2) & (yl == 1))
            def _():
                held[...] = total

            @pl.when(y == yl)
            def _():
                acc[...] = total

    def pass_both(y, flag):
        @pl.when(flag)
        def _():
            pass_on(y, 1)
            pass_on(y, 3)

    make(0)
    make(1)
    g_pass(1)
    pass_both(near(0), early(0))
    hand_on(0)
    g_pass(2)
    pass_both(near(1), early(1))
    hand_on(1)

    @pl.when(late)
    def _():
        spread(yl)

    g_pass(3)
    for i in range(2):

        @pl.when(early(i))
        def _():
            swap(near(i))

    collect(far(0))
    for way in range(2):
        g_arrival(way, 3, way).wait_recv()
    first = (yh == 0) & (yl == 0)
    product(1, first)
    for y in (3, 2, 1, 0):

        @pl.when(far(1) == y)
        def _():
            collect(y)

        if y == 1:
            pass_both(yl, late)
        product(y, jnp.logical_not(first) if y == 1 else True)

    def n_copy(to):
        return remote(
            row_src.at[pl.ds(pl.multiple_of(to * 8, 8), 8)],
            row_in.at[yl],
            n_send.at[to],
            n_recv.at[yl],
            (to, c),
        )

    @pl.when(z == 7)
    def _():
        @pl.when(yl == 3)
        def _():
            for q in range(4):
                row_mid[q * 64 : (q + 1) * 64, :] += x_ref[
                    192:256, q * 128 : (q + 1) * 128
                ].astype(F32)

        for q in range(4):
            for i in range(2):
                row_src[pl.ds(i * 4 + q, 32, stride=8), :] = row_mid[
                    pl.ds(q * 64 + i, 32, stride=2), :
                ]

        @pl.loop(0, 32)
        def _(to):
            @pl.when(to != r)
            def _():
                n_copy(to).start()

        row_in[yl] = row_src[pl.ds(pl.multiple_of(r * 8, 8), 8), :]

    def finish(rows, *slots):
        total = acc[rows, :]
        for q in slots:
            total += cin[q, rows, :].astype(F32)
        out_ref[rows, :] = (step_size * total).astype(BF)

    halves = [slice(0, 128), slice(128, 256)]

    @pl.when(yl == 0)
    def _():
        for i in range(2):
            finish(halves[i])

    @pl.when(yl == 1)
    def _():
        for i in range(2):
            round_copy(i).wait_recv()
            round_pass(i).start()
        for i in range(2):
            rows = halves[i]
            half_copy(i).wait_recv()
            part[1, rows, :] = (held[rows, :] + cin[1, rows, :].astype(F32)).astype(BF)
            half_copy(i).start()
        c_arrival(0).wait_recv()
        for i in range(2):
            finish(halves[i], 0)

    @pl.when(yl == 2)
    def _():
        for i in range(2):
            half_copy(i).wait_recv()
            finish(halves[i], 1)

    @pl.when(yl == 3)
    def _():
        c_arrival(2).wait_recv()
        c_arrival(1).wait_recv()
        for i in range(2):
            round_pass(i).wait_recv()
            finish(halves[i], 1, 2, 0)

    for q in range(4):

        @pl.when((z != 7) | (yl != q))
        def _():
            remote(
                row_src.at[pl.ds(0, 8)], row_in.at[q], n_send.at[0], n_recv.at[q], up
            ).wait_recv()

    new_ref[...] = (row_in[0] + row_in[1]) + (row_in[2] + row_in[3])

    @pl.when(z == 7)
    def _():
        @pl.loop(0, 32)
        def _(to):
            @pl.when(to != r)
            def _():
                n_copy(to).wait_send()

    for h in range(2):

        @pl.when(gives_piece & jnp.logical_not(piece_self(h)))
        def _():
            piece_copy(h).wait_send()

    for h in range(2):

        @pl.when(gives_mirror & jnp.logical_not(mirror_self(h)))
        def _():
            mirror_copy(h).wait_send()

    for step in range(4):
        for way in range(2):
            for rows in range(2):
                if step < 3 or rows == way:
                    g_copy(way, step, rows).wait_send()
    for i in range(2):

        @pl.when(near(i) >= yl)
        def _():
            y_copy(near(i)).wait_send()

    for y in range(4):

        @pl.when(y >= yl)
        def _():
            for d in (1, 3):
                x_copy(y, d).wait_send()

                @pl.when(y // 2 == yh)
                def _():
                    h_copy(y, d).wait_send()

            @pl.when(y // 2 != yh)
            def _():
                two_copy(y).wait_send()

            for d in range(4):
                k_copy(y, d).wait_send()

        if y > 0:

            if y != 2:

                @pl.when((y > yl) & ((y != 3) | (yl != 0)))
                def _():
                    c_copy(y).wait_send()

    for i in range(2):

        @pl.when(yl == 0)
        def _():
            round_copy(i).wait_send()
            half_copy(i).wait_send()

        @pl.when(yl == 1)
        def _():
            round_pass(i).wait_send()
            half_copy(i).wait_send()


def shards(green, coupling):
    rows, cols, width = green.shape
    orbit = coupling.shape[0]
    high, wide = rows * orbit, cols * orbit
    vmem = pl.BlockSpec(memory_space=pltpu.VMEM)
    dma = pltpu.SemaphoreType.DMA
    collision, fresh = pl.pallas_call(
        kernel,
        out_shape=(
            jax.ShapeDtypeStruct((high, wide), BF),
            jax.ShapeDtypeStruct((8, 128), F32),
        ),
        in_specs=[pl.BlockSpec(memory_space=pl.ANY)] * 2,
        out_specs=(vmem, vmem),
        scratch_shapes=[
            pltpu.VMEM((rows * cols, width), BF),
            pltpu.VMEM((1, orbit), F32),
            pltpu.VMEM((high, wide), BF),
            dma((2,)),
            pltpu.VMEM((8, high, wide), BF),
            pltpu.VMEM((2, high, high), BF),
            pltpu.VMEM((2, high, high), BF),
            pltpu.VMEM((4, 8, high, high), BF),
            pltpu.VMEM((3, high, wide), BF),
            pltpu.VMEM((3, high, wide), BF),
            pltpu.VMEM((high, wide), BF),
            pltpu.VMEM((high, wide), F32),
            pltpu.VMEM((high, wide), F32),
            pltpu.VMEM((256, 128), F32),
            pltpu.VMEM((256, 128), F32),
            pltpu.VMEM((4, 8, 128), F32),
            dma((2, 4, 2)),
            dma((2, 4, 2)),
            dma((2,)),
            dma((2,)),
            dma((2,)),
            dma((2,)),
            dma((4,)),
            dma((4,)),
            dma((4, 2)),
            dma((4, 2)),
            dma((4, 2)),
            dma((4, 2)),
            dma((4, 4)),
            dma((4, 4)),
            dma((3,)),
            dma((3,)),
            dma((2,)),
            dma((2,)),
            dma((2,)),
            dma((2,)),
            dma((2,)),
            dma((2,)),
            dma((32,)),
            dma((4,)),
        ],
        compiler_params=pltpu.CompilerParams(
            collective_id=0, has_side_effects=True, vmem_limit_bytes=54848 << 10
        ),
        cost_estimate=pl.CostEstimate(
            flops=2 * high * wide * 8192, bytes_accessed=4 * high * wide, transcendentals=0
        ),
        name="collide",
    )(green.reshape(rows * cols, width), coupling.reshape(1, orbit))
    collision = collision.reshape(rows, orbit, cols, orbit).transpose(0, 2, 1, 3)
    collision = collision.reshape(rows, cols, width)
    fresh = fresh.reshape(2, 4, 2, orbit).transpose(1, 2, 0, 3).reshape(cols, 128)
    return (collision, fresh.astype(BF))


def solution(mesh):
    placed = (P("row", "col", None), P())
    return jax.shard_map(
        shards,
        mesh=mesh,
        in_specs=placed,
        out_specs=(P("row", "col", None), P("col", "row")),
        check_vma=False,
    )
```

```python
import jax
import jax.numpy as jnp
from jax import lax
from jax.experimental import pallas as pl
from jax.experimental.pallas import tpu as pltpu
from jax.sharding import PartitionSpec as P

step_size = 0.01
MESH = pl.DeviceIdType.MESH
BF = jnp.bfloat16
F32 = jnp.float32


def kernel(
    green_ref,
    strength_ref,
    out_ref,
    new_ref,
    raw,
    coupling_ref,
    x_ref,
    in_sem,
    gz,
    mir,
    own,
    sig,
    part,
    cin,
    relay,
    acc,
    held,
    row_mid,
    row_src,
    row_in,
    g_send,
    g_recv,
    m_send,
    m_recv,
    s_send,
    s_recv,
    y_send,
    y_recv,
    x_send,
    x_recv,
    h_send,
    h_recv,
    k_send,
    k_recv,
    c_send,
    c_recv,
    e_send,
    e_recv,
    r_send,
    r_recv,
    q_send,
    q_recv,
    n_send,
    n_recv,
):
    r = lax.axis_index("row")
    c = lax.axis_index("col")
    yl, z = r // 8, r % 8
    yh, x, k = c // 8, (c // 2) % 4, c % 2
    goal = c // 4

    def part_of(x_):
        m = jnp.where((x_ == 1) | (x_ == 2), 2, 0) + x_ // 2
        return 2 * jnp.where(yl % 2 == 0, m, 3 - m) + k

    def place_of(j):
        m = jnp.where(yl % 2 == 0, j // 2, 3 - j // 2)
        return jnp.where(m == 1, 3, (m + 1) // 2)

    part_at = part_of(x)
    m_at = part_at // 2

    def at(yl_, z_, yh_, x_, k_):
        return (yl_ * 8 + z_, yh_ * 8 + x_ * 2 + k_)

    def remote(src, dst, send, recv, device):
        return pltpu.make_async_remote_copy(
            src, dst, send, recv, device_id=device, device_id_type=MESH
        )

    up, down = at(yl, (z + 1) % 8, yh, x, k), at(yl, (z + 7) % 8, yh, x, k)
    other = at(yl, z, yh, x, 1 - k)
    across = at(yl, z, 1 - yh, x, k)

    gives_mirror = goal >= yl

    def mirror_to(h):
        return at(yl, (x % 2) * 4 + k * 2 + h, yh, place_of(z), z % 2)

    def mirror_self(h):
        return (z == part_at) & (z == (x % 2) * 4 + k * 2 + h)

    def mirror_from(s):
        return at(yl, part_at, yh, s * 2 + z // 4, (z // 2) % 2)

    def mirror_from_self(s):
        return (z == part_at) & (x == s * 2 + z // 4) & (k == (z // 2) % 2)

    gives_piece = yl >= goal

    def piece_to(h):
        return at(goal, z, yl // 2, (x + 4 + k * (2 * (x % 2) - 1)) % 4, h)

    def piece_self(h):
        return (goal == yl) & (k == 0) if h == 0 else False

    def piece_from(s):
        return at(2 * yh + s, z, yl // 2, (yl % 2) * 2 + m_at // 2, m_at % 2)

    def piece_from_self(s):
        mine = (2 * yh + s == yl) & (x == (yl % 2) * 2 + m_at // 2) & (k == m_at % 2)
        return mine & (yl // 2 == yh)

    def adds(q):
        return (q < yl) & ((yl == 1) | (q != 0))

    def one(flag):
        return jnp.where(flag, 1, 0)

    barrier = pltpu.get_barrier_semaphore()
    loads = [
        pltpu.make_async_copy(green_ref, raw, in_sem.at[0]),
        pltpu.make_async_copy(strength_ref, coupling_ref, in_sem.at[1]),
    ]
    for load in loads:
        load.start()

    def greet(device):
        pl.semaphore_signal(barrier, inc=1, device_id=device, device_id_type=MESH)

    greet(up)
    greet(down)
    greet(other)
    for d in (1, 2, 3):
        greet(at(yl, z, yh, (x + d) % 4, k))
    for s in range(2):

        @pl.when((2 * yh + s >= yl) & jnp.logical_not(mirror_from_self(s)))
        def _():
            greet(mirror_from(s))

        @pl.when((2 * yh + s >= yl) & jnp.logical_not(piece_from_self(s)))
        def _():
            greet(piece_from(s))

    @pl.when(3 - 2 * yh >= yl)
    def _():
        greet(across)

    for q in range(3):

        @pl.when(adds(q))
        def _():
            greet(at(q, z, yh, x, k))

    @pl.when(yl == 1)
    def _():
        greet(at(0, z, 1 - yh, x, k))

    @pl.when(yl == 3)
    def _():
        greet(at(1, z, 1 - yh, x, k))

    for q in range(4):

        @pl.when((z != 7) | (yl != q))
        def _():
            greet(at(q, 7, yh, x, k))

    for load in loads:
        load.wait()
    for t in range(0, 4, 2):
        pair_of_times = raw[t * 8 : t * 8 + 16, :]
        for i in range(2):
            block = pair_of_times[i * 8 : i * 8 + 8, :].reshape(8, 64, 64)
            first_row = (t + i) * 64
            x_ref[first_row : first_row + 64, :] = block.swapaxes(0, 1).reshape(64, 512)

    peers = 6 + jnp.minimum(3 - yl, 2) + one(yl == 1) + jnp.where(z == 7, 31, 0)
    peers += one(2 * yh + 1 >= yl)
    for h in range(2):
        peers += one(gives_mirror & jnp.logical_not(mirror_self(h)))
        peers += one(gives_piece & jnp.logical_not(piece_self(h)))
    pl.semaphore_wait(barrier, peers)

    def half_of(h):
        return x_ref.at[:, pl.ds(h * 256, 256)]

    def piece_copy(h):
        return remote(
            half_of(h), own.at[yl % 2], s_send.at[h], s_recv.at[yl % 2], piece_to(h)
        )

    def piece_arrival(s):
        return remote(half_of(0), own.at[s], s_send.at[0], s_recv.at[s], up)

    def g_copy(way, step, rows):
        held = (z - step + 8) % 8 if way == 0 else (z + step) % 8
        src = x_ref if step == 0 else gz.at[held]
        return remote(
            src.at[pl.ds(rows * 128, 128)],
            gz.at[held, pl.ds(rows * 128, 128)],
            g_send.at[way, step, rows],
            g_recv.at[way, step, rows],
            up if way == 0 else down,
        )

    def g_arrival(way, step, rows):
        held = (z - step + 7) % 8 if way == 0 else (z + step + 1) % 8
        return remote(
            x_ref.at[pl.ds(0, 128)],
            gz.at[held, pl.ds(rows * 128, 128)],
            g_send.at[way, step, rows],
            g_recv.at[way, step, rows],
            up,
        )

    def g_pass(step):
        for rows in range(2):
            for way in range(2):
                g_arrival(way, step - 1, rows).wait_recv()
                if step < 3 or rows == way:
                    g_copy(way, step, rows).start()

    def mirror_copy(h):
        return remote(
            half_of(h), mir.at[x // 2], m_send.at[h], m_recv.at[x // 2], mirror_to(h)
        )

    def mirror_arrival(s):
        return remote(half_of(0), mir.at[s], m_send.at[0], m_recv.at[s], up)

    for h in range(2):

        @pl.when(gives_mirror & jnp.logical_not(mirror_self(h)))
        def _():
            mirror_copy(h).start()

        @pl.when(gives_mirror & mirror_self(h))
        def _():
            mir[x // 2] = x_ref[:, h * 256 : (h + 1) * 256]

    for rows in range(2):
        for way in range(2):
            g_copy(way, 0, rows).start()
    for h in range(2):

        @pl.when(gives_piece & jnp.logical_not(piece_self(h)))
        def _():
            piece_copy(h).start()

        @pl.when(gives_piece & piece_self(h))
        def _():
            own[yl % 2] = x_ref[:, h * 256 : (h + 1) * 256]

    gz[z] = x_ref[...]

    def y_copy(y):
        return remote(
            sig.at[y, part_at], sig.at[y, part_at], y_send.at[y], y_recv.at[y], across
        )

    def x_copy(y, d):
        return remote(
            sig.at[y, part_at],
            sig.at[y, part_at],
            x_send.at[y, d // 2],
            x_recv.at[y, d // 2],
            at(yl, z, yh, (x + d) % 4, k),
        )

    def two_copy(y):
        return remote(
            sig.at[y, part_at],
            sig.at[y, part_at],
            h_send.at[y, 0],
            h_recv.at[y, 0],
            at(yl, z, yh, (x + 2) % 4, k),
        )

    def two_arrival(y):
        j = behind(2)
        return remote(
            sig.at[y, j], sig.at[y, j], h_send.at[y, 0], h_recv.at[y, 0], up
        )

    def behind(d):
        return part_of((x + 4 - d) % 4)

    def x_arrival(y, d):
        j = behind(d)
        return remote(
            sig.at[y, j], sig.at[y, j], x_send.at[y, 0], x_recv.at[y, d // 2], up
        )

    def h_copy(y, d):
        rows = pl.ds((d // 2) * 128, 128)
        block = sig.at[y, behind(d), rows]
        return remote(
            block,
            block,
            h_send.at[y, d // 2],
            h_recv.at[y, d // 2],
            at(yl, z, yh, (x + d) % 4, k),
        )

    def h_arrival(y, d):
        block = sig.at[y, behind(2), pl.ds((d // 2) * 128, 128)]
        return remote(block, block, h_send.at[y, 0], h_recv.at[y, d // 2], up)

    def k_copy(y, d):
        block = sig.at[y, behind(d)]
        return remote(block, block, k_send.at[y, d], k_recv.at[y, d], other)

    def k_arrival(y, d):
        block = sig.at[y, behind(d) + 1 - 2 * k]
        return remote(block, block, k_send.at[y, d], k_recv.at[y, d], other)

    def spread(y):
        for d in (1, 3):
            x_copy(y, d).start()
        k_copy(y, 0).start()

    def pass_on(y, d):
        @pl.when(y >= yl)
        def _():
            x_arrival(y, d).wait_recv()
            h_copy(y, d).start()
            k_copy(y, d).start()

    def near(i):
        return 2 * yh + 1 - i

    def far(i):
        return 3 - 2 * yh - i

    late = (yh == 0) & (yl < 2)

    def early(i):
        return jnp.logical_not(late & (near(i) == yl))

    strength = coupling_ref[...]
    square = jnp.broadcast_to(strength, (64, 64))
    diagonal = lax.broadcasted_iota(jnp.int32, (64, 64), 0) == lax.broadcasted_iota(
        jnp.int32, (64, 64), 1
    )
    column = jnp.sum(jnp.where(diagonal, square, 0.0), axis=1, keepdims=True)
    pair = column * jnp.concatenate([strength] * 4, axis=1)

    def make(i):
        i_near = i
        s = 1 - i
        y = near(i)

        @pl.when(y >= yl)
        def _():
            @pl.when(jnp.logical_not(mirror_from_self(s)))
            def _():
                mirror_arrival(s).wait_recv()

            @pl.when(jnp.logical_not(piece_from_self(s)))
            def _():
                piece_arrival(s).wait_recv()

            partner = mir[s].T
            later = lax.broadcasted_iota(jnp.int32, (64, 256), 1) // 64
            first = 32 * (y - yl) + 4 * z - 4 * part_at
            for i in range(4):
                rows = slice(i * 64, (i + 1) * 64)
                g = own[s, rows, :].astype(F32)
                value = pair * (g * g) * partner[rows].astype(F32)
                keep = later <= first + i
                sig[y, part_at, rows, :] = jnp.where(keep, value, 0.0).astype(BF)
            y_copy(y).start()

            @pl.when(early(i_near))
            def _():
                spread(y)

    def hand_on(i):
        y = far(i)

        @pl.when(y >= yl)
        def _():
            y_copy(y).wait_recv()
            spread(y)
            two_copy(y).start()

    def swap(y):
        @pl.when((y >= yl) & (y // 2 == yh))
        def _():
            for d in (1, 3):
                h_arrival(y, d).wait_recv()
            k_copy(y, 2).start()

    def collect(y):
        @pl.when(y >= yl)
        def _():
            for d in (1, 3):
                x_arrival(y, d).wait_recv()
                k_copy(y, d).start()
            two_arrival(y).wait_recv()
            k_copy(y, 2).start()

    def c_copy(y):
        return remote(
            part.at[y - 1],
            cin.at[yl],
            c_send.at[y - 1],
            c_recv.at[yl],
            at(y, z, yh, x, k),
        )

    def quarter_copy(i):
        rows = pl.ds(i * 64, 64)
        return remote(
            part.at[1, rows],
            cin.at[1, rows],
            e_send.at[i],
            e_recv.at[i],
            at(jnp.minimum(yl + 1, 2), z, yh, x, k),
        )

    def round_copy(i):
        rows = pl.ds(i * 64, 64)
        return remote(
            part.at[2, rows],
            relay.at[rows],
            r_send.at[i],
            r_recv.at[i],
            at(1, z, 1 - yh, x, k),
        )

    def round_pass(i):
        rows = pl.ds(i * 64, 64)
        return remote(
            relay.at[rows],
            cin.at[0, rows],
            q_send.at[i],
            q_recv.at[i],
            at(3, z, 1 - yh, x, k),
        )

    def c_arrival(q):
        return remote(part.at[0], cin.at[q], c_send.at[0], c_recv.at[q], up)

    def product(y, flag=True):
        @pl.when((y >= yl) & flag)
        def _():
            @pl.when(late & (y == yl))
            def _():
                swap(y)

            for d in range(4):
                k_arrival(y, d).wait_recv()
            total = jnp.zeros((256, 512), F32)
            for j in range(8):
                total += jnp.dot(sig[y, j], gz[j], preferred_element_type=F32)

            if y == 3:
                for q in range(4):
                    row_mid[q * 64 : (q + 1) * 64, :] = (
                        step_size * total[192:256, q * 128 : (q + 1) * 128]
                    )

            @pl.when((y > yl) & ((y != 2) | (yl != 1)))
            def _():
                part[y - 1] = total.astype(BF)
                if y == 1:
                    c_copy(y).start()
                elif y == 2:
                    for i in range(4):
                        quarter_copy(i).start()
                else:

                    @pl.when(yl != 0)
                    def _():
                        c_copy(y).start()

                    @pl.when(yl == 0)
                    def _():
                        for i in range(4):
                            round_copy(i).start()

            @pl.when((y == 2) & (yl == 1))
            def _():
                held[...] = total

            @pl.when(y == yl)
            def _():
                acc[...] = total

    def pass_both(y, flag):
        @pl.when(flag)
        def _():
            pass_on(y, 1)
            pass_on(y, 3)

    make(0)
    make(1)
    g_pass(1)
    pass_both(near(0), early(0))
    hand_on(0)
    g_pass(2)
    pass_both(near(1), early(1))
    hand_on(1)

    @pl.when(late)
    def _():
        spread(yl)

    g_pass(3)
    for i in range(2):

        @pl.when(early(i))
        def _():
            swap(near(i))

    collect(far(0))
    for way in range(2):
        g_arrival(way, 3, way).wait_recv()
    first = (yh == 0) & (yl == 0)
    product(1, first)
    for y in (3, 2, 1, 0):

        @pl.when(far(1) == y)
        def _():
            collect(y)

        if y == 1:
            pass_both(yl, late)
        product(y, jnp.logical_not(first) if y == 1 else True)

    def n_copy(to):
        return remote(
            row_src.at[pl.ds(pl.multiple_of(to * 8, 8), 8)],
            row_in.at[yl],
            n_send.at[to],
            n_recv.at[yl],
            (to, c),
        )

    @pl.when(z == 7)
    def _():
        @pl.when(yl == 3)
        def _():
            for q in range(4):
                row_mid[q * 64 : (q + 1) * 64, :] += x_ref[
                    192:256, q * 128 : (q + 1) * 128
                ].astype(F32)

        for q in range(4):
            for i in range(2):
                row_src[pl.ds(i * 4 + q, 32, stride=8), :] = row_mid[
                    pl.ds(q * 64 + i, 32, stride=2), :
                ]

        @pl.loop(0, 32)
        def _(to):
            @pl.when(to != r)
            def _():
                n_copy(to).start()

        row_in[yl] = row_src[pl.ds(pl.multiple_of(r * 8, 8), 8), :]

    def finish(rows, *slots):
        total = acc[rows, :]
        for q in slots:
            total += cin[q, rows, :].astype(F32)
        out_ref[rows, :] = (step_size * total).astype(BF)

    quarters = [slice(i * 64, i * 64 + 64) for i in range(4)]

    @pl.when(yl == 0)
    def _():
        for i in range(4):
            finish(quarters[i])

    @pl.when(yl == 1)
    def _():
        for i in range(4):
            round_copy(i).wait_recv()
            round_pass(i).start()
        for i in range(4):
            rows = quarters[i]
            quarter_copy(i).wait_recv()
            part[1, rows, :] = (held[rows, :] + cin[1, rows, :].astype(F32)).astype(BF)
            quarter_copy(i).start()
        c_arrival(0).wait_recv()
        for i in range(4):
            finish(quarters[i], 0)

    @pl.when(yl == 2)
    def _():
        for i in range(4):
            quarter_copy(i).wait_recv()
            finish(quarters[i], 1)

    @pl.when(yl == 3)
    def _():
        c_arrival(2).wait_recv()
        c_arrival(1).wait_recv()
        for i in range(4):
            round_pass(i).wait_recv()
            finish(quarters[i], 1, 2, 0)

    for q in range(4):

        @pl.when((z != 7) | (yl != q))
        def _():
            remote(
                row_src.at[pl.ds(0, 8)], row_in.at[q], n_send.at[0], n_recv.at[q], up
            ).wait_recv()

    new_ref[...] = (row_in[0] + row_in[1]) + (row_in[2] + row_in[3])

    @pl.when(z == 7)
    def _():
        @pl.loop(0, 32)
        def _(to):
            @pl.when(to != r)
            def _():
                n_copy(to).wait_send()

    for h in range(2):

        @pl.when(gives_piece & jnp.logical_not(piece_self(h)))
        def _():
            piece_copy(h).wait_send()

    for h in range(2):

        @pl.when(gives_mirror & jnp.logical_not(mirror_self(h)))
        def _():
            mirror_copy(h).wait_send()

    for step in range(4):
        for way in range(2):
            for rows in range(2):
                if step < 3 or rows == way:
                    g_copy(way, step, rows).wait_send()
    for i in range(2):

        @pl.when(near(i) >= yl)
        def _():
            y_copy(near(i)).wait_send()

    for y in range(4):

        @pl.when(y >= yl)
        def _():
            for d in (1, 3):
                x_copy(y, d).wait_send()

                @pl.when(y // 2 == yh)
                def _():
                    h_copy(y, d).wait_send()

            @pl.when(y // 2 != yh)
            def _():
                two_copy(y).wait_send()

            for d in range(4):
                k_copy(y, d).wait_send()

        if y > 0:

            if y != 2:

                @pl.when((y > yl) & ((y != 3) | (yl != 0)))
                def _():
                    c_copy(y).wait_send()

    for i in range(4):

        @pl.when(yl == 0)
        def _():
            round_copy(i).wait_send()
            quarter_copy(i).wait_send()

        @pl.when(yl == 1)
        def _():
            round_pass(i).wait_send()
            quarter_copy(i).wait_send()


def shards(green, coupling):
    rows, cols, width = green.shape
    orbit = coupling.shape[0]
    high, wide = rows * orbit, cols * orbit
    vmem = pl.BlockSpec(memory_space=pltpu.VMEM)
    dma = pltpu.SemaphoreType.DMA
    collision, fresh = pl.pallas_call(
        kernel,
        out_shape=(
            jax.ShapeDtypeStruct((high, wide), BF),
            jax.ShapeDtypeStruct((8, 128), F32),
        ),
        in_specs=[pl.BlockSpec(memory_space=pl.ANY)] * 2,
        out_specs=(vmem, vmem),
        scratch_shapes=[
            pltpu.VMEM((rows * cols, width), BF),
            pltpu.VMEM((1, orbit), F32),
            pltpu.VMEM((high, wide), BF),
            dma((2,)),
            pltpu.VMEM((8, high, wide), BF),
            pltpu.VMEM((2, high, high), BF),
            pltpu.VMEM((2, high, high), BF),
            pltpu.VMEM((4, 8, high, high), BF),
            pltpu.VMEM((3, high, wide), BF),
            pltpu.VMEM((3, high, wide), BF),
            pltpu.VMEM((high, wide), BF),
            pltpu.VMEM((high, wide), F32),
            pltpu.VMEM((high, wide), F32),
            pltpu.VMEM((256, 128), F32),
            pltpu.VMEM((256, 128), F32),
            pltpu.VMEM((4, 8, 128), F32),
            dma((2, 4, 2)),
            dma((2, 4, 2)),
            dma((2,)),
            dma((2,)),
            dma((2,)),
            dma((2,)),
            dma((4,)),
            dma((4,)),
            dma((4, 2)),
            dma((4, 2)),
            dma((4, 2)),
            dma((4, 2)),
            dma((4, 4)),
            dma((4, 4)),
            dma((3,)),
            dma((3,)),
            dma((4,)),
            dma((4,)),
            dma((4,)),
            dma((4,)),
            dma((4,)),
            dma((4,)),
            dma((32,)),
            dma((4,)),
        ],
        compiler_params=pltpu.CompilerParams(
            collective_id=0, has_side_effects=True, vmem_limit_bytes=54848 << 10
        ),
        cost_estimate=pl.CostEstimate(
            flops=2 * high * wide * 8192, bytes_accessed=4 * high * wide, transcendentals=0
        ),
        name="collide",
    )(green.reshape(rows * cols, width), coupling.reshape(1, orbit))
    collision = collision.reshape(rows, orbit, cols, orbit).transpose(0, 2, 1, 3)
    collision = collision.reshape(rows, cols, width)
    fresh = fresh.reshape(2, 4, 2, orbit).transpose(1, 2, 0, 3).reshape(cols, 128)
    return (collision, fresh.astype(BF))


def solution(mesh):
    placed = (P("row", "col", None), P())
    return jax.shard_map(
        shards,
        mesh=mesh,
        in_specs=placed,
        out_specs=(P("row", "col", None), P("col", "row")),
        check_vma=False,
    )
```
